32 devices in a mesh: dp: 4 (over z), seq: 4 (over y, x), mp: 2 (over core).
Axes of the slice: x: 2, y: 2, z: 4, core: 2. Of those that a mesh axis runs over, the one named last changes fastest.
Arguments:
- features: bfloat16 [4, 2048, 1408], P('dp', ('seq', 'mp')), may hold values from -6 to 6
- conv_weight: bfloat16 [5, 1408, 1536], P(None, ('seq', 'mp')), may hold values from -0.0625 to 0.0625
- norm_gain: float32 [1536], replicated, may hold values from 0.25 to 1.75
- query_weight: bfloat16 [1536, 1024], replicated, may hold values from -0.15625 to 0.15625
- keyval_weight: bfloat16 [1536, 320], replicated, may hold values from -0.15625 to 0.15625
- head_scale: float32 [8], replicated, may hold values from 0.5 to 24
- output_weight: bfloat16 [1536, 1536], replicated, may hold values from -0.15625 to 0.15625
- pair_weight: bfloat16 [1536, 256], replicated, may hold values from -0.625 to 0.625
- pair_input: bfloat16 [4, 64, 64, 128], P('dp', ('seq', 'mp')), may hold values from -6 to 6
- flip_weight: bfloat16 [128, 128], replicated, may hold values from -0.5 to 0.5
- pair_cotangent: bfloat16 [4, 64, 64, 128], P('dp', ('seq', 'mp')), may hold values from -0.09375 to 0.09375
Outputs:
- block_out: bfloat16 [4, 1024, 1536], P('dp', ('seq', 'mp'))
- pair_out: bfloat16 [4, 64, 64, 128], P('dp', ('seq', 'mp'))
- grad_flip: float32 [128, 128], replicated
The draws below stay inside these ranges and needn't reach their ends.
All inputs are finite; a program needn't handle non-finite values.
Results may differ from the reference program's by a relative error of at most 0.011.
Values may be sent and summed in bfloat16 or wider, within the bound.
No kernel may reach another device: no remote copies, remote signals or barrier semaphores. Data moves between devices by JAX's collectives and lax.ppermute only.
A program may use at most 192 MiB of HBM per device.

```python
import math
import jax
import jax.numpy as jnp
from jax import lax

CIN = 1408
D = 1536
HEADS = 8
DK = 128
DV = 192
PC = 128
KW = 5
PAIR_POOL = 16
BATCH = 4
POS = 1024
PR = 64


def block_scale(stream_key, shape, shards, low, largest):
    def one(position, shards_of):
        draws = jax.random.uniform(jax.random.fold_in(jax.random.fold_in(stream_key, 6), position), (shards_of,), jnp.float32, low / len(shards), largest / len(shards))
        return jnp.repeat(jnp.exp(draws), shape[position] // shards_of).reshape((-1,) + (1,) * (len(shape) - position - 1))

    loudness = one(*shards[0])
    for cut in shards[1:]:
        loudness = loudness * one(*cut)
    return loudness


def scatter_about(key, shape, scale, most, shards=(), held_as=jnp.bfloat16):
    level = block_scale(key, shape, shards, -0.22, 0.18) if shards else 1.0
    array = jax.random.normal(key, shape, jnp.float32) * scale * level
    return jnp.minimum(jnp.maximum(array, -most), most).astype(held_as)


def setup_inputs(seed: int = 0) -> dict:
    splits = jax.random.split(jax.random.key(seed), 12)
    return {
        "features": scatter_about(splits[0], (BATCH, 2 * POS, CIN), 1.0, 6.0, ((0, 4), (1, 8))),
        "conv_weight": scatter_about(splits[1], (KW, CIN, D), (KW * CIN) ** -0.5, 0.0625, ((1, 8),)),
        "norm_gain": jnp.clip(1.0 + 0.15 * jax.random.normal(splits[2], (D,), jnp.float32), 0.25, 1.75),
        "query_weight": scatter_about(splits[3], (D, HEADS * DK), D ** -0.5, 0.15625),
        "keyval_weight": scatter_about(splits[4], (D, DK + DV), D ** -0.5, 0.15625),
        "head_scale": jnp.clip(jnp.exp(jax.random.uniform(splits[5], (HEADS,), jnp.float32, math.log(0.5), math.log(24.0))), 0.5, 24.0),
        "output_weight": scatter_about(splits[6], (HEADS * DV, D), (HEADS * DV) ** -0.5, 0.15625),
        "pair_weight": scatter_about(splits[7], (D, 2 * PC), (D // 16) ** -0.5, 0.625),
        "pair_input": scatter_about(splits[8], (BATCH, PR, PR, PC), 1.0, 6.0, ((0, 4), (1, 8))),
        "flip_weight": scatter_about(splits[9], (PC, PC), PC ** -0.5, 0.5),
        "pair_cotangent": scatter_about(splits[10], (BATCH, PR, PR, PC), (1.0 / PR), 0.09375, ((0, 4), (1, 8))),
    }


norm_eps = 1e-06
logit_cap = 50.0

def root_norm(values_in):
    return values_in * lax.rsqrt(lax.optimization_barrier(jnp.mean(values_in * values_in, axis=-1, keepdims=True)) + norm_eps)

def prepare(raw):
    return jax.nn.gelu(root_norm(raw.astype(jnp.float32)), approximate=False).astype(jnp.bfloat16)

def one_window(features, pair_input, pair_cotangent, conv_weight, norm_gain, query_weight, keyval_weight, head_scale, output_weight, pair_weight, flip_weight):
    fine_len = features.shape[0]
    margin = KW // 2
    prepared = prepare(features)
    padded = jnp.pad(prepared, ((margin, margin), (0, 0)))
    conv_sum = jnp.zeros((fine_len, D), jnp.float32)
    for lag_index in range(KW):
        conv_sum = conv_sum + jnp.dot(padded[lag_index:lag_index + fine_len], conv_weight[lag_index], preferred_element_type=jnp.float32)
    skipped = jnp.pad(features.astype(jnp.float32), ((0, 0), (0, D - CIN)))
    encoded = lax.optimization_barrier(jnp.max((conv_sum + skipped).reshape(fine_len // 2, 2, D), axis=1)).astype(jnp.bfloat16)
    widened = encoded.astype(jnp.float32)
    normed = (root_norm(widened) * norm_gain).astype(jnp.bfloat16)
    scale_row = jnp.repeat(head_scale, DK) / math.sqrt(DK)
    queries = (jnp.dot(normed, query_weight, preferred_element_type=jnp.float32) * scale_row).astype(jnp.bfloat16)
    keyvals = jnp.dot(normed, keyval_weight, preferred_element_type=jnp.float32).astype(jnp.bfloat16)
    key_rows = keyvals[:, :DK]
    value_rows = keyvals[:, DK:]
    block_len = math.gcd(POS, 512)
    query_blocks = queries.reshape(POS // block_len, block_len * HEADS, DK)

    def attend(query_block):
        scores = jnp.dot(query_block, key_rows.T, preferred_element_type=jnp.float32)
        weights = jnp.exp(logit_cap * jnp.tanh(scores / logit_cap))
        totals = lax.optimization_barrier(jnp.sum(weights, axis=-1, keepdims=True))
        mixed = jnp.dot(weights.astype(jnp.bfloat16), value_rows, preferred_element_type=jnp.float32) / totals
        return mixed.astype(jnp.bfloat16)
    heads_out = lax.map(attend, query_blocks).reshape(POS, HEADS * DV)
    block_out = (widened + jnp.dot(heads_out, output_weight, preferred_element_type=jnp.float32)).astype(jnp.bfloat16)
    pooled = lax.optimization_barrier(jnp.mean(widened.reshape(POS // PAIR_POOL, PAIR_POOL, D), axis=1)).astype(jnp.bfloat16)
    pair_feats = jnp.dot(pooled, pair_weight, preferred_element_type=jnp.float32).astype(jnp.bfloat16)
    pair_q = pair_feats[:, :PC].astype(jnp.float32)
    pair_k = pair_feats[:, PC:].astype(jnp.float32)
    summed = (pair_input.astype(jnp.float32) + pair_q[:, None, :] * pair_k[None, :, :]).astype(jnp.bfloat16)
    flipped = jnp.swapaxes(summed, 0, 1).astype(jnp.float32)
    turned = jnp.einsum('abc,cd->abd', flipped, flip_weight.astype(jnp.float32), precision=lax.Precision.HIGHEST)
    pair_out = (summed.astype(jnp.float32) + turned).astype(jnp.bfloat16)
    grad_part = jnp.einsum('abc,abd->cd', flipped, pair_cotangent.astype(jnp.float32), precision=lax.Precision.HIGHEST)
    return (block_out, pair_out, grad_part)

def reference(features, conv_weight, norm_gain, query_weight, keyval_weight, head_scale, output_weight, pair_weight, pair_input, flip_weight, pair_cotangent):

    def per_window(packed):
        return one_window(packed[0], packed[1], packed[2], conv_weight, norm_gain, query_weight, keyval_weight, head_scale, output_weight, pair_weight, flip_weight)
    block_out, pair_out, grad_parts = lax.map(per_window, (features, pair_input, pair_cotangent))
    return (block_out, pair_out, lax.optimization_barrier(jnp.sum(grad_parts, axis=0)))
```

```python
import functools
import math

import jax
import jax.numpy as jnp
from jax import lax
from jax.experimental import pallas as pl
from jax.experimental.pallas import tpu as pltpu
from jax.sharding import PartitionSpec as P

PAIR_POOL = 16
norm_eps = 1e-06
logit_cap = 50.0
MIB = 1 << 20
GROUP = ("seq", "mp")
f32, bf16 = jnp.float32, jnp.bfloat16


def whole_vmem():
    return pl.BlockSpec(memory_space=pltpu.VMEM)


def smem():
    return pl.BlockSpec(memory_space=pltpu.SMEM)


def tree_sum(terms):
    while len(terms) > 1:
        terms = [terms[i] + terms[i + 1] for i in range(0, len(terms), 2)]
    return terms[0]


def flipped_bits(mask, bits):
    return sum(((mask >> b) & 1) << (bits - 1 - b) for b in range(bits))


def hop_pairs(chips, core_masks, core_flip):
    pairs = []
    for chip in range(chips):
        for core in range(2):
            target = (chip ^ core_masks[core]) * 2 + (core ^ core_flip)
            pairs.append((chip * 2 + core, target))
    return pairs


def prep_kernel(chips, width, order_ref, order2_ref, feat_ref, raw_ref, *rest):
    block_refs = rest[:chips]
    edge_refs = rest[chips : 2 * chips]
    wide, split = rest[2 * chips :]
    rows = feat_ref.shape[0]
    half = rows // 2
    target = lax.broadcasted_iota(jnp.int32, (rows, rows), 0)
    source = lax.broadcasted_iota(jnp.int32, (rows, rows), 1)
    wanted = jnp.where(target < half, 2 * target, 2 * (target - half) + 1)
    pick = jnp.where(source == wanted, 1.0, 0.0).astype(bf16)
    wide[...] = jnp.dot(pick, feat_ref[...], preferred_element_type=f32)
    step = 16

    def body(i, carry):
        at = pl.ds(pl.multiple_of(i * step, step), step)
        x = wide[at, :]
        raw_ref[at, :] = x.astype(bf16)
        v = x * lax.rsqrt(jnp.mean(x * x, axis=-1, keepdims=True) + norm_eps)
        g = (0.5 * v) * (1.0 + lax.erf(v * math.sqrt(0.5)))
        g = g.astype(bf16)
        for q in range(chips):
            split[q, at, :] = g[:, q * width : (q + 1) * width]
        return carry

    lax.fori_loop(0, rows // step, body, 0)
    for k in range(chips):
        block_refs[k][...] = split[order_ref[k]]
        strip = split[order2_ref[k]]
        head = strip[0:16].astype(f32)
        head2 = strip[half : half + 16].astype(f32)
        tail = strip[half - 16 : half].astype(f32)
        tail2 = strip[rows - 16 : rows].astype(f32)
        edge_refs[k][...] = jnp.concatenate(
            [head[0:1], head2[0:1], tail[15:16], tail2[15:16], jnp.zeros((4, width), f32)], axis=0
        )


def prep(features, order, order2, chips):
    rows, channels = features.shape
    width = channels // chips
    outs = [jax.ShapeDtypeStruct((rows, channels), bf16)]
    outs += [jax.ShapeDtypeStruct((rows, width), bf16)] * chips
    outs += [jax.ShapeDtypeStruct((8, width), f32)] * chips
    got = pl.pallas_call(
        functools.partial(prep_kernel, chips, width),
        name="prep",
        out_shape=outs,
        in_specs=[smem(), smem(), whole_vmem()],
        out_specs=[whole_vmem()] * len(outs),
        scratch_shapes=[
            pltpu.VMEM((rows, channels), f32),
            pltpu.VMEM((chips, rows, width), bf16),
        ],
        compiler_params=pltpu.CompilerParams(vmem_limit_bytes=16 * MIB),
        cost_estimate=pl.CostEstimate(
            flops=40 * rows * channels, bytes_accessed=6 * rows * channels, transcendentals=0
        ),
    )(order, order2, features)
    return got[0], got[1 : 1 + chips], got[1 + chips :]


def conv_kernel(chips, taps, where_ref, block_ref, *rest):
    edge_refs = rest[:chips]
    weight_ref, out_ref, cols = rest[chips:]
    rows, width = block_ref.shape
    half = rows // 2

    @pl.when(pl.program_id(0) == 0)
    def _():
        before = jnp.zeros((8, width), f32)
        after = jnp.zeros((8, width), f32)
        for k in range(chips):
            strip = edge_refs[k][...]
            before = jnp.where(where_ref[0] == k, strip, before)
            after = jnp.where(where_ref[1] == k, strip, after)
        even = block_ref[0:half, :].astype(f32)
        odd = block_ref[half:rows, :].astype(f32)
        row = lax.broadcasted_iota(jnp.int32, (half, width), 0)

        def back(v, strip_row):
            return jnp.where(row == 0, before[strip_row : strip_row + 1], pltpu.roll(v, 1, 0))

        def ahead(v, strip_row):
            return jnp.where(
                row == half - 1, after[strip_row : strip_row + 1], pltpu.roll(v, half - 1, 0)
            )

        lagged = [back(even, 2), back(odd, 3), even, odd, ahead(even, 0), ahead(odd, 1)]
        lagged = [v.astype(bf16) for v in lagged]
        for k in range(taps):
            cols[0:half, k * width : (k + 1) * width] = lagged[k]
            cols[half:rows, k * width : (k + 1) * width] = lagged[k + 1]

    out_ref[...] = jnp.dot(cols[...], weight_ref[...], preferred_element_type=f32).astype(
        out_ref.dtype
    )


def conv(block, edges, weight, where, taps, out_dtype):
    rows, width = block.shape
    depth, model_dim = weight.shape
    chips = len(edges)
    tile = 512
    return pl.pallas_call(
        functools.partial(conv_kernel, chips, taps),
        name="conv",
        grid=(model_dim // tile,),
        out_shape=jax.ShapeDtypeStruct((rows, model_dim), out_dtype),
        in_specs=[smem()]
        + [whole_vmem()] * (1 + chips)
        + [pl.BlockSpec((depth, tile), lambda n: (0, n))],
        out_specs=pl.BlockSpec((rows, tile), lambda n: (0, n)),
        scratch_shapes=[pltpu.VMEM((rows, depth), bf16)],
        compiler_params=pltpu.CompilerParams(vmem_limit_bytes=20 * MIB),
        cost_estimate=pl.CostEstimate(
            flops=2 * rows * depth * model_dim,
            bytes_accessed=2 * depth * model_dim,
            transcendentals=0,
        ),
    )(where, block, *edges, weight)


def encode_kernel(
    arrivals, raw_ref, gain_ref, keyval_weight_ref, pair_weight_ref, own_ref, *rest
):
    come_refs = rest[:arrivals]
    encoded_ref, normed_ref, keyval_ref, feats_ref = rest[arrivals:]
    rows, model_dim = own_ref.shape
    half = rows // 2
    channels = raw_ref.shape[1]
    total = own_ref[...]
    for ref in come_refs:
        total = total + ref[...].astype(f32)
    skip = raw_ref[...].astype(f32)
    if channels < model_dim:
        skip = jnp.concatenate([skip, jnp.zeros((rows, model_dim - channels), f32)], axis=1)
    total = total + skip
    encoded = jnp.maximum(total[:half], total[half:]).astype(bf16)
    encoded_ref[...] = encoded
    wide = encoded.astype(f32)
    scale = lax.rsqrt(jnp.mean(wide * wide, axis=-1, keepdims=True) + norm_eps)
    normed = (wide * scale * gain_ref[...]).astype(bf16)
    normed_ref[...] = normed
    pairs = half // PAIR_POOL
    at = lax.broadcasted_iota(jnp.int32, (pairs, half), 0)
    of = lax.broadcasted_iota(jnp.int32, (pairs, half), 1) // PAIR_POOL
    spread = jnp.where(at == of, 1.0 / PAIR_POOL, 0.0).astype(bf16)
    pooled = jnp.dot(spread, encoded, preferred_element_type=f32).astype(bf16)
    feats_ref[...] = (
        jnp.dot(pooled, pair_weight_ref[...], preferred_element_type=f32).astype(bf16).astype(f32)
    )
    keyval_ref[...] = jnp.dot(
        normed, keyval_weight_ref[...], preferred_element_type=f32
    ).astype(bf16)


def encode(own, come, raw, gain, keyval_weight, pair_weight):
    rows, model_dim = own.shape
    half = rows // 2
    return pl.pallas_call(
        functools.partial(encode_kernel, len(come)),
        name="encode",
        out_shape=[
            jax.ShapeDtypeStruct((half, model_dim), bf16),
            jax.ShapeDtypeStruct((half, model_dim), bf16),
            jax.ShapeDtypeStruct((half, keyval_weight.shape[1]), bf16),
            jax.ShapeDtypeStruct((half // PAIR_POOL, pair_weight.shape[1]), f32),
        ],
        in_specs=[whole_vmem()] * (5 + len(come)),
        out_specs=[whole_vmem()] * 4,
        compiler_params=pltpu.CompilerParams(vmem_limit_bytes=24 * MIB),
        cost_estimate=pl.CostEstimate(
            flops=2 * half * model_dim * keyval_weight.shape[1],
            bytes_accessed=6 * rows * model_dim,
            transcendentals=0,
        ),
    )(raw, gain, keyval_weight, pair_weight, own, *come)


def query_kernel(normed_ref, weight_ref, scale_ref, out_ref):
    got = jnp.dot(normed_ref[...], weight_ref[...], preferred_element_type=f32)
    out_ref[...] = (got * scale_ref[...]).astype(bf16)


def project_queries(normed, weight, scale_row):
    rows, model_dim = normed.shape
    columns = weight.shape[1]
    tile = 256
    return pl.pallas_call(
        query_kernel,
        name="queries",
        grid=(columns // tile,),
        out_shape=jax.ShapeDtypeStruct((rows, columns), bf16),
        in_specs=[
            whole_vmem(),
            pl.BlockSpec((model_dim, tile), lambda n: (0, n)),
            pl.BlockSpec((1, tile), lambda n: (0, n)),
        ],
        out_specs=pl.BlockSpec((rows, tile), lambda n: (0, n)),
        compiler_params=pltpu.CompilerParams(vmem_limit_bytes=16 * MIB),
        cost_estimate=pl.CostEstimate(
            flops=2 * rows * columns * model_dim,
            bytes_accessed=2 * columns * model_dim,
            transcendentals=0,
        ),
    )(normed, weight, scale_row)


def attend_kernel(parts, heads_step, key_dim, query_ref, encoded_ref, weight_ref, *rest):
    part_refs = rest[:parts]
    out_ref, keys, values, total = rest[parts:]
    rows = query_ref.shape[0]
    span = part_refs[0].shape[0]
    value_dim = values.shape[1]

    @pl.when(pl.program_id(0) == 0)
    def _():
        for k in range(parts):
            got = part_refs[k][...]
            keys[k * span : (k + 1) * span, :] = got[:, :key_dim]
            values[k * span : (k + 1) * span, :] = got[:, key_dim:]
        total[...] = encoded_ref[...].astype(f32)

    queries = query_ref[...]
    queries = jnp.concatenate(
        [queries[:, h * key_dim : (h + 1) * key_dim] for h in range(heads_step)], axis=0
    )
    scores = lax.dot_general(
        queries, keys[...], (((1,), (1,)), ((), ())), preferred_element_type=f32
    )
    weights = jnp.exp(logit_cap * jnp.tanh(scores * (1.0 / logit_cap)))
    sums = jnp.sum(weights, axis=-1, keepdims=True)
    mixed = jnp.dot(weights.astype(bf16), values[...], preferred_element_type=f32) / sums
    mixed = mixed.astype(bf16)
    update = total[...]
    for h in range(heads_step):
        update = update + jnp.dot(
            mixed[h * rows : (h + 1) * rows],
            weight_ref[h * value_dim : (h + 1) * value_dim, :],
            preferred_element_type=f32,
        )
    total[...] = update

    @pl.when(pl.program_id(0) == pl.num_programs(0) - 1)
    def _():
        out_ref[...] = update.astype(bf16)


def attend(queries, encoded, output_weight, parts, heads):
    rows, model_dim = encoded.shape
    key_dim = queries.shape[1] // heads
    value_dim = output_weight.shape[0] // heads
    span = parts[0].shape[0]
    total_keys = span * len(parts)
    heads_step = 2
    return pl.pallas_call(
        functools.partial(attend_kernel, len(parts), heads_step, key_dim),
        name="attend",
        grid=(heads // heads_step,),
        out_shape=jax.ShapeDtypeStruct((rows, model_dim), bf16),
        in_specs=[
            pl.BlockSpec((rows, heads_step * key_dim), lambda h: (0, h)),
            whole_vmem(),
            pl.BlockSpec((heads_step * value_dim, model_dim), lambda h: (h, 0)),
        ]
        + [whole_vmem()] * len(parts),
        out_specs=pl.BlockSpec((rows, model_dim), lambda h: (0, 0)),
        scratch_shapes=[
            pltpu.VMEM((total_keys, key_dim), bf16),
            pltpu.VMEM((total_keys, value_dim), bf16),
            pltpu.VMEM((rows, model_dim), f32),
        ],
        compiler_params=pltpu.CompilerParams(vmem_limit_bytes=32 * MIB),
        cost_estimate=pl.CostEstimate(
            flops=2 * rows * heads * (total_keys * (key_dim + value_dim) + value_dim * model_dim),
            bytes_accessed=2 * heads * value_dim * model_dim,
            transcendentals=2 * rows * heads * total_keys,
        ),
    )(queries, encoded, output_weight, *parts)


def pair_kernel(parts, slot_ref, input_ref, turned_ref, cotangent_ref, flip_ref, *rest):
    feat_refs = rest[:parts]
    out_ref, grad_ref, stack, summed, flipped = rest[parts:]
    rows, columns, dim = input_ref.shape
    for k in range(parts):
        stack[k] = feat_refs[k][...]
    every = jnp.concatenate([stack[slot_ref[b]] for b in range(parts)], axis=0)
    own = feat_refs[0][...]
    for i in range(rows):
        at = pl.ds(i * columns, columns)
        mine = own[i : i + 1]
        summed[at, :] = (
            input_ref[i].astype(f32) + mine[:, :dim] * every[:, dim:]
        ).astype(bf16)
        flipped[at, :] = (
            turned_ref[i].astype(f32) + every[:, :dim] * mine[:, dim:]
        ).astype(bf16)
    update = jnp.dot(flipped[...], flip_ref[...], preferred_element_type=f32)
    update = update + summed[...].astype(f32)
    out_ref[...] = update.astype(bf16).reshape(rows, columns, dim)
    grad_ref[...] = lax.dot_general(
        flipped[...],
        cotangent_ref[...].reshape(rows * columns, dim),
        (((0,), (0,)), ((), ())),
        preferred_element_type=f32,
    )


def pair_update(pair_input, turned, cotangent, flip_weight, feats, slots):
    rows, columns, dim = pair_input.shape
    parts = len(feats)
    return pl.pallas_call(
        functools.partial(pair_kernel, parts),
        name="pair",
        out_shape=[
            jax.ShapeDtypeStruct((rows, columns, dim), bf16),
            jax.ShapeDtypeStruct((dim, dim), f32),
        ],
        in_specs=[smem()] + [whole_vmem()] * (4 + parts),
        out_specs=[whole_vmem()] * 2,
        scratch_shapes=[
            pltpu.VMEM((parts, rows, 2 * dim), f32),
            pltpu.VMEM((rows * columns, dim), bf16),
            pltpu.VMEM((rows * columns, dim), bf16),
        ],
        compiler_params=pltpu.CompilerParams(vmem_limit_bytes=24 * MIB),
        cost_estimate=pl.CostEstimate(
            flops=4 * rows * columns * dim * dim,
            bytes_accessed=8 * rows * columns * dim,
            transcendentals=0,
        ),
    )(slots, pair_input, turned, cotangent, flip_weight, *feats)


def per_device(
    features,
    conv_weight,
    norm_gain,
    query_weight,
    keyval_weight,
    head_scale,
    output_weight,
    pair_weight,
    pair_input,
    flip_weight,
    pair_cotangent,
):
    chips = lax.axis_size("seq")
    bits = chips.bit_length() - 1
    windows = lax.axis_size("dp")
    taps = conv_weight.shape[0]
    model_dim = output_weight.shape[1]
    heads = head_scale.shape[0]
    key_dim = query_weight.shape[1] // heads
    chip = lax.axis_index("seq")
    core = lax.axis_index("mp")

    masks = [(k, flipped_bits(k, bits)) for k in range(chips)]
    plain = jnp.arange(chips, dtype=jnp.int32)
    mirrored = jnp.array([k[1] for k in masks], jnp.int32)
    owner = chip ^ jnp.where(core == 0, plain, mirrored)
    order2 = chip ^ plain

    def send(value, mask, flip=0):
        cores = mask if isinstance(mask, tuple) else (mask, mask)
        return lax.ppermute(value, GROUP, hop_pairs(chips, cores, flip))

    def spots(k):
        place = owner[k]
        left = jnp.where(core == 0, place - 1, place)
        right = jnp.where(core == 0, place, place + 1)
        left = jnp.where(left >= 0, left ^ chip, -1)
        right = jnp.where(right < chips, right ^ chip, -1)
        return jnp.stack([left, right]).astype(jnp.int32)

    weight = lax.all_gather(conv_weight, "mp", axis=1, tiled=True)
    weight = weight.reshape(-1, model_dim)

    raw, blocks, strips = prep(features[0], owner, order2, chips)
    edges = [send(strips[k], k, 1) for k in range(chips)]
    held = {0: blocks[0]}
    for k in range(chips - 1, 0, -1):
        held[k] = send(blocks[k], masks[k])

    order = sorted(range(1, chips), key=lambda k: ([(k >> b) & 1 for b in range(bits)], k))[::-1]
    partial = {}
    for k in order:
        first = k & 1
        partial[k] = conv(held[k], edges, weight, spots(k), taps, bf16 if first else f32)
    partial[0] = conv(held[0], edges, weight, spots(0), taps, f32)
    arrived = []
    for b in range(bits):
        bit = 1 << b
        leaving = [k for k in order if k in partial and k & bit]
        got = {k ^ bit: send(partial.pop(k).astype(bf16), masks[bit]) for k in leaving}
        for k, value in got.items():
            if k == 0:
                arrived.append(value)
            else:
                partial[k] = partial[k] + value.astype(f32)

    encoded, normed, keyval, feats = encode(
        partial[0], arrived, raw, norm_gain[None], keyval_weight, pair_weight
    )

    all_feats = [feats] + [
        send(feats, k >> 1, k & 1) for k in range(1, 2 * chips)
    ]
    keyvals = [keyval] + [send(keyval, k >> 1, k & 1) for k in range(1, 2 * chips)]
    scale_row = jnp.repeat(head_scale, key_dim) / math.sqrt(key_dim)
    queries = project_queries(normed, query_weight, scale_row[None])

    turned = lax.all_to_all(pair_input[0], GROUP, split_axis=1, concat_axis=0, tiled=True)
    turned = jnp.swapaxes(turned, 0, 1)
    places = jnp.arange(2 * chips, dtype=jnp.int32)
    slots = ((places >> 1) ^ chip) * 2 + ((places & 1) ^ core)
    pair_out, grad = pair_update(
        pair_input[0], turned, pair_cotangent[0], flip_weight, all_feats, slots.astype(jnp.int32)
    )
    grad = tree_sum([grad] + [send(grad, k >> 1, k & 1) for k in range(1, 2 * chips)])
    grad = tree_sum(
        [grad]
        + [
            lax.ppermute(grad, "dp", [(w, w ^ k) for w in range(windows)])
            for k in range(1, windows)
        ]
    )
    block_out = attend(queries, encoded, output_weight, keyvals, heads)
    return (block_out[None], pair_out[None], grad)


def solution(mesh):
    placed = (
        P("dp", ("seq", "mp"), None),
        P(None, ("seq", "mp"), None),
        P(),
        P(),
        P(),
        P(),
        P(),
        P(),
        P("dp", ("seq", "mp"), None, None),
        P(),
        P("dp", ("seq", "mp"), None, None),
    )
    return jax.shard_map(
        per_device,
        mesh=mesh,
        in_specs=placed,
        out_specs=(P("dp", ("seq", "mp"), None), P("dp", ("seq", "mp"), None, None), P()),
        check_vma=False,
    )
```

```python
import functools
import math

import jax
import jax.numpy as jnp
from jax import lax
from jax.experimental import pallas as pl
from jax.experimental.pallas import tpu as pltpu
from jax.sharding import PartitionSpec as P

PAIR_POOL = 16
norm_eps = 1e-06
logit_cap = 50.0
MIB = 1 << 20
GROUP = ("seq", "mp")
f32, bf16 = jnp.float32, jnp.bfloat16


def whole_vmem():
    return pl.BlockSpec(memory_space=pltpu.VMEM)


def anywhere():
    return pl.BlockSpec(memory_space=pl.ANY)


def smem():
    return pl.BlockSpec(memory_space=pltpu.SMEM)


def in_hbm(value):
    return pltpu.with_memory_space_constraint(value, pltpu.HBM)


def array(shape, dtype):
    return jax.ShapeDtypeStruct(shape, dtype)


def lane_pad(width):
    return (width + 127) // 128 * 128


def tree_sum(terms):
    while len(terms) > 1:
        terms = [terms[i] + terms[i + 1] for i in range(0, len(terms), 2)]
    return terms[0]


def flipped_bits(mask, bits):
    return sum(((mask >> b) & 1) << (bits - 1 - b) for b in range(bits))


def here():
    return lax.axis_index("seq"), lax.axis_index("mp")


def hop_pairs(chips, core_masks, core_flip):
    pairs = []
    for chip in range(chips):
        for core in range(2):
            target = (chip ^ core_masks[core]) * 2 + (core ^ core_flip)
            pairs.append((chip * 2 + core, target))
    return pairs


def strip_kernel(margin, feat_hbm, out_ref, top, bottom, sems):
    rows = feat_hbm.shape[0]
    copies = [
        pltpu.make_async_copy(feat_hbm.at[0:16, :], top, sems.at[0]),
        pltpu.make_async_copy(feat_hbm.at[rows - 16 : rows, :], bottom, sems.at[1]),
    ]
    for c in copies:
        c.start()
    for c in copies:
        c.wait()
    first = top[...].astype(f32)[:margin]
    last = bottom[...].astype(f32)[16 - margin :]
    rest = jnp.zeros((16 - 2 * margin, first.shape[1]), f32)
    out_ref[...] = jnp.concatenate([first, last, rest], axis=0).astype(bf16)


def edge_strip(features, margin):
    channels = features.shape[1]
    return pl.pallas_call(
        functools.partial(strip_kernel, margin),
        name="edge_strip",
        out_shape=array((16, channels), bf16),
        in_specs=[anywhere()],
        out_specs=whole_vmem(),
        scratch_shapes=[
            pltpu.VMEM((16, channels), bf16),
            pltpu.VMEM((16, channels), bf16),
            pltpu.SemaphoreType.DMA((2,)),
        ],
        compiler_params=pltpu.CompilerParams(vmem_limit_bytes=2 * MIB),
    )(in_hbm(features))


def pick_rows(rows):
    half = rows // 2
    target = lax.broadcasted_iota(jnp.int32, (rows, rows), 0)
    source = lax.broadcasted_iota(jnp.int32, (rows, rows), 1)
    wanted = jnp.where(target < half, 2 * target, 2 * (target - half) + 1)
    return jnp.where(source == wanted, 1.0, 0.0).astype(bf16)


def prep_kernel(chips, width, feat_hbm, strip_ref, *rest):
    block_refs = rest[:chips]
    feat, wide, split, sem = rest[chips:]
    rows = feat.shape[0]
    chip, _ = here()
    copy = pltpu.make_async_copy(feat_hbm, feat, sem)
    copy.start()
    split[:, :, width:] = jnp.zeros((chips, split.shape[1], split.shape[2] - width), bf16)
    pick = pick_rows(rows)
    wide[rows:, :] = strip_ref[...].astype(f32)
    copy.wait()
    wide[0:rows, :] = jnp.dot(pick, feat[...], preferred_element_type=f32)

    def gelu_rows(at):
        x = wide[at, :]
        v = x * lax.rsqrt(jnp.mean(x * x, axis=-1, keepdims=True) + norm_eps)
        g = (0.5 * v) * (1.0 + lax.erf(v * math.sqrt(0.5)))
        g = g.astype(bf16)
        for q in range(chips):
            split[q, at, 0:width] = g[:, q * width : (q + 1) * width]

    step = 32

    def body(i, carry):
        gelu_rows(pl.ds(pl.multiple_of(i * step, step), step))
        return carry

    lax.fori_loop(0, rows // step, body, 0)
    gelu_rows(pl.ds(rows, wide.shape[0] - rows))
    for k in range(chips):
        block_refs[k][...] = split[chip ^ k]


def prep(features, strip, chips):
    rows, channels = features.shape
    width = channels // chips
    padded = lane_pad(width)
    tall = rows + strip.shape[0]
    return pl.pallas_call(
        functools.partial(prep_kernel, chips, width),
        name="prep",
        out_shape=[array((tall, padded), bf16)] * chips,
        in_specs=[anywhere(), whole_vmem()],
        out_specs=[whole_vmem()] * chips,
        scratch_shapes=[
            pltpu.VMEM((rows, channels), bf16),
            pltpu.VMEM((tall, channels), f32),
            pltpu.VMEM((chips, tall, padded), bf16),
            pltpu.SemaphoreType.DMA,
        ],
        compiler_params=pltpu.CompilerParams(vmem_limit_bytes=6 * MIB),
        cost_estimate=pl.CostEstimate(
            flops=40 * rows * channels, bytes_accessed=6 * rows * channels, transcendentals=0
        ),
    )(in_hbm(features), strip)


def pack_kernel(taps, padded, own_hbm, peer_hbm, out_ref, sems):
    part = own_hbm.shape[0] // taps
    _, core = here()
    copies = []
    for p, source in enumerate((own_hbm, peer_hbm)):
        place = core if p == 0 else 1 - core
        for k in range(taps):
            to = pl.ds(pl.multiple_of(k * padded + place * part, 16), part)
            copies.append(
                pltpu.make_async_copy(
                    source.at[k * part : (k + 1) * part, :], out_ref.at[to, :], sems.at[p, k]
                )
            )
    for c in copies:
        c.start()
    if padded > 2 * part:
        for k in range(taps):
            out_ref[k * padded + 2 * part : (k + 1) * padded, :] = jnp.zeros(
                (padded - 2 * part, out_ref.shape[1]), bf16
            )
    for c in copies:
        c.wait()


def pack_filter(own, peer, taps, padded):
    model_dim = own.shape[1]
    part = own.shape[0] // taps
    if part % 16:
        own, peer = (w.reshape(taps, part, model_dim) for w in (own, peer))
        first = lax.axis_index("mp") == 0
        low, high = jnp.where(first, own, peer), jnp.where(first, peer, own)
        both = jnp.concatenate([low, high], axis=1)
        both = jnp.pad(both, ((0, 0), (0, padded - 2 * part), (0, 0)))
        return both.reshape(taps * padded, model_dim)
    return pl.pallas_call(
        functools.partial(pack_kernel, taps, padded),
        name="pack_filter",
        out_shape=array((taps * padded, model_dim), bf16),
        in_specs=[anywhere()] * 2,
        out_specs=whole_vmem(),
        scratch_shapes=[pltpu.SemaphoreType.DMA((2, taps))],
        compiler_params=pltpu.CompilerParams(vmem_limit_bytes=2 * MIB),
        cost_estimate=pl.CostEstimate(
            flops=0, bytes_accessed=4 * own.shape[0] * model_dim, transcendentals=0
        ),
    )(in_hbm(own), peer)


def conv_kernel(chips, bits, taps, tile, wanted, *rest):
    count = len(wanted)
    message_refs = rest[:chips]
    weight_ref = rest[chips]
    out_refs = rest[chips + 1 : chips + 1 + count]
    held, cols = rest[chips + 1 + count :]
    tall, padded = held.shape[1:]
    rows, model_dim = out_refs[0].shape
    half = rows // 2
    chip, core = here()
    for k in range(chips):
        held[k] = message_refs[k][...]
    row = lax.broadcasted_iota(jnp.int32, (half, padded), 0)
    for j, k in enumerate(wanted):
        mask = jnp.where(core == 0, k, flipped_bits(k, bits))
        left = (chip ^ mask) - (1 - core)
        right = (chip ^ mask) + core
        block = held[mask]
        before = held[jnp.where(left >= 0, left ^ chip, 0), rows:tall, :].astype(f32)
        before = jnp.where(left >= 0, before, 0.0)
        after = held[jnp.where(right < chips, right ^ chip, 0), rows:tall, :].astype(f32)
        after = jnp.where(right < chips, after, 0.0)
        even = block[0:half].astype(f32)
        odd = block[half:rows].astype(f32)

        def back(v, strip_row):
            return jnp.where(row == 0, before[strip_row : strip_row + 1], pltpu.roll(v, 1, 0))

        def ahead(v, strip_row):
            return jnp.where(
                row == half - 1, after[strip_row : strip_row + 1], pltpu.roll(v, half - 1, 0)
            )

        lagged = [back(even, 2), back(odd, 3), even, odd, ahead(even, 0), ahead(odd, 1)]
        for i, v in enumerate(lagged):
            piece = v.astype(bf16)
            if i < taps:
                cols[j * rows : j * rows + half, i * padded : (i + 1) * padded] = piece
            if i > 0:
                cols[j * rows + half : (j + 1) * rows, (i - 1) * padded : i * padded] = piece
    for j in range(count):
        for n in range(model_dim // tile):
            at = pl.ds(n * tile, tile)
            got = jnp.dot(
                cols[j * rows : (j + 1) * rows], weight_ref[:, at], preferred_element_type=f32
            )
            out_refs[j][:, at] = got.astype(out_refs[j].dtype)


def conv(messages, weight, taps, wanted, dtypes):
    chips = len(messages)
    bits = chips.bit_length() - 1
    tall, padded = messages[0].shape
    depth, model_dim = weight.shape
    rows = tall - 16
    count = len(wanted)
    return pl.pallas_call(
        functools.partial(conv_kernel, chips, bits, taps, 512, wanted),
        name="conv",
        out_shape=[array((rows, model_dim), d) for d in dtypes],
        in_specs=[whole_vmem()] * (chips + 1),
        out_specs=[whole_vmem()] * count,
        scratch_shapes=[
            pltpu.VMEM((chips, tall, padded), bf16),
            pltpu.VMEM((count * rows, depth), bf16),
        ],
        compiler_params=pltpu.CompilerParams(vmem_limit_bytes=(4 + 2 * count) * MIB),
        cost_estimate=pl.CostEstimate(
            flops=2 * count * rows * depth * model_dim,
            bytes_accessed=2 * depth * model_dim,
            transcendentals=0,
        ),
    )(*messages, weight)


def sum_kernel(count, *refs):
    out_ref = refs[-1]
    out_ref[...] = tree_sum([r[...].astype(f32) for r in refs[:count]]).astype(out_ref.dtype)


def add_up(terms, dtype, after=()):
    return pl.pallas_call(
        functools.partial(sum_kernel, len(terms)),
        name="add_up",
        out_shape=array(terms[0].shape, dtype),
        in_specs=[whole_vmem()] * len(terms) + [anywhere()] * len(after),
        out_specs=whole_vmem(),
        compiler_params=pltpu.CompilerParams(vmem_limit_bytes=4 * MIB),
    )(*terms, *after)


def encode_kernel(
    arrivals, gain_ref, feat_hbm, keyval_weight_ref, pair_weight_ref, own_ref, *rest
):
    come_refs = rest[:arrivals]
    encoded_ref, normed_ref, keyval_ref, feats_ref, feat, sem = rest[-6:]
    copy = pltpu.make_async_copy(feat_hbm, feat, sem)
    copy.start()
    rows, model_dim = own_ref.shape
    half = rows // 2
    channels = feat.shape[1]
    pick = pick_rows(rows)
    total = own_ref[...]
    for ref in come_refs:
        total = total + ref[...].astype(f32)
    copy.wait()
    skip = jnp.dot(pick, feat[...], preferred_element_type=f32)
    if channels < model_dim:
        skip = jnp.concatenate([skip, jnp.zeros((rows, model_dim - channels), f32)], axis=1)
    total = total + skip
    encoded = jnp.maximum(total[:half], total[half:]).astype(bf16)
    encoded_ref[...] = encoded
    wide = encoded.astype(f32)
    scale = lax.rsqrt(jnp.mean(wide * wide, axis=-1, keepdims=True) + norm_eps)
    normed = (wide * scale * gain_ref[...][None]).astype(bf16)
    normed_ref[...] = normed
    pairs = half // PAIR_POOL
    at = lax.broadcasted_iota(jnp.int32, (pairs, half), 0)
    of = lax.broadcasted_iota(jnp.int32, (pairs, half), 1) // PAIR_POOL
    spread = jnp.where(at == of, 1.0 / PAIR_POOL, 0.0).astype(bf16)
    pooled = jnp.dot(spread, encoded, preferred_element_type=f32).astype(bf16)
    feats_ref[...] = (
        jnp.dot(pooled, pair_weight_ref[...], preferred_element_type=f32)
        .astype(bf16)
        .astype(f32)
    )
    keyval_ref[...] = lax.dot_general(
        normed, keyval_weight_ref[...], (((1,), (1,)), ((), ())), preferred_element_type=f32
    ).astype(bf16)


def encode(own, come, features, gain, keyval_weight_t, pair_weight, after):
    rows, model_dim = own.shape
    half = rows // 2
    columns = keyval_weight_t.shape[0]
    return pl.pallas_call(
        functools.partial(encode_kernel, len(come)),
        name="encode",
        out_shape=[
            array((half, model_dim), bf16),
            array((half, model_dim), bf16),
            array((half, columns), bf16),
            array((half // PAIR_POOL, pair_weight.shape[1]), f32),
        ],
        in_specs=[whole_vmem(), anywhere()]
        + [whole_vmem()] * (3 + len(come))
        + [anywhere()] * len(after),
        out_specs=[whole_vmem()] * 4,
        scratch_shapes=[pltpu.VMEM(features.shape, bf16), pltpu.SemaphoreType.DMA],
        compiler_params=pltpu.CompilerParams(vmem_limit_bytes=8 * MIB),
        cost_estimate=pl.CostEstimate(
            flops=2 * half * model_dim * columns,
            bytes_accessed=6 * rows * model_dim,
            transcendentals=0,
        ),
    )(gain, in_hbm(features), keyval_weight_t, pair_weight, own, *come, *after)


def query_kernel(heads, normed_ref, scale_ref, weight_ref, out_ref):
    columns = weight_ref.shape[1]
    key_dim = columns // heads
    tile = 2 * key_dim
    for n in range(columns // tile):
        at = pl.ds(n * tile, tile)
        got = jnp.dot(normed_ref[...], weight_ref[:, at], preferred_element_type=f32)
        for h in range(2):
            head = n * 2 + h
            piece = got[:, h * key_dim : (h + 1) * key_dim]
            piece = piece * (scale_ref[head] / math.sqrt(key_dim))
            out_ref[:, head * key_dim : (head + 1) * key_dim] = piece.astype(bf16)


def project_queries(normed, weight, scale):
    rows, model_dim = normed.shape
    columns = weight.shape[1]
    return pl.pallas_call(
        functools.partial(query_kernel, scale.shape[0]),
        name="queries",
        out_shape=array((rows, columns), bf16),
        in_specs=[whole_vmem(), smem(), whole_vmem()],
        out_specs=whole_vmem(),
        compiler_params=pltpu.CompilerParams(vmem_limit_bytes=3 * MIB),
        cost_estimate=pl.CostEstimate(
            flops=2 * rows * columns * model_dim,
            bytes_accessed=2 * columns * model_dim,
            transcendentals=0,
        ),
    )(normed, scale, weight)


def attend_kernel(parts, heads, first, last, group, query_ref, start_ref, weight_ref, *rest):
    part_refs = rest[:parts]
    out_ref, keys, values = rest[-3:]
    rows = query_ref.shape[0]
    key_dim = query_ref.shape[1] // heads
    span = part_refs[0].shape[0]
    value_dim = values.shape[1]
    for k in range(parts):
        got = part_refs[k][...]
        keys[k * span : (k + 1) * span, :] = got[:, :key_dim]
        values[k * span : (k + 1) * span, :] = got[:, key_dim:]
    total = start_ref[...].astype(f32)
    for n in range(first, last, group):
        queries = jnp.concatenate(
            [query_ref[:, (n + h) * key_dim : (n + h + 1) * key_dim] for h in range(group)],
            axis=0,
        )
        scores = lax.dot_general(
            queries, keys[...], (((1,), (1,)), ((), ())), preferred_element_type=f32
        )
        weights = jnp.exp(logit_cap * jnp.tanh(scores * (1.0 / logit_cap)))
        sums = jnp.sum(weights, axis=-1, keepdims=True)
        mixed = jnp.dot(weights.astype(bf16), values[...], preferred_element_type=f32) / sums
        mixed = mixed.astype(bf16)
        for h in range(group):
            at = (n + h) * value_dim
            total = total + jnp.dot(
                mixed[h * rows : (h + 1) * rows],
                weight_ref[at : at + value_dim, :],
                preferred_element_type=f32,
            )
    out_ref[...] = total.astype(out_ref.dtype)


def attend(queries, start, output_weight, parts, heads, first, last, dtype, after=()):
    rows, model_dim = start.shape
    key_dim = queries.shape[1] // heads
    value_dim = output_weight.shape[0] // heads
    total_keys = parts[0].shape[0] * len(parts)
    group = 2
    return pl.pallas_call(
        functools.partial(attend_kernel, len(parts), heads, first, last, group),
        name="attend",
        out_shape=array((rows, model_dim), dtype),
        in_specs=[whole_vmem()] * (3 + len(parts)) + [anywhere()] * len(after),
        out_specs=whole_vmem(),
        scratch_shapes=[
            pltpu.VMEM((total_keys, key_dim), bf16),
            pltpu.VMEM((total_keys, value_dim), bf16),
        ],
        compiler_params=pltpu.CompilerParams(
            vmem_limit_bytes=8 * MIB if total_keys <= 1024 else 32 * MIB
        ),
        cost_estimate=pl.CostEstimate(
            flops=2
            * rows
            * (last - first)
            * (total_keys * (key_dim + value_dim) + value_dim * model_dim),
            bytes_accessed=2 * (last - first) * value_dim * model_dim,
            transcendentals=2 * rows * (last - first) * total_keys,
        ),
    )(queries, start, output_weight, *parts, *after)


def split_kernel(parts, input_ref, *rest):
    out_refs = rest[-1 - parts : -1]
    wide = rest[-1]
    rows = input_ref.shape[0]
    chip, core = here()
    me = chip * 2 + core
    wide[...] = input_ref[...].astype(f32)
    for k in range(parts):
        at = pl.ds(pl.multiple_of((me ^ k) * rows, 8), rows)
        out_refs[k][...] = wide[:, at, :].astype(bf16)


def split_pairs(pair_input, parts, after):
    rows, columns, dim = pair_input.shape
    return pl.pallas_call(
        functools.partial(split_kernel, parts),
        name="split_pairs",
        out_shape=[array((rows, rows, dim), bf16)] * parts,
        in_specs=[whole_vmem()] + [anywhere()] * len(after),
        out_specs=[whole_vmem()] * parts,
        scratch_shapes=[pltpu.VMEM((rows, columns, dim), f32)],
        compiler_params=pltpu.CompilerParams(vmem_limit_bytes=4 * MIB),
    )(pair_input, *after)


def pair_kernel(parts, input_ref, cotangent_ref, flip_ref, *rest):
    turned_refs = rest[:parts]
    feat_refs = rest[parts : 2 * parts]
    out_ref, keep_ref, give_ref, stack, mirror, summed, flipped = rest[2 * parts :]
    rows, columns, dim = input_ref.shape
    chip, core = here()
    me = chip * 2 + core
    own = feat_refs[0][...]
    mine_k = own[:, dim:][None]
    for k in range(parts):
        got = feat_refs[k][...]
        stack[k] = got
        value = turned_refs[k][...].astype(f32) + got[:, None, :dim] * mine_k
        mirror[k] = value.reshape(rows * rows, dim).astype(bf16)
    target = lax.broadcasted_iota(jnp.int32, (rows * rows, rows * rows), 0)
    source = lax.broadcasted_iota(jnp.int32, (rows * rows, rows * rows), 1)
    swap = jnp.where(source == (target % rows) * rows + target // rows, 1.0, 0.0).astype(bf16)
    for b in range(parts):
        turned = jnp.dot(swap, mirror[b ^ me], preferred_element_type=f32)
        flipped[:, b * rows : (b + 1) * rows, :] = turned.reshape(rows, rows, dim)
    every = jnp.concatenate([stack[b ^ me] for b in range(parts)], axis=0)[:, dim:]
    for i in range(rows):
        at = pl.ds(i * columns, columns)
        value = input_ref[i].astype(f32) + own[i : i + 1, :dim] * every
        summed[at, :] = value.astype(bf16)
    facing = flipped[...].reshape(rows * columns, dim).astype(bf16)
    update = jnp.dot(facing, flip_ref[...], preferred_element_type=f32)
    update = update + summed[...].astype(f32)
    out_ref[...] = update.astype(bf16).reshape(rows, columns, dim)
    grad = lax.dot_general(
        facing,
        cotangent_ref[...].reshape(rows * columns, dim),
        (((0,), (0,)), ((), ())),
        preferred_element_type=f32,
    )
    low, high = grad[: dim // 2], grad[dim // 2 :]
    keep_ref[...] = jnp.where(core == 0, low, high)
    give_ref[...] = jnp.where(core == 0, high, low)


def pair_update(pair_input, cotangent, flip_weight, turned, feats):
    rows, columns, dim = pair_input.shape
    parts = len(feats)
    return pl.pallas_call(
        functools.partial(pair_kernel, parts),
        name="pair",
        out_shape=[
            array((rows, columns, dim), bf16),
            array((dim // 2, dim), f32),
            array((dim // 2, dim), f32),
        ],
        in_specs=[whole_vmem()] * (3 + 2 * parts),
        out_specs=[whole_vmem()] * 3,
        scratch_shapes=[
            pltpu.VMEM((parts, rows, 2 * dim), f32),
            pltpu.VMEM((parts, rows * rows, dim), bf16),
            pltpu.VMEM((rows * columns, dim), bf16),
            pltpu.VMEM((rows, columns, dim), f32),
        ],
        compiler_params=pltpu.CompilerParams(
            vmem_limit_bytes=4 * MIB if parts <= 8 else 24 * MIB
        ),
        cost_estimate=pl.CostEstimate(
            flops=4 * rows * columns * dim * dim,
            bytes_accessed=8 * rows * columns * dim,
            transcendentals=0,
        ),
    )(pair_input, cotangent, flip_weight, *turned, *feats)


def join_kernel(mine_ref, other_ref, out_ref):
    _, core = here()
    half = mine_ref.shape[0]
    mine, other = mine_ref[...], other_ref[...]
    out_ref[0:half, :] = jnp.where(core == 0, mine, other)
    out_ref[half:, :] = jnp.where(core == 0, other, mine)


def join_halves(mine, other):
    half, dim = mine.shape
    return pl.pallas_call(
        join_kernel,
        name="join_halves",
        out_shape=array((2 * half, dim), f32),
        in_specs=[whole_vmem()] * 2,
        out_specs=whole_vmem(),
        compiler_params=pltpu.CompilerParams(vmem_limit_bytes=2 * MIB),
    )(mine, other)


def per_device(
    features,
    conv_weight,
    norm_gain,
    query_weight,
    keyval_weight,
    head_scale,
    output_weight,
    pair_weight,
    pair_input,
    flip_weight,
    pair_cotangent,
):
    chips = lax.axis_size("seq")
    bits = chips.bit_length() - 1
    windows = lax.axis_size("dp")
    taps = conv_weight.shape[0]
    model_dim = output_weight.shape[1]
    heads = head_scale.shape[0]
    features = features[0]

    masks = [(k, flipped_bits(k, bits)) for k in range(chips)]

    def send(value, mask, flip=0):
        cores = mask if isinstance(mask, tuple) else (mask, mask)
        return lax.ppermute(value, GROUP, hop_pairs(chips, cores, flip))

    strip = send(edge_strip(features, taps // 2), 0, 1)
    own_weight = conv_weight.reshape(-1, model_dim)
    peer_weight = send(own_weight, 0, 1)

    blocks = prep(features, strip, chips)
    messages = [blocks[0]] + [None] * (chips - 1)
    for k in range(chips - 1, 0, -1):
        messages[k] = send(blocks[k], k)
    weight = pack_filter(own_weight, peer_weight, taps, messages[0].shape[1])

    last = chips - 1
    rest = sorted(range(last), key=lambda k: (1 - (k & 1), -k))

    def partials(ks):
        dtypes = [bf16 if k & 1 else f32 for k in ks]
        return dict(zip(ks, conv(messages, weight, taps, ks, dtypes)))

    partial = partials([last])
    partial.update(partials(rest))
    pieces = split_pairs(pair_input[0], 2 * chips, [partial[1]])
    turned = [pieces[0]] + [send(pieces[k], k >> 1, k & 1) for k in range(1, 2 * chips)]
    arrived = []
    for b in range(bits):
        bit = 1 << b
        leaving = [k for k in [last] + rest if k in partial and k & bit]
        got = {k ^ bit: send(partial.pop(k), masks[bit]) for k in leaving}
        for k, value in got.items():
            if k == 0:
                arrived.append(value)
            else:
                goes = k & (2 * bit)
                partial[k] = add_up([partial[k], value], bf16 if goes else f32)

    encoded, normed, keyval, feats = encode(
        partial[0], arrived, features, norm_gain, keyval_weight.T, pair_weight, turned
    )

    def gather(value):
        mine = [value] + [send(value, k) for k in range(chips - 1, 0, -1)][::-1]
        return sum(([v, send(v, 0, 1)] for v in mine), [])

    all_feats = gather(feats)
    keyvals = gather(keyval)
    queries = project_queries(normed, query_weight, head_scale)
    pair_out, keep, give = pair_update(
        pair_input[0], pair_cotangent[0], flip_weight, turned, all_feats
    )
    grad = add_up([keep, send(give, 0, 1)], f32)
    grad = add_up([grad] + [send(grad, k) for k in range(1, chips)], f32)
    grad = add_up(
        [grad]
        + [
            lax.ppermute(grad, "dp", [(w, w ^ k) for w in range(windows)])
            for k in range(1, windows)
        ],
        f32,
    )
    grad = join_halves(grad, send(grad, 0, 1))
    block_out = attend(queries, encoded, output_weight, keyvals, heads, 0, heads, bf16)
    return (block_out[None], pair_out[None], grad)


def solution(mesh):
    placed = (
        P("dp", ("seq", "mp"), None),
        P(None, ("seq", "mp"), None),
        P(),
        P(),
        P(),
        P(),
        P(),
        P(),
        P("dp", ("seq", "mp"), None, None),
        P(),
        P("dp", ("seq", "mp"), None, None),
    )
    return jax.shard_map(
        per_device,
        mesh=mesh,
        in_specs=placed,
        out_specs=(P("dp", ("seq", "mp"), None), P("dp", ("seq", "mp"), None, None), P()),
        check_vma=False,
    )
```

```python
import functools
import math

import jax
import jax.numpy as jnp
from jax import lax
from jax.experimental import pallas as pl
from jax.experimental.pallas import tpu as pltpu
from jax.sharding import PartitionSpec as P

PAIR_POOL = 16
norm_eps = 1e-06
logit_cap = 50.0
MIB = 1 << 20
GROUP = ("seq", "mp")
f32, bf16 = jnp.float32, jnp.bfloat16


def whole_vmem():
    return pl.BlockSpec(memory_space=pltpu.VMEM)


def anywhere():
    return pl.BlockSpec(memory_space=pl.ANY)


def smem():
    return pl.BlockSpec(memory_space=pltpu.SMEM)


def in_hbm(value):
    return pltpu.with_memory_space_constraint(value, pltpu.HBM)


def array(shape, dtype):
    return jax.ShapeDtypeStruct(shape, dtype)


def lane_pad(width):
    return (width + 127) // 128 * 128


def tree_sum(terms):
    while len(terms) > 1:
        terms = [terms[i] + terms[i + 1] for i in range(0, len(terms), 2)]
    return terms[0]


def flipped_bits(mask, bits):
    return sum(((mask >> b) & 1) << (bits - 1 - b) for b in range(bits))


def here():
    return lax.axis_index("seq"), lax.axis_index("mp")


def hop_pairs(chips, core_masks, core_flip):
    pairs = []
    for chip in range(chips):
        for core in range(2):
            target = (chip ^ core_masks[core]) * 2 + (core ^ core_flip)
            pairs.append((chip * 2 + core, target))
    return pairs


def strip_kernel(margin, feat_hbm, out_ref, top, bottom, sems):
    rows = feat_hbm.shape[0]
    copies = [
        pltpu.make_async_copy(feat_hbm.at[0:16, :], top, sems.at[0]),
        pltpu.make_async_copy(feat_hbm.at[rows - 16 : rows, :], bottom, sems.at[1]),
    ]
    for c in copies:
        c.start()
    for c in copies:
        c.wait()
    first = top[...].astype(f32)[:margin]
    last = bottom[...].astype(f32)[16 - margin :]
    rest = jnp.zeros((16 - 2 * margin, first.shape[1]), f32)
    out_ref[...] = jnp.concatenate([first, last, rest], axis=0).astype(bf16)


def edge_strip(features, margin):
    channels = features.shape[1]
    return pl.pallas_call(
        functools.partial(strip_kernel, margin),
        name="edge_strip",
        out_shape=array((16, channels), bf16),
        in_specs=[anywhere()],
        out_specs=whole_vmem(),
        scratch_shapes=[
            pltpu.VMEM((16, channels), bf16),
            pltpu.VMEM((16, channels), bf16),
            pltpu.SemaphoreType.DMA((2,)),
        ],
        compiler_params=pltpu.CompilerParams(vmem_limit_bytes=2 * MIB),
    )(in_hbm(features))


def pick_rows(rows):
    half = rows // 2
    target = lax.broadcasted_iota(jnp.int32, (rows, rows), 0)
    source = lax.broadcasted_iota(jnp.int32, (rows, rows), 1)
    wanted = jnp.where(target < half, 2 * target, 2 * (target - half) + 1)
    return jnp.where(source == wanted, 1.0, 0.0).astype(bf16)


def prep_kernel(chips, width, feat_hbm, pair_hbm, strip_ref, *rest):
    block_refs = rest[:chips]
    feat, pair, wide, split, sems = rest[chips:]
    rows = feat.shape[0]
    chip, _ = here()
    copy = pltpu.make_async_copy(feat_hbm, feat, sems.at[0])
    pair_copy = pltpu.make_async_copy(pair_hbm, pair, sems.at[1])
    copy.start()
    pair_copy.start()
    split[:, :, width:] = jnp.zeros((chips, split.shape[1], split.shape[2] - width), bf16)
    pick = pick_rows(rows)
    wide[rows:, :] = strip_ref[...].astype(f32)
    copy.wait()
    wide[0:rows, :] = jnp.dot(pick, feat[...], preferred_element_type=f32)

    def gelu_rows(at):
        x = wide[at, :]
        v = x * lax.rsqrt(jnp.mean(x * x, axis=-1, keepdims=True) + norm_eps)
        g = (0.5 * v) * (1.0 + lax.erf(v * math.sqrt(0.5)))
        g = g.astype(bf16)
        for q in range(chips):
            split[q, at, 0:width] = g[:, q * width : (q + 1) * width]

    step = 32

    def body(i, carry):
        gelu_rows(pl.ds(pl.multiple_of(i * step, step), step))
        return carry

    lax.fori_loop(0, rows // step, body, 0)
    gelu_rows(pl.ds(rows, wide.shape[0] - rows))
    pair_copy.wait()
    pairs, columns, dim = pair.shape
    lanes = split.shape[2] // dim
    extra = block_refs[0].shape[0] - wide.shape[0]
    for k in range(chips):
        block_refs[k][0 : wide.shape[0], :] = split[chip ^ k]
        at = pl.ds(pl.multiple_of((chip ^ k) * 2 * pairs, 16), 2 * pairs)
        piece = pair[:, at, :].reshape(2 * pairs * pairs, dim)
        for g in range(lanes):
            part = piece[g * extra : (g + 1) * extra]
            to = wide.shape[0]
            block_refs[k][to : to + part.shape[0], g * dim : (g + 1) * dim] = part


def prep(features, strip, pair_input, chips):
    rows, channels = features.shape
    width = channels // chips
    padded = lane_pad(width)
    tall = rows + strip.shape[0]
    pairs, columns, dim = pair_input.shape
    lanes = padded // dim
    extra = -(-2 * pairs * pairs // (16 * lanes)) * 16
    return pl.pallas_call(
        functools.partial(prep_kernel, chips, width),
        name="prep",
        out_shape=[array((tall + extra, padded), bf16)] * chips,
        in_specs=[anywhere(), anywhere(), whole_vmem()],
        out_specs=[whole_vmem()] * chips,
        scratch_shapes=[
            pltpu.VMEM((rows, channels), bf16),
            pltpu.VMEM(pair_input.shape, bf16),
            pltpu.VMEM((tall, channels), f32),
            pltpu.VMEM((chips, tall, padded), bf16),
            pltpu.SemaphoreType.DMA((2,)),
        ],
        compiler_params=pltpu.CompilerParams(vmem_limit_bytes=6 * MIB),
    )(in_hbm(features), in_hbm(pair_input), strip)


def pack_kernel(taps, padded, own_hbm, peer_hbm, out_ref, sems):
    part = own_hbm.shape[0] // taps
    _, core = here()
    copies = []
    for p, source in enumerate((own_hbm, peer_hbm)):
        place = core if p == 0 else 1 - core
        for k in range(taps):
            to = pl.ds(pl.multiple_of(k * padded + place * part, 16), part)
            copies.append(
                pltpu.make_async_copy(
                    source.at[k * part : (k + 1) * part, :], out_ref.at[to, :], sems.at[p, k]
                )
            )
    for c in copies:
        c.start()
    if padded > 2 * part:
        for k in range(taps):
            out_ref[k * padded + 2 * part : (k + 1) * padded, :] = jnp.zeros(
                (padded - 2 * part, out_ref.shape[1]), bf16
            )
    for c in copies:
        c.wait()


def pack_filter(own, peer, taps, padded):
    model_dim = own.shape[1]
    part = own.shape[0] // taps
    if part % 16:
        own, peer = (w.reshape(taps, part, model_dim) for w in (own, peer))
        first = lax.axis_index("mp") == 0
        low, high = jnp.where(first, own, peer), jnp.where(first, peer, own)
        both = jnp.concatenate([low, high], axis=1)
        both = jnp.pad(both, ((0, 0), (0, padded - 2 * part), (0, 0)))
        return both.reshape(taps * padded, model_dim)
    return pl.pallas_call(
        functools.partial(pack_kernel, taps, padded),
        name="pack_filter",
        out_shape=array((taps * padded, model_dim), bf16),
        in_specs=[anywhere()] * 2,
        out_specs=whole_vmem(),
        scratch_shapes=[pltpu.SemaphoreType.DMA((2, taps))],
        compiler_params=pltpu.CompilerParams(vmem_limit_bytes=2 * MIB),
    )(in_hbm(own), peer)


def conv_kernel(chips, bits, taps, tile, wanted, *rest):
    count = len(wanted)
    message_refs = rest[:chips]
    weight_ref = rest[chips]
    out_refs = rest[chips + 1 : chips + 1 + count]
    held, cols = rest[chips + 1 + count :]
    tall, padded = held.shape[1:]
    rows, model_dim = out_refs[0].shape
    half = rows // 2
    chip, core = here()
    for k in range(chips):
        held[k] = message_refs[k][0:tall, :]
    row = lax.broadcasted_iota(jnp.int32, (half, padded), 0)
    for j, k in enumerate(wanted):
        mask = jnp.where(core == 0, k, flipped_bits(k, bits))
        left = (chip ^ mask) - (1 - core)
        right = (chip ^ mask) + core
        block = held[mask]
        before = held[jnp.where(left >= 0, left ^ chip, 0), rows:tall, :].astype(f32)
        before = jnp.where(left >= 0, before, 0.0)
        after = held[jnp.where(right < chips, right ^ chip, 0), rows:tall, :].astype(f32)
        after = jnp.where(right < chips, after, 0.0)
        even = block[0:half].astype(f32)
        odd = block[half:rows].astype(f32)

        def back(v, strip_row):
            return jnp.where(row == 0, before[strip_row : strip_row + 1], pltpu.roll(v, 1, 0))

        def ahead(v, strip_row):
            return jnp.where(
                row == half - 1, after[strip_row : strip_row + 1], pltpu.roll(v, half - 1, 0)
            )

        lagged = [back(even, 2), back(odd, 3), even, odd, ahead(even, 0), ahead(odd, 1)]
        for i, v in enumerate(lagged):
            piece = v.astype(bf16)
            if i < taps:
                cols[j * rows : j * rows + half, i * padded : (i + 1) * padded] = piece
            if i > 0:
                cols[j * rows + half : (j + 1) * rows, (i - 1) * padded : i * padded] = piece
    for j in range(count):
        for n in range(model_dim // tile):
            at = pl.ds(n * tile, tile)
            got = jnp.dot(
                cols[j * rows : (j + 1) * rows], weight_ref[:, at], preferred_element_type=f32
            )
            out_refs[j][:, at] = got.astype(out_refs[j].dtype)


def conv(messages, rows, weight, taps, wanted, dtypes):
    chips = len(messages)
    bits = chips.bit_length() - 1
    padded = messages[0].shape[1]
    tall = rows + 16
    depth, model_dim = weight.shape
    count = len(wanted)
    return pl.pallas_call(
        functools.partial(conv_kernel, chips, bits, taps, 512, wanted),
        name="conv",
        out_shape=[array((rows, model_dim), d) for d in dtypes],
        in_specs=[whole_vmem()] * (chips + 1),
        out_specs=[whole_vmem()] * count,
        scratch_shapes=[
            pltpu.VMEM((chips, tall, padded), bf16),
            pltpu.VMEM((count * rows, depth), bf16),
        ],
        compiler_params=pltpu.CompilerParams(vmem_limit_bytes=(4 + 2 * count) * MIB),
    )(*messages, weight)


def sum_kernel(count, *refs):
    out_ref = refs[-1]
    out_ref[...] = tree_sum([r[...].astype(f32) for r in refs[:count]]).astype(out_ref.dtype)


def add_up(terms, dtype, after=()):
    return pl.pallas_call(
        functools.partial(sum_kernel, len(terms)),
        name="add_up",
        out_shape=array(terms[0].shape, dtype),
        in_specs=[whole_vmem()] * len(terms) + [anywhere()] * len(after),
        out_specs=whole_vmem(),
        compiler_params=pltpu.CompilerParams(vmem_limit_bytes=4 * MIB),
    )(*terms, *after)


def encode_kernel(arrivals, gain_ref, feat_hbm, pair_weight_ref, own_ref, *rest):
    come_refs = rest[:arrivals]
    encoded_ref, normed_ref, feats_ref, feat, sem = rest[-5:]
    copy = pltpu.make_async_copy(feat_hbm, feat, sem)
    copy.start()
    rows, model_dim = own_ref.shape
    half = rows // 2
    channels = feat.shape[1]
    pick = pick_rows(rows)
    total = own_ref[...]
    for ref in come_refs:
        total = total + ref[...].astype(f32)
    copy.wait()
    skip = jnp.dot(pick, feat[...], preferred_element_type=f32)
    if channels < model_dim:
        skip = jnp.concatenate([skip, jnp.zeros((rows, model_dim - channels), f32)], axis=1)
    total = total + skip
    encoded = jnp.maximum(total[:half], total[half:]).astype(bf16)
    encoded_ref[...] = encoded
    wide = encoded.astype(f32)
    scale = lax.rsqrt(jnp.mean(wide * wide, axis=-1, keepdims=True) + norm_eps)
    normed = (wide * scale * gain_ref[...][None]).astype(bf16)
    normed_ref[...] = normed
    pairs = half // PAIR_POOL
    at = lax.broadcasted_iota(jnp.int32, (pairs, half), 0)
    of = lax.broadcasted_iota(jnp.int32, (pairs, half), 1) // PAIR_POOL
    spread = jnp.where(at == of, 1.0 / PAIR_POOL, 0.0).astype(bf16)
    pooled = jnp.dot(spread, encoded, preferred_element_type=f32).astype(bf16)
    feats_ref[...] = (
        jnp.dot(pooled, pair_weight_ref[...], preferred_element_type=f32)
        .astype(bf16)
        .astype(f32)
    )


def encode(own, come, features, gain, pair_weight, after):
    rows, model_dim = own.shape
    half = rows // 2
    return pl.pallas_call(
        functools.partial(encode_kernel, len(come)),
        name="encode",
        out_shape=[
            array((half, model_dim), bf16),
            array((half, model_dim), bf16),
            array((half // PAIR_POOL, pair_weight.shape[1]), f32),
        ],
        in_specs=[whole_vmem(), anywhere()]
        + [whole_vmem()] * (2 + len(come))
        + [anywhere()] * len(after),
        out_specs=[whole_vmem()] * 3,
        scratch_shapes=[pltpu.VMEM(features.shape, bf16), pltpu.SemaphoreType.DMA],
        compiler_params=pltpu.CompilerParams(vmem_limit_bytes=8 * MIB),
    )(gain, in_hbm(features), pair_weight, own, *come, *after)


def bundle_kernel(normed_ref, weight_ref, mine_ref, other_ref, out_ref):
    keyval = lax.dot_general(
        normed_ref[...], weight_ref[...], (((1,), (1,)), ((), ())), preferred_element_type=f32
    )
    rows, columns = keyval.shape
    spare = out_ref.shape[1] - columns
    pieces = []
    for ref in (mine_ref, other_ref):
        feats = ref[...]
        pieces += [feats[:, g : g + spare] for g in range(0, feats.shape[1], spare)]
    used = sum(p.shape[0] for p in pieces)
    pieces.append(jnp.zeros((rows - used, spare), f32))
    out_ref[...] = jnp.concatenate(
        [keyval, jnp.concatenate(pieces, axis=0)], axis=1
    ).astype(bf16)


def bundle(normed, keyval_weight_t, mine, other):
    rows = normed.shape[0]
    return pl.pallas_call(
        bundle_kernel,
        name="bundle",
        out_shape=array((rows, lane_pad(keyval_weight_t.shape[0])), bf16),
        in_specs=[whole_vmem()] * 4,
        out_specs=whole_vmem(),
        compiler_params=pltpu.CompilerParams(vmem_limit_bytes=3 * MIB),
    )(normed, keyval_weight_t, mine, other)


def query_kernel(heads, normed_ref, scale_ref, weight_ref, out_ref):
    columns = weight_ref.shape[1]
    key_dim = columns // heads
    tile = 2 * key_dim
    for n in range(columns // tile):
        at = pl.ds(n * tile, tile)
        got = jnp.dot(normed_ref[...], weight_ref[:, at], preferred_element_type=f32)
        for h in range(2):
            head = n * 2 + h
            piece = got[:, h * key_dim : (h + 1) * key_dim]
            piece = piece * (scale_ref[head] / math.sqrt(key_dim))
            out_ref[:, head * key_dim : (head + 1) * key_dim] = piece.astype(bf16)


def project_queries(normed, weight, scale):
    rows, model_dim = normed.shape
    columns = weight.shape[1]
    return pl.pallas_call(
        functools.partial(query_kernel, scale.shape[0]),
        name="queries",
        out_shape=array((rows, columns), bf16),
        in_specs=[whole_vmem(), smem(), whole_vmem()],
        out_specs=whole_vmem(),
        compiler_params=pltpu.CompilerParams(vmem_limit_bytes=3 * MIB),
    )(normed, scale, weight)


def attend_kernel(parts, heads, first, last, group, query_ref, start_ref, weight_ref, *rest):
    part_refs = rest[:parts]
    out_ref, done_ref, keys, values = rest[-4:]
    rows = query_ref.shape[0]
    key_dim = query_ref.shape[1] // heads
    span = part_refs[0].shape[0]
    value_dim = values.shape[1]
    for k in range(parts):
        got = part_refs[k][...]
        keys[k * span : (k + 1) * span, :] = got[:, :key_dim]
        values[k * span : (k + 1) * span, :] = got[:, key_dim : key_dim + value_dim]
    total = start_ref[...].astype(f32)
    for n in range(first, last, group):
        queries = jnp.concatenate(
            [query_ref[:, (n + h) * key_dim : (n + h + 1) * key_dim] for h in range(group)],
            axis=0,
        )
        scores = lax.dot_general(
            queries, keys[...], (((1,), (1,)), ((), ())), preferred_element_type=f32
        )
        weights = jnp.exp(logit_cap * jnp.tanh(scores * (1.0 / logit_cap)))
        sums = jnp.sum(weights, axis=-1, keepdims=True)
        mixed = jnp.dot(weights.astype(bf16), values[...], preferred_element_type=f32) / sums
        mixed = mixed.astype(bf16)
        for h in range(group):
            at = (n + h) * value_dim
            total = total + jnp.dot(
                mixed[h * rows : (h + 1) * rows],
                weight_ref[at : at + value_dim, :],
                preferred_element_type=f32,
            )
    out_ref[...] = total.astype(out_ref.dtype)
    done_ref[...] = total[0:8, 0:128]


def attend(queries, start, output_weight, parts, heads, first, last, dtype, after=()):
    rows, model_dim = start.shape
    key_dim = queries.shape[1] // heads
    value_dim = output_weight.shape[0] // heads
    total_keys = parts[0].shape[0] * len(parts)
    group = 2
    return pl.pallas_call(
        functools.partial(attend_kernel, len(parts), heads, first, last, group),
        name="attend",
        out_shape=[array((rows, model_dim), dtype), array((8, 128), f32)],
        in_specs=[whole_vmem()] * (3 + len(parts)) + [anywhere()] * len(after),
        out_specs=[whole_vmem()] * 2,
        scratch_shapes=[
            pltpu.VMEM((total_keys, key_dim), bf16),
            pltpu.VMEM((total_keys, value_dim), bf16),
        ],
        compiler_params=pltpu.CompilerParams(
            vmem_limit_bytes=8 * MIB if total_keys <= 1024 else 32 * MIB
        ),
    )(queries, start, output_weight, *parts, *after)


def unpack_kernel(chips, pairs, tall, *refs):
    message_refs = refs[:chips]
    keep_ref, give_ref, wide = refs[-3:]
    _, core = here()
    dim = keep_ref.shape[3]
    padded = message_refs[0].shape[1]
    for k in range(chips):
        piece = message_refs[k][tall:, :]
        piece = jnp.concatenate([piece[:, g : g + dim] for g in range(0, padded, dim)], axis=0)
        piece = piece[: 2 * pairs * pairs].astype(f32)
        wide[...] = piece.reshape(pairs, 2 * pairs, dim)
        mine = pl.ds(pl.multiple_of(core * pairs, 8), pairs)
        other = pl.ds(pl.multiple_of((1 - core) * pairs, 8), pairs)
        keep_ref[k] = wide[:, mine, :].astype(bf16)
        give_ref[k] = wide[:, other, :].astype(bf16)


def unpack_pairs(messages, pairs, dim, tall, after):
    chips = len(messages)
    return pl.pallas_call(
        functools.partial(unpack_kernel, chips, pairs, tall),
        name="unpack_pairs",
        out_shape=[array((chips, pairs, pairs, dim), bf16)] * 2,
        in_specs=[whole_vmem()] * chips + [anywhere()] * len(after),
        out_specs=[whole_vmem()] * 2,
        scratch_shapes=[pltpu.VMEM((pairs, 2 * pairs, dim), f32)],
        compiler_params=pltpu.CompilerParams(vmem_limit_bytes=4 * MIB),
    )(*messages, *after)


def pair_kernel(parts, columns_used, input_ref, cotangent_ref, flip_ref, *rest):
    turned_refs = rest[:2]
    bundle_refs = rest[2 : 2 + parts // 2]
    out_ref, keep_ref, give_ref, stack, mirror, summed, flipped = rest[-7:]
    rows, columns, dim = input_ref.shape
    chip, core = here()
    me = chip * 2 + core
    for k in range(parts // 2):
        got = bundle_refs[k][:, columns_used:].astype(f32)
        spare = got.shape[1]
        count = 2 * dim // spare
        for f in range(2):
            at = f * count * rows
            pieces = [got[at + g * rows : at + (g + 1) * rows] for g in range(count)]
            stack[2 * k + f] = jnp.concatenate(pieces, axis=1)
    own = stack[0]
    mine_k = own[:, dim:][None]
    for k in range(parts):
        got = stack[k]
        value = turned_refs[k % 2][k // 2].astype(f32) + got[:, None, :dim] * mine_k
        mirror[k] = value.reshape(rows * rows, dim).astype(bf16)
    target = lax.broadcasted_iota(jnp.int32, (rows * rows, rows * rows), 0)
    source = lax.broadcasted_iota(jnp.int32, (rows * rows, rows * rows), 1)
    swap = jnp.where(source == (target % rows) * rows + target // rows, 1.0, 0.0).astype(bf16)
    for b in range(parts):
        turned = jnp.dot(swap, mirror[b ^ me], preferred_element_type=f32)
        flipped[:, b * rows : (b + 1) * rows, :] = turned.reshape(rows, rows, dim)
    every = jnp.concatenate([stack[b ^ me] for b in range(parts)], axis=0)[:, dim:]
    for i in range(rows):
        at = pl.ds(i * columns, columns)
        value = input_ref[i].astype(f32) + own[i : i + 1, :dim] * every
        summed[at, :] = value.astype(bf16)
    facing = flipped[...].reshape(rows * columns, dim).astype(bf16)
    update = jnp.dot(facing, flip_ref[...], preferred_element_type=f32)
    update = update + summed[...].astype(f32)
    out_ref[...] = update.astype(bf16).reshape(rows, columns, dim)
    grad = lax.dot_general(
        facing,
        cotangent_ref[...].reshape(rows * columns, dim),
        (((0,), (0,)), ((), ())),
        preferred_element_type=f32,
    )
    low, high = grad[: dim // 2], grad[dim // 2 :]
    keep_ref[...] = jnp.where(core == 0, low, high)
    give_ref[...] = jnp.where(core == 0, high, low)


def pair_update(pair_input, cotangent, flip_weight, turned, bundles, columns_used, after):
    rows, columns, dim = pair_input.shape
    parts = 2 * len(bundles)
    return pl.pallas_call(
        functools.partial(pair_kernel, parts, columns_used),
        name="pair",
        out_shape=[
            array((rows, columns, dim), bf16),
            array((dim // 2, dim), f32),
            array((dim // 2, dim), f32),
        ],
        in_specs=[whole_vmem()] * (5 + len(bundles)) + [anywhere()] * len(after),
        out_specs=[whole_vmem()] * 3,
        scratch_shapes=[
            pltpu.VMEM((parts, rows, 2 * dim), f32),
            pltpu.VMEM((parts, rows * rows, dim), bf16),
            pltpu.VMEM((rows * columns, dim), bf16),
            pltpu.VMEM((rows, columns, dim), f32),
        ],
        compiler_params=pltpu.CompilerParams(
            vmem_limit_bytes=4 * MIB if parts <= 8 else 24 * MIB
        ),
    )(pair_input, cotangent, flip_weight, *turned, *bundles, *after)


def join_kernel(mine_ref, other_ref, out_ref):
    _, core = here()
    half = mine_ref.shape[0]
    mine, other = mine_ref[...], other_ref[...]
    out_ref[0:half, :] = jnp.where(core == 0, mine, other)
    out_ref[half:, :] = jnp.where(core == 0, other, mine)


def join_halves(mine, other):
    half, dim = mine.shape
    return pl.pallas_call(
        join_kernel,
        name="join_halves",
        out_shape=array((2 * half, dim), f32),
        in_specs=[whole_vmem()] * 2,
        out_specs=whole_vmem(),
        compiler_params=pltpu.CompilerParams(vmem_limit_bytes=2 * MIB),
    )(mine, other)


def per_device(
    features,
    conv_weight,
    norm_gain,
    query_weight,
    keyval_weight,
    head_scale,
    output_weight,
    pair_weight,
    pair_input,
    flip_weight,
    pair_cotangent,
):
    chips = lax.axis_size("seq")
    bits = chips.bit_length() - 1
    windows = lax.axis_size("dp")
    taps = conv_weight.shape[0]
    model_dim = output_weight.shape[1]
    heads = head_scale.shape[0]
    features = features[0]

    masks = [(k, flipped_bits(k, bits)) for k in range(chips)]

    def send(value, mask, flip=0):
        cores = mask if isinstance(mask, tuple) else (mask, mask)
        return lax.ppermute(value, GROUP, hop_pairs(chips, cores, flip))

    strip = send(edge_strip(features, taps // 2), 0, 1)
    own_weight = conv_weight.reshape(-1, model_dim)
    own_weight, strip = lax.optimization_barrier((own_weight, strip))
    peer_weight = send(own_weight, 0, 1)

    blocks = prep(features, strip, pair_input[0], chips)
    messages = [blocks[0]] + [None] * (chips - 1)
    for k in range(chips - 1, 0, -1):
        messages[k] = send(blocks[k], k)
    weight = pack_filter(own_weight, peer_weight, taps, messages[0].shape[1])

    last = chips - 1
    rest = sorted(range(last), key=lambda k: (1 - (k & 1), -k))

    def partials(ks):
        dtypes = [bf16 if k & 1 else f32 for k in ks]
        return dict(zip(ks, conv(messages, features.shape[0], weight, taps, ks, dtypes)))

    partial = partials([last])
    partial.update(partials(rest))
    pairs, _, pair_dim = pair_input.shape[1:]
    kept, given = unpack_pairs(
        messages, pairs, pair_dim, features.shape[0] + strip.shape[0], [partial[1]]
    )
    turned = [kept, send(given, 0, 1)]
    arrived = []
    for b in range(bits):
        bit = 1 << b
        leaving = [k for k in [last] + rest if k in partial and k & bit]
        got = {k ^ bit: send(partial.pop(k), masks[bit]) for k in leaving}
        for k, value in got.items():
            if k == 0:
                arrived.append(value)
            else:
                goes = k & (2 * bit)
                partial[k] = add_up([partial[k], value], bf16 if goes else f32)

    encoded, normed, feats = encode(
        partial[0], arrived, features, norm_gain, pair_weight, turned
    )
    own_bundle = bundle(normed, keyval_weight.T, feats, send(feats, 0, 1))
    bundles = [own_bundle] + [send(own_bundle, k) for k in range(chips - 1, 0, -1)][::-1]
    queries = project_queries(normed, query_weight, head_scale)
    pair_out, keep, give = pair_update(
        pair_input[0],
        pair_cotangent[0],
        flip_weight,
        turned,
        bundles,
        keyval_weight.shape[1],
        [queries],
    )
    keyvals = bundles + [send(v, 0, 1) for v in bundles]
    grad = add_up([keep, send(give, 0, 1)], f32)
    halfway = heads // 2
    first_half, done = attend(queries, encoded, output_weight, keyvals, heads, 0, halfway, f32)
    grad = add_up([grad] + [send(grad, k) for k in range(1, chips)], f32, [done])
    block_out, done = attend(
        queries, first_half, output_weight, keyvals, heads, halfway, heads, bf16, [grad]
    )
    grad = add_up(
        [grad]
        + [
            lax.ppermute(grad, "dp", [(w, w ^ k) for w in range(windows)])
            for k in range(1, windows)
        ],
        f32,
        [done],
    )
    grad = join_halves(grad, send(grad, 0, 1))
    return (block_out[None], pair_out[None], grad)


def solution(mesh):
    placed = (
        P("dp", ("seq", "mp"), None),
        P(None, ("seq", "mp"), None),
        P(),
        P(),
        P(),
        P(),
        P(),
        P(),
        P("dp", ("seq", "mp"), None, None),
        P(),
        P("dp", ("seq", "mp"), None, None),
    )
    return jax.shard_map(
        per_device,
        mesh=mesh,
        in_specs=placed,
        out_specs=(P("dp", ("seq", "mp"), None), P("dp", ("seq", "mp"), None, None), P()),
        check_vma=False,
    )
```

```python
import functools
import math

import jax
import jax.numpy as jnp
from jax import lax
from jax.experimental import pallas as pl
from jax.experimental.pallas import tpu as pltpu
from jax.sharding import PartitionSpec as P

PAIR_POOL = 16
norm_eps = 1e-06
logit_cap = 50.0
MIB = 1 << 20
GROUP = ("seq", "mp")
f32, bf16 = jnp.float32, jnp.bfloat16


def whole_vmem():
    return pl.BlockSpec(memory_space=pltpu.VMEM)


def anywhere():
    return pl.BlockSpec(memory_space=pl.ANY)


def smem():
    return pl.BlockSpec(memory_space=pltpu.SMEM)


def in_hbm(value):
    return pltpu.with_memory_space_constraint(value, pltpu.HBM)


def array(shape, dtype):
    return jax.ShapeDtypeStruct(shape, dtype)


def lane_pad(width):
    return (width + 127) // 128 * 128


def tree_sum(terms):
    while len(terms) > 1:
        terms = [terms[i] + terms[i + 1] for i in range(0, len(terms), 2)]
    return terms[0]


def flipped_bits(mask, bits):
    return sum(((mask >> b) & 1) << (bits - 1 - b) for b in range(bits))


def here():
    return lax.axis_index("seq"), lax.axis_index("mp")


def hop_pairs(chips, core_masks, core_flip):
    pairs = []
    for chip in range(chips):
        for core in range(2):
            target = (chip ^ core_masks[core]) * 2 + (core ^ core_flip)
            pairs.append((chip * 2 + core, target))
    return pairs


def strip_kernel(margin, feat_hbm, out_ref, top, bottom, sems):
    rows = feat_hbm.shape[0]
    copies = [
        pltpu.make_async_copy(feat_hbm.at[0:16, :], top, sems.at[0]),
        pltpu.make_async_copy(feat_hbm.at[rows - 16 : rows, :], bottom, sems.at[1]),
    ]
    for c in copies:
        c.start()
    for c in copies:
        c.wait()
    first = top[...].astype(f32)[:margin]
    last = bottom[...].astype(f32)[16 - margin :]
    rest = jnp.zeros((16 - 2 * margin, first.shape[1]), f32)
    out_ref[...] = jnp.concatenate([first, last, rest], axis=0).astype(bf16)


def edge_strip(features, margin):
    channels = features.shape[1]
    return pl.pallas_call(
        functools.partial(strip_kernel, margin),
        name="edge_strip",
        out_shape=array((16, channels), bf16),
        in_specs=[anywhere()],
        out_specs=whole_vmem(),
        scratch_shapes=[
            pltpu.VMEM((16, channels), bf16),
            pltpu.VMEM((16, channels), bf16),
            pltpu.SemaphoreType.DMA((2,)),
        ],
        compiler_params=pltpu.CompilerParams(vmem_limit_bytes=2 * MIB),
    )(in_hbm(features))


def pick_rows(rows):
    half = rows // 2
    target = lax.broadcasted_iota(jnp.int32, (rows, rows), 0)
    source = lax.broadcasted_iota(jnp.int32, (rows, rows), 1)
    wanted = jnp.where(target < half, 2 * target, 2 * (target - half) + 1)
    return jnp.where(source == wanted, 1.0, 0.0).astype(bf16)


def gelu_rows(x, out_ref, at, chips, width):
    v = x * lax.rsqrt(jnp.mean(x * x, axis=-1, keepdims=True) + norm_eps)
    g = (0.5 * v) * (1.0 + lax.erf(v * math.sqrt(0.5)))
    g = g.astype(bf16)
    for q in range(chips):
        out_ref[q, at, 0:width] = g[:, q * width : (q + 1) * width]


def prep_kernel(chips, width, feat_hbm, pair_hbm, *rest):
    block_refs = rest[:chips]
    feat, pair, wide, split, sems = rest[chips:]
    rows = feat.shape[0]
    chip, _ = here()
    copy = pltpu.make_async_copy(feat_hbm, feat, sems.at[0])
    pair_copy = pltpu.make_async_copy(pair_hbm, pair, sems.at[1])
    copy.start()
    pair_copy.start()
    split[:, :, width:] = jnp.zeros((chips, rows, split.shape[2] - width), bf16)
    pick = pick_rows(rows)
    copy.wait()
    wide[...] = jnp.dot(pick, feat[...], preferred_element_type=f32)
    step = 32

    def body(i, carry):
        at = pl.ds(pl.multiple_of(i * step, step), step)
        gelu_rows(wide[at, :], split, at, chips, width)
        return carry

    lax.fori_loop(0, rows // step, body, 0)
    pair_copy.wait()
    pairs, _, dim = pair.shape
    lanes = split.shape[2] // dim
    extra = block_refs[0].shape[0] - rows - 16
    for k in range(chips):
        block_refs[k][0:rows, :] = split[chip ^ k]
        at = pl.ds(pl.multiple_of((chip ^ k) * 2 * pairs, 16), 2 * pairs)
        piece = pair[:, at, :].reshape(2 * pairs * pairs, dim)
        for g in range(lanes):
            part = piece[g * extra : (g + 1) * extra]
            to = rows + 16
            block_refs[k][to : to + part.shape[0], g * dim : (g + 1) * dim] = part


def prep(features, pair_input, chips):
    rows, channels = features.shape
    width = channels // chips
    padded = lane_pad(width)
    pairs, _, dim = pair_input.shape
    extra = -(-2 * pairs * pairs // (16 * (padded // dim))) * 16
    return pl.pallas_call(
        functools.partial(prep_kernel, chips, width),
        name="prep",
        out_shape=[array((rows + 16 + extra, padded), bf16)] * chips,
        in_specs=[anywhere()] * 2,
        out_specs=[whole_vmem()] * chips,
        scratch_shapes=[
            pltpu.VMEM((rows, channels), bf16),
            pltpu.VMEM(pair_input.shape, bf16),
            pltpu.VMEM((rows, channels), f32),
            pltpu.VMEM((chips, rows, padded), bf16),
            pltpu.SemaphoreType.DMA((2,)),
        ],
        compiler_params=pltpu.CompilerParams(vmem_limit_bytes=6 * MIB),
    )(in_hbm(features), in_hbm(pair_input))


def edges_kernel(chips, width, rows, strip_ref, *rest):
    block_refs = rest[chips : 2 * chips]
    split = rest[2 * chips]
    chip, _ = here()
    split[:, :, width:] = jnp.zeros((chips, 16, split.shape[2] - width), bf16)
    gelu_rows(strip_ref[...].astype(f32), split, pl.ds(0, 16), chips, width)
    for k in range(chips):
        block_refs[k][rows : rows + 16, :] = split[chip ^ k]


def add_edges(blocks, strip, rows):
    chips = len(blocks)
    width = strip.shape[1] // chips
    padded = blocks[0].shape[1]
    return pl.pallas_call(
        functools.partial(edges_kernel, chips, width, rows),
        name="add_edges",
        out_shape=[array(b.shape, bf16) for b in blocks],
        in_specs=[whole_vmem()] * (1 + chips),
        out_specs=[whole_vmem()] * chips,
        scratch_shapes=[pltpu.VMEM((chips, 16, padded), bf16)],
        input_output_aliases={1 + k: k for k in range(chips)},
        compiler_params=pltpu.CompilerParams(vmem_limit_bytes=2 * MIB),
    )(strip, *blocks)


def pack_kernel(taps, padded, own_hbm, peer_hbm, out_ref, sems):
    part = own_hbm.shape[0] // taps
    _, core = here()
    copies = []
    for p, source in enumerate((own_hbm, peer_hbm)):
        place = core if p == 0 else 1 - core
        for k in range(taps):
            to = pl.ds(pl.multiple_of(k * padded + place * part, 16), part)
            copies.append(
                pltpu.make_async_copy(
                    source.at[k * part : (k + 1) * part, :], out_ref.at[to, :], sems.at[p, k]
                )
            )
    for c in copies:
        c.start()
    if padded > 2 * part:
        for k in range(taps):
            out_ref[k * padded + 2 * part : (k + 1) * padded, :] = jnp.zeros(
                (padded - 2 * part, out_ref.shape[1]), bf16
            )
    for c in copies:
        c.wait()


def pack_filter(own, peer, taps, padded):
    model_dim = own.shape[1]
    part = own.shape[0] // taps
    if part % 16:
        own, peer = (w.reshape(taps, part, model_dim) for w in (own, peer))
        first = lax.axis_index("mp") == 0
        low, high = jnp.where(first, own, peer), jnp.where(first, peer, own)
        both = jnp.concatenate([low, high], axis=1)
        both = jnp.pad(both, ((0, 0), (0, padded - 2 * part), (0, 0)))
        return both.reshape(taps * padded, model_dim)
    return pl.pallas_call(
        functools.partial(pack_kernel, taps, padded),
        name="pack_filter",
        out_shape=array((taps * padded, model_dim), bf16),
        in_specs=[anywhere()] * 2,
        out_specs=whole_vmem(),
        scratch_shapes=[pltpu.SemaphoreType.DMA((2, taps))],
        compiler_params=pltpu.CompilerParams(vmem_limit_bytes=2 * MIB),
    )(in_hbm(own), peer)


def conv_kernel(chips, bits, taps, tile, wanted, first, outs, feat_hbm, *rest):
    count = len(wanted)
    message_refs = rest[:chips][::-1]
    weight_ref = rest[chips]
    held, cols, feat, sem = rest[-4:]
    out_refs = rest[-4 - outs : -4]
    tall, padded = held.shape[1:]
    rows = tall - 16
    half = rows // 2
    chip, core = here()
    if 0 in wanted:
        copy = pltpu.make_async_copy(feat_hbm, feat, sem)
        copy.start()
    for k in range(chips):
        held[k] = message_refs[k][0:tall, :]
    row = lax.broadcasted_iota(jnp.int32, (half, padded), 0)
    for j, k in enumerate(wanted):
        mask = jnp.where(core == 0, k, flipped_bits(k, bits))
        left = (chip ^ mask) - (1 - core)
        right = (chip ^ mask) + core
        block = held[mask]
        before = held[jnp.where(left >= 0, left ^ chip, 0), rows:tall, :].astype(f32)
        before = jnp.where(left >= 0, before, 0.0)
        after = held[jnp.where(right < chips, right ^ chip, 0), rows:tall, :].astype(f32)
        after = jnp.where(right < chips, after, 0.0)
        even = block[0:half].astype(f32)
        odd = block[half:rows].astype(f32)

        def back(v, strip_row):
            return jnp.where(row == 0, before[strip_row : strip_row + 1], pltpu.roll(v, 1, 0))

        def ahead(v, strip_row):
            return jnp.where(
                row == half - 1, after[strip_row : strip_row + 1], pltpu.roll(v, half - 1, 0)
            )

        lagged = [back(even, 2), back(odd, 3), even, odd, ahead(even, 0), ahead(odd, 1)]
        for i, v in enumerate(lagged):
            piece = v.astype(bf16)
            if i < taps:
                cols[j * rows : j * rows + half, i * padded : (i + 1) * padded] = piece
            if i > 0:
                cols[j * rows + half : (j + 1) * rows, (i - 1) * padded : i * padded] = piece
    pick = pick_rows(rows)
    if 0 in wanted:
        copy.wait()
    halves = len(out_refs) // count
    span = out_refs[0].shape[1]
    for j, k in enumerate(wanted):
        for h in range(halves):
            for n in range(0, span, tile):
                at = first + h * span + n
                got = jnp.dot(
                    cols[j * rows : (j + 1) * rows],
                    weight_ref[:, at : at + tile],
                    preferred_element_type=f32,
                )
                if k == 0 and at < feat.shape[1]:
                    width = min(tile, feat.shape[1] - at)
                    skip = jnp.dot(
                        pick, feat[:, at : at + width], preferred_element_type=f32
                    )
                    if width < tile:
                        skip = jnp.concatenate(
                            [skip, jnp.zeros((rows, tile - width), f32)], axis=1
                        )
                    got = got + skip
                out_refs[j * halves + h][:, n : n + tile] = got.astype(out_refs[j * halves].dtype)


def conv(messages, features, weight, taps, wanted, dtypes, columns, after):
    chips = len(messages)
    bits = chips.bit_length() - 1
    padded = messages[0].shape[1]
    depth, model_dim = weight.shape
    rows = features.shape[0]
    tall = rows + 16
    count = len(wanted)
    first, last = columns
    span = model_dim // 2
    halves = (last - first) // span
    got = pl.pallas_call(
        functools.partial(
            conv_kernel, chips, bits, taps, 256, wanted, first, count * halves
        ),
        name="conv",
        out_shape=[array((rows, span), d) for d in dtypes for _ in range(halves)],
        in_specs=[anywhere()] + [whole_vmem()] * (chips + 1) + [anywhere()] * len(after),
        out_specs=[whole_vmem()] * (count * halves),
        scratch_shapes=[
            pltpu.VMEM((chips, tall, padded), bf16),
            pltpu.VMEM((count * rows, depth), bf16),
            pltpu.VMEM(features.shape, bf16),
            pltpu.SemaphoreType.DMA,
        ],
        compiler_params=pltpu.CompilerParams(vmem_limit_bytes=(5 + 2 * count) * MIB),
    )(in_hbm(features), *messages[::-1], weight, *after)
    return [got[j * halves : (j + 1) * halves] for j in range(count)]


def sum_kernel(count, *refs):
    out_ref = refs[-1]
    out_ref[...] = tree_sum([r[...].astype(f32) for r in refs[:count][::-1]]).astype(out_ref.dtype)


def add_up(terms, dtype, after=()):
    return pl.pallas_call(
        functools.partial(sum_kernel, len(terms)),
        name="add_up",
        out_shape=array(terms[0].shape, dtype),
        in_specs=[whole_vmem()] * len(terms) + [anywhere()] * len(after),
        out_specs=whole_vmem(),
        compiler_params=pltpu.CompilerParams(vmem_limit_bytes=4 * MIB),
    )(*terms[::-1], *after)


def encode_kernel(pieces, arrivals, pair_weight_ref, *rest):
    own_refs = rest[:pieces]
    come_refs = rest[pieces : pieces + arrivals * pieces]
    encoded_ref, feats_ref = rest[-2:]
    rows, span = own_refs[0].shape
    half = rows // 2
    pairs = half // PAIR_POOL
    at = lax.broadcasted_iota(jnp.int32, (pairs, half), 0)
    of = lax.broadcasted_iota(jnp.int32, (pairs, half), 1) // PAIR_POOL
    spread = jnp.where(at == of, 1.0 / PAIR_POOL, 0.0).astype(bf16)
    feats = jnp.zeros(feats_ref.shape, f32)
    for h in range(pieces):
        total = own_refs[h][...]
        for a in range(arrivals):
            total = total + come_refs[a * pieces + h][...].astype(f32)
        encoded = jnp.maximum(total[:half], total[half:]).astype(bf16)
        encoded_ref[:, h * span : (h + 1) * span] = encoded
        pooled = jnp.dot(spread, encoded, preferred_element_type=f32).astype(bf16)
        feats = feats + jnp.dot(
            pooled, pair_weight_ref[h * span : (h + 1) * span, :], preferred_element_type=f32
        )
    feats_ref[...] = feats.astype(bf16).astype(f32)


def encode(own, come, pair_weight, after):
    rows, span = own[0].shape
    pieces = len(own)
    half = rows // 2
    return pl.pallas_call(
        functools.partial(encode_kernel, pieces, len(come)),
        name="encode",
        out_shape=[
            array((half, span * pieces), bf16),
            array((half // PAIR_POOL, pair_weight.shape[1]), f32),
        ],
        in_specs=[whole_vmem()] * (1 + pieces * (1 + len(come))) + [anywhere()] * len(after),
        out_specs=[whole_vmem()] * 2,
        compiler_params=pltpu.CompilerParams(vmem_limit_bytes=8 * MIB),
    )(pair_weight, *own, *sum(come, []), *after)


def normalised(encoded_ref, gain_ref):
    wide = encoded_ref[...].astype(f32)
    scale = lax.rsqrt(jnp.mean(wide * wide, axis=-1, keepdims=True) + norm_eps)
    return (wide * scale * gain_ref[...][None]).astype(bf16)


def bundle_kernel(encoded_ref, gain_ref, weight_ref, mine_ref, other_ref, out_ref):
    keyval = lax.dot_general(
        normalised(encoded_ref, gain_ref),
        weight_ref[...],
        (((1,), (1,)), ((), ())),
        preferred_element_type=f32,
    )
    rows, columns = keyval.shape
    spare = out_ref.shape[1] - columns
    pieces = []
    for ref in (mine_ref, other_ref):
        feats = ref[...]
        pieces += [feats[:, g : g + spare] for g in range(0, feats.shape[1], spare)]
    used = sum(p.shape[0] for p in pieces)
    pieces.append(jnp.zeros((rows - used, spare), f32))
    out_ref[...] = jnp.concatenate(
        [keyval, jnp.concatenate(pieces, axis=0)], axis=1
    ).astype(bf16)


def bundle(encoded, gain, weight_t, mine, other):
    return pl.pallas_call(
        bundle_kernel,
        name="bundle",
        out_shape=array((encoded.shape[0], lane_pad(weight_t.shape[0])), bf16),
        in_specs=[whole_vmem()] * 5,
        out_specs=whole_vmem(),
        compiler_params=pltpu.CompilerParams(vmem_limit_bytes=4 * MIB),
    )(encoded, gain, weight_t, mine, other)


def attend_kernel(
    parts,
    heads,
    first,
    last,
    group,
    scale_ref,
    encoded_ref,
    gain_ref,
    query_weight_ref,
    start_ref,
    weight_ref,
    *rest,
):
    part_refs = rest[:parts]
    out_ref, done_ref, keys, values = rest[-4:]
    rows = encoded_ref.shape[0]
    key_dim = query_weight_ref.shape[1] // heads
    normed = normalised(encoded_ref, gain_ref)
    span = part_refs[0].shape[0]
    value_dim = values.shape[1]
    for k in range(parts):
        got = part_refs[k][...]
        keys[k * span : (k + 1) * span, :] = got[:, :key_dim]
        values[k * span : (k + 1) * span, :] = got[:, key_dim : key_dim + value_dim]
    total = start_ref[...].astype(f32)
    for n in range(first, last, group):
        got = jnp.dot(
            normed,
            query_weight_ref[:, n * key_dim : (n + group) * key_dim],
            preferred_element_type=f32,
        )
        queries = jnp.concatenate(
            [
                got[:, h * key_dim : (h + 1) * key_dim]
                * (scale_ref[n + h] / math.sqrt(key_dim))
                for h in range(group)
            ],
            axis=0,
        ).astype(bf16)
        scores = lax.dot_general(
            queries, keys[...], (((1,), (1,)), ((), ())), preferred_element_type=f32
        )
        weights = jnp.exp(logit_cap * jnp.tanh(scores * (1.0 / logit_cap)))
        sums = jnp.sum(weights, axis=-1, keepdims=True)
        mixed = jnp.dot(weights.astype(bf16), values[...], preferred_element_type=f32) / sums
        mixed = mixed.astype(bf16)
        for h in range(group):
            at = (n + h) * value_dim
            total = total + jnp.dot(
                mixed[h * rows : (h + 1) * rows],
                weight_ref[at : at + value_dim, :],
                preferred_element_type=f32,
            )
    out_ref[...] = total.astype(out_ref.dtype)
    done_ref[...] = total[0:8, 0:128]


def attend(
    encoded, gain, query_weight, scale, start, output_weight, parts, first, last, dtype, after
):
    rows, model_dim = start.shape
    heads = scale.shape[0]
    key_dim = query_weight.shape[1] // heads
    value_dim = output_weight.shape[0] // heads
    total_keys = parts[0].shape[0] * len(parts)
    group = 2
    return pl.pallas_call(
        functools.partial(attend_kernel, len(parts), heads, first, last, group),
        name="attend",
        out_shape=[array((rows, model_dim), dtype), array((8, 128), f32)],
        in_specs=[smem()] + [whole_vmem()] * (5 + len(parts)) + [anywhere()] * len(after),
        out_specs=[whole_vmem()] * 2,
        scratch_shapes=[
            pltpu.VMEM((total_keys, key_dim), bf16),
            pltpu.VMEM((total_keys, value_dim), bf16),
        ],
        compiler_params=pltpu.CompilerParams(
            vmem_limit_bytes=8 * MIB if total_keys <= 1024 else 32 * MIB
        ),
    )(scale, encoded, gain, query_weight, start, output_weight, *parts, *after)


def unpack_kernel(chips, pairs, tall, *refs):
    message_refs = refs[:chips][::-1]
    out_ref = refs[-1]
    dim = out_ref.shape[2]
    padded = message_refs[0].shape[1]
    for k in range(chips):
        piece = message_refs[k][tall:, :]
        piece = jnp.concatenate([piece[:, g : g + dim] for g in range(0, padded, dim)], axis=0)
        piece = piece[: 2 * pairs * pairs].reshape(pairs, 2 * pairs, dim)
        out_ref[k * pairs : (k + 1) * pairs] = piece


def unpack_pairs(messages, pairs, dim, tall, after):
    chips = len(messages)
    return pl.pallas_call(
        functools.partial(unpack_kernel, chips, pairs, tall),
        name="unpack_pairs",
        out_shape=array((chips * pairs, 2 * pairs, dim), bf16),
        in_specs=[whole_vmem()] * chips + [anywhere()] * len(after),
        out_specs=whole_vmem(),
        compiler_params=pltpu.CompilerParams(vmem_limit_bytes=4 * MIB),
    )(*messages[::-1], *after)


def pair_kernel(
    chips, columns_used, input_ref, cotangent_ref, other_cotangent_ref, flip_ref, turned_ref, other_ref, *rest
):
    bundle_refs = rest[:chips][::-1]
    out_ref, grad_ref, stacked, mirror, summed, flipped, cotangent = rest[-7:]
    rows, columns, dim = input_ref.shape
    parts = 2 * chips
    wide = 2 * rows
    chip, core = here()
    me = chip * 2 + core
    for k in range(chips):
        got = bundle_refs[k][:, columns_used:].astype(f32)
        count = 2 * dim // got.shape[1]
        for f in range(2):
            at = f * count * rows
            stacked[2 * k + f] = jnp.concatenate(
                [got[at + g * rows : at + (g + 1) * rows] for g in range(count)], axis=1
            )
    own, other = stacked[0], stacked[1]
    both_k = jnp.concatenate(
        [jnp.where(core == 0, own, other), jnp.where(core == 0, other, own)], axis=0
    )[:, dim:][None]
    for k in range(parts):
        source = turned_ref if k % 2 == 0 else other_ref
        value = source[k // 2 * rows : (k // 2 + 1) * rows].astype(f32)
        value = value + stacked[k][:, None, :dim] * both_k
        mirror[k] = value.reshape(rows * wide, dim).astype(bf16)
    target = lax.broadcasted_iota(jnp.int32, (rows * wide, rows * wide), 0)
    origin = lax.broadcasted_iota(jnp.int32, (rows * wide, rows * wide), 1)
    swap = jnp.where(origin == (target % rows) * wide + target // rows, 1.0, 0.0).astype(bf16)
    for b in range(parts):
        turned = jnp.dot(swap, mirror[b ^ me], preferred_element_type=f32)
        flipped[:, b * rows : (b + 1) * rows, :] = turned.reshape(wide, rows, dim)
    every = jnp.concatenate([stacked[b ^ me] for b in range(parts)], axis=0)[:, dim:]
    for i in range(rows):
        at = pl.ds(i * columns, columns)
        value = input_ref[i].astype(f32) + own[i : i + 1, :dim] * every
        summed[at, :] = value.astype(bf16)
    facing = flipped[pl.ds(core * rows, rows)].reshape(rows * columns, dim).astype(bf16)
    update = jnp.dot(facing, flip_ref[...], preferred_element_type=f32)
    update = update + summed[...].astype(f32)
    out_ref[...] = update.astype(bf16).reshape(rows, columns, dim)
    cotangent[pl.ds(core * rows, rows)] = cotangent_ref[...]
    cotangent[pl.ds((1 - core) * rows, rows)] = other_cotangent_ref[...]
    grad = lax.dot_general(
        flipped[...].reshape(wide * columns, dim).astype(bf16),
        cotangent[...].reshape(wide * columns, dim),
        (((0,), (0,)), ((), ())),
        preferred_element_type=f32,
    )
    grad_ref[...] = grad.astype(bf16)


def pair_update(pair_input, cotangents, flip_weight, turned, bundles, columns_used):
    rows, columns, dim = pair_input.shape
    chips = len(bundles)
    return pl.pallas_call(
        functools.partial(pair_kernel, chips, columns_used),
        name="pair",
        out_shape=[array((rows, columns, dim), bf16), array((dim, dim), bf16)],
        in_specs=[whole_vmem()] * (6 + chips),
        out_specs=[whole_vmem()] * 2,
        scratch_shapes=[
            pltpu.VMEM((2 * chips, rows, 2 * dim), f32),
            pltpu.VMEM((2 * chips, 2 * rows * rows, dim), bf16),
            pltpu.VMEM((rows * columns, dim), bf16),
            pltpu.VMEM((2 * rows, columns, dim), f32),
            pltpu.VMEM((2 * rows, columns, dim), bf16),
        ],
        compiler_params=pltpu.CompilerParams(
            vmem_limit_bytes=6 * MIB if chips <= 4 else 32 * MIB
        ),
    )(pair_input, *cotangents, flip_weight, *turned, *bundles[::-1])


def per_device(
    features,
    conv_weight,
    norm_gain,
    query_weight,
    keyval_weight,
    head_scale,
    output_weight,
    pair_weight,
    pair_input,
    flip_weight,
    pair_cotangent,
):
    chips = lax.axis_size("seq")
    bits = chips.bit_length() - 1
    windows = lax.axis_size("dp")
    taps = conv_weight.shape[0]
    model_dim = output_weight.shape[1]
    heads = head_scale.shape[0]
    features = features[0]

    masks = [(k, flipped_bits(k, bits)) for k in range(chips)]

    def send(value, mask, flip=0):
        cores = mask if isinstance(mask, tuple) else (mask, mask)
        return lax.ppermute(value, GROUP, hop_pairs(chips, cores, flip))

    strip = send(edge_strip(features, taps // 2), 0, 1)
    own_weight = conv_weight.reshape(-1, model_dim)
    own_weight, strip = lax.optimization_barrier((own_weight, strip))
    peer_weight = send(own_weight, 0, 1)

    blocks = add_edges(prep(features, pair_input[0], chips), strip, features.shape[0])
    messages = [blocks[0]] + [None] * (chips - 1)
    for k in range(chips - 1, 0, -1):
        messages[k] = send(blocks[k], k)
    weight = pack_filter(own_weight, peer_weight, taps, blocks[0].shape[1])
    cotangent, weight = lax.optimization_barrier((pair_cotangent[0], weight))
    cotangents = (pair_cotangent[0], send(cotangent, 0, 1))

    last = chips - 1
    rest = sorted(range(last), key=lambda k: (1 - (k & 1), -k))

    def partials(ks, columns, after):
        dtypes = [bf16 if k & 1 else f32 for k in ks]
        return dict(zip(ks, conv(messages, features, weight, taps, ks, dtypes, columns, after)))

    partial = partials([last], (0, model_dim // 2), [])
    partial[last] += partials([last], (model_dim // 2, model_dim), [cotangents[1]])[last]
    pairs, _, pair_dim = pair_input.shape[1:]
    turned = unpack_pairs(
        messages, pairs, pair_dim, features.shape[0] + strip.shape[0], partial[last]
    )
    turned = (turned, send(turned, 0, 1))
    for ks in ([k for k in rest if k & 1], [k for k in rest if k and not k & 1], [0]):
        partial.update(partials(ks, (0, model_dim), []))
    arrived = []
    for b in range(bits):
        bit = 1 << b
        leaving = [k for k in [last] + rest if k in partial and k & bit]
        got = {k ^ bit: [send(v, masks[bit]) for v in partial.pop(k)] for k in leaving}
        for k, values in got.items():
            if k == 0:
                arrived.append(values)
            else:
                dtype = bf16 if k & (2 * bit) else f32
                partial[k] = [
                    add_up([p, v], dtype, [turned[1]]) for p, v in zip(partial[k], values)
                ]

    encoded, feats = encode(partial[0], arrived, pair_weight, [])
    own_bundle = bundle(encoded, norm_gain, keyval_weight.T, feats, send(feats, 0, 1))
    bundles = [own_bundle] + [send(own_bundle, k) for k in range(chips - 1, 0, -1)][::-1]
    pair_out, grad = pair_update(
        pair_input[0], cotangents, flip_weight, turned, bundles, keyval_weight.shape[1]
    )
    keyvals = bundles + [send(v, 0, 1) for v in bundles]

    def attend_heads(start, first, end, dtype, after):
        return attend(
            encoded,
            norm_gain,
            query_weight,
            head_scale,
            start,
            output_weight,
            keyvals,
            first,
            end,
            dtype,
            after,
        )

    halfway = heads // 2
    first_half, done = attend_heads(encoded, 0, halfway, f32, [])
    grad = add_up([grad] + [send(grad, k) for k in range(1, chips)], bf16, [done])
    block_out, done = attend_heads(first_half, halfway, heads, bf16, [grad])
    grad = add_up(
        [grad]
        + [
            lax.ppermute(grad, "dp", [(w, w ^ k) for w in range(windows)])
            for k in range(1, windows)
        ],
        f32,
        [done],
    )
    return (block_out[None], pair_out[None], grad)


def solution(mesh):
    placed = (
        P("dp", ("seq", "mp"), None),
        P(None, ("seq", "mp"), None),
        P(),
        P(),
        P(),
        P(),
        P(),
        P(),
        P("dp", ("seq", "mp"), None, None),
        P(),
        P("dp", ("seq", "mp"), None, None),
    )
    return jax.shard_map(
        per_device,
        mesh=mesh,
        in_specs=placed,
        out_specs=(P("dp", ("seq", "mp"), None), P("dp", ("seq", "mp"), None, None), P()),
        check_vma=False,
    )
```

```python
import functools
import math

import jax
import jax.numpy as jnp
from jax import lax
from jax.experimental import pallas as pl
from jax.experimental.pallas import tpu as pltpu
from jax.sharding import PartitionSpec as P

PAIR_POOL = 16
SPARE_ROWS = 32
norm_eps = 1e-06
logit_cap = 50.0
MIB = 1 << 20
GROUP = ("seq", "mp")
f32, bf16 = jnp.float32, jnp.bfloat16


def whole_vmem():
    return pl.BlockSpec(memory_space=pltpu.VMEM)


def anywhere():
    return pl.BlockSpec(memory_space=pl.ANY)


def smem():
    return pl.BlockSpec(memory_space=pltpu.SMEM)


def in_hbm(value):
    return pltpu.with_memory_space_constraint(value, pltpu.HBM)


def array(shape, dtype):
    return jax.ShapeDtypeStruct(shape, dtype)


def lane_pad(width):
    return (width + 127) // 128 * 128


def tree_sum(terms):
    while len(terms) > 1:
        terms = [terms[i] + terms[i + 1] for i in range(0, len(terms), 2)]
    return terms[0]


def flipped_bits(mask, bits):
    return sum(((mask >> b) & 1) << (bits - 1 - b) for b in range(bits))


def here():
    return lax.axis_index("seq"), lax.axis_index("mp")


def hop_pairs(chips, core_masks, core_flip):
    pairs = []
    for chip in range(chips):
        for core in range(2):
            target = (chip ^ core_masks[core]) * 2 + (core ^ core_flip)
            pairs.append((chip * 2 + core, target))
    return pairs


def pick_rows(rows):
    half = rows // 2
    target = lax.broadcasted_iota(jnp.int32, (rows, rows), 0)
    source = lax.broadcasted_iota(jnp.int32, (rows, rows), 1)
    wanted = jnp.where(target < half, 2 * target, 2 * (target - half) + 1)
    return jnp.where(source == wanted, 1.0, 0.0).astype(bf16)


def prep_kernel(chips, width, feat_hbm, pair_hbm, *rest):
    block_refs = rest[:chips]
    feat, pair, split, sems = rest[chips:]
    rows = feat.shape[0]
    chip, _ = here()
    copy = pltpu.make_async_copy(feat_hbm, feat, sems.at[0])
    pair_copy = pltpu.make_async_copy(pair_hbm, pair, sems.at[1])
    copy.start()
    pair_copy.start()
    copy.wait()
    x = feat[...].astype(f32)
    scale = lax.rsqrt(jnp.mean(x * x, axis=-1, keepdims=True) + norm_eps)
    high = scale.astype(bf16)
    middle = (scale - high.astype(f32)).astype(bf16)
    low = (scale - high.astype(f32) - middle.astype(f32)).astype(bf16)
    lane = lax.broadcasted_iota(jnp.int32, (rows, split.shape[2] - width), 1)
    tail = jnp.where(
        lane == 0,
        high.astype(f32),
        jnp.where(
            lane == 1, middle.astype(f32), jnp.where(lane == 2, low.astype(f32), 0.0)
        ),
    ).astype(bf16)
    for q in range(chips):
        split[q, :, 0:width] = feat[:, q * width : (q + 1) * width]
        split[q, :, width:] = tail
    pair_copy.wait()
    pairs, _, dim = pair.shape
    lanes = split.shape[2] // dim
    extra = block_refs[0].shape[0] - rows
    spare = dim * SPARE_ROWS // rows
    for k in range(chips):
        at = pl.ds(pl.multiple_of((chip ^ k) * 2 * pairs, 16), 2 * pairs)
        piece = pair[:, at, :].reshape(2 * pairs * pairs, dim)
        block_refs[k][0:rows, :] = split[chip ^ k]
        for g in range(dim // spare):
            block_refs[k][
                g * SPARE_ROWS : (g + 1) * SPARE_ROWS, width + 8 : width + 8 + spare
            ] = piece[:SPARE_ROWS, g * spare : (g + 1) * spare]
        for g in range(lanes):
            part = piece[SPARE_ROWS + g * extra : SPARE_ROWS + (g + 1) * extra]
            block_refs[k][rows : rows + part.shape[0], g * dim : (g + 1) * dim] = part


def prep(features, pair_input, chips):
    rows, channels = features.shape
    width = channels // chips
    padded = lane_pad(width)
    pairs, _, dim = pair_input.shape
    extra = -(-(2 * pairs * pairs - SPARE_ROWS) // (16 * (padded // dim))) * 16
    return pl.pallas_call(
        functools.partial(prep_kernel, chips, width),
        name="prep",
        out_shape=[array((rows + extra, padded), bf16)] * chips,
        in_specs=[anywhere()] * 2,
        out_specs=[whole_vmem()] * chips,
        scratch_shapes=[
            pltpu.VMEM((rows, channels), bf16),
            pltpu.VMEM(pair_input.shape, bf16),
            pltpu.VMEM((chips, rows, padded), bf16),
            pltpu.SemaphoreType.DMA((2,)),
        ],
        compiler_params=pltpu.CompilerParams(vmem_limit_bytes=10 * MIB),
    )(in_hbm(features), in_hbm(pair_input))


def gelu_of(block, width):
    scale = block[:, width : width + 1] + block[:, width + 1 : width + 2]
    scale = scale + block[:, width + 2 : width + 3]
    v = block * scale
    g = (0.5 * v) * (1.0 + lax.erf(v * math.sqrt(0.5)))
    lane = lax.broadcasted_iota(jnp.int32, block.shape, 1)
    return jnp.where(lane < width, g, 0.0)


def edges_kernel(chips, width, rows, *refs):
    message_refs = refs[:chips][::-1]
    out_ref = refs[-1]
    strips = []
    for ref in message_refs:
        for start, row in ((0, 0), (0, 1), (rows - 16, 14), (rows - 16, 15)):
            strips.append(ref[start : start + 16, :].astype(f32)[row : row + 1])
    prepared = gelu_of(jnp.concatenate(strips, axis=0), width)
    for k in range(chips):
        out_ref[k, 0:4] = prepared[4 * k : 4 * k + 4]
        out_ref[k, 4:8] = jnp.zeros((4, prepared.shape[1]), f32)


def edge_rows(messages, width, rows, after):
    chips = len(messages)
    padded = messages[0].shape[1]
    return pl.pallas_call(
        functools.partial(edges_kernel, chips, width, rows),
        name="edge_rows",
        out_shape=array((chips, 8, padded), f32),
        in_specs=[whole_vmem()] * chips + [anywhere()] * len(after),
        out_specs=whole_vmem(),
        compiler_params=pltpu.CompilerParams(vmem_limit_bytes=2 * MIB),
    )(*messages[::-1], *after)


def activate_kernel(width, count, *refs):
    message_refs, out_ref, wide = refs[:count], refs[-2], refs[-1]
    _, core = here()
    step = 32
    rows = out_ref.shape[0]
    pick = pick_rows(rows)
    if count == 1:
        wide[...] = jnp.dot(pick, message_refs[0][0:rows, :], preferred_element_type=f32)
    else:

        @pl.when(core == 0)
        def _():
            wide[...] = jnp.dot(pick, message_refs[0][0:rows, :], preferred_element_type=f32)

        @pl.when(core != 0)
        def _():
            wide[...] = jnp.dot(pick, message_refs[1][0:rows, :], preferred_element_type=f32)

    def body(i, carry):
        at = pl.ds(pl.multiple_of(i * step, step), step)
        out_ref[at, :] = gelu_of(wide[at, :], width).astype(bf16)
        return carry

    lax.fori_loop(0, out_ref.shape[0] // step, body, 0)


def activate(messages, width, rows, after):
    return pl.pallas_call(
        functools.partial(activate_kernel, width, len(messages)),
        name="activate",
        out_shape=array((rows, messages[0].shape[1]), bf16),
        in_specs=[whole_vmem()] * len(messages) + [anywhere()] * len(after),
        out_specs=whole_vmem(),
        scratch_shapes=[pltpu.VMEM((rows, messages[0].shape[1]), f32)],
        compiler_params=pltpu.CompilerParams(vmem_limit_bytes=3 * MIB),
    )(*messages, *after)


def pack_kernel(taps, padded, own_hbm, peer_hbm, out_ref, sems):
    part = own_hbm.shape[0] // taps
    _, core = here()
    copies = []
    for p, source in enumerate((own_hbm, peer_hbm)):
        place = core if p == 0 else 1 - core
        for k in range(taps):
            to = pl.ds(pl.multiple_of(k * padded + place * part, 16), part)
            copies.append(
                pltpu.make_async_copy(
                    source.at[k * part : (k + 1) * part, :], out_ref.at[to, :], sems.at[p, k]
                )
            )
    for c in copies:
        c.start()
    if padded > 2 * part:
        for k in range(taps):
            out_ref[k * padded + 2 * part : (k + 1) * padded, :] = jnp.zeros(
                (padded - 2 * part, out_ref.shape[1]), bf16
            )
    for c in copies:
        c.wait()


def pack_filter(own, peer, taps, padded):
    model_dim = own.shape[1]
    part = own.shape[0] // taps
    if part % 16:
        own, peer = (w.reshape(taps, part, model_dim) for w in (own, peer))
        first = lax.axis_index("mp") == 0
        low, high = jnp.where(first, own, peer), jnp.where(first, peer, own)
        both = jnp.concatenate([low, high], axis=1)
        both = jnp.pad(both, ((0, 0), (0, padded - 2 * part), (0, 0)))
        return both.reshape(taps * padded, model_dim)
    return pl.pallas_call(
        functools.partial(pack_kernel, taps, padded),
        name="pack_filter",
        out_shape=array((taps * padded, model_dim), bf16),
        in_specs=[anywhere()] * 2,
        out_specs=whole_vmem(),
        scratch_shapes=[pltpu.SemaphoreType.DMA((2, taps))],
        compiler_params=pltpu.CompilerParams(vmem_limit_bytes=2 * MIB),
    )(in_hbm(own), peer)


def conv_kernel(chips, bits, taps, tile, wanted, first, outs, feat_hbm, edge_ref, *rest):
    count = len(wanted)
    block_refs = rest[:count]
    weight_ref = rest[count]
    cols, feat, sem = rest[-3:]
    out_refs = rest[-3 - outs : -3]
    rows, padded = block_refs[0].shape
    half = rows // 2
    chip, core = here()
    if 0 in wanted:
        copy = pltpu.make_async_copy(feat_hbm, feat, sem)
        copy.start()
    row = lax.broadcasted_iota(jnp.int32, (half, padded), 0)
    for j, k in enumerate(wanted):
        mask = jnp.where(core == 0, k, flipped_bits(k, bits))
        left = (chip ^ mask) - (1 - core)
        right = (chip ^ mask) + core
        block = block_refs[j][...]
        before = edge_ref[jnp.where(left >= 0, left ^ chip, 0)]
        before = jnp.where(left >= 0, before, 0.0)
        after = edge_ref[jnp.where(right < chips, right ^ chip, 0)]
        after = jnp.where(right < chips, after, 0.0)
        even = block[0:half].astype(f32)
        odd = block[half:rows].astype(f32)

        def back(v, strip_row):
            return jnp.where(row == 0, before[strip_row : strip_row + 1], pltpu.roll(v, 1, 0))

        def ahead(v, strip_row):
            return jnp.where(
                row == half - 1, after[strip_row : strip_row + 1], pltpu.roll(v, half - 1, 0)
            )

        lagged = [back(even, 2), back(odd, 3), even, odd, ahead(even, 0), ahead(odd, 1)]
        for i, v in enumerate(lagged):
            piece = v.astype(bf16)
            if i < taps:
                cols[j * rows : j * rows + half, i * padded : (i + 1) * padded] = piece
            if i > 0:
                cols[j * rows + half : (j + 1) * rows, (i - 1) * padded : i * padded] = piece
    pick = pick_rows(rows)
    if 0 in wanted:
        copy.wait()
    halves = len(out_refs) // count
    span = out_refs[0].shape[1]
    for j, k in enumerate(wanted):
        for h in range(halves):
            for n in range(0, span, tile):
                at = first + h * span + n
                got = jnp.dot(
                    cols[j * rows : (j + 1) * rows],
                    weight_ref[:, at : at + tile],
                    preferred_element_type=f32,
                )
                if k == 0 and at < feat.shape[1]:
                    width = min(tile, feat.shape[1] - at)
                    skip = jnp.dot(
                        pick, feat[:, at : at + width], preferred_element_type=f32
                    )
                    if width < tile:
                        skip = jnp.concatenate(
                            [skip, jnp.zeros((rows, tile - width), f32)], axis=1
                        )
                    got = got + skip
                out_refs[j * halves + h][:, n : n + tile] = got.astype(out_refs[j * halves].dtype)


def conv(blocks, edges, features, weight, taps, wanted, dtypes, columns, after):
    chips = edges.shape[0]
    bits = chips.bit_length() - 1
    rows = features.shape[0]
    depth, model_dim = weight.shape
    count = len(wanted)
    first, last = columns
    span = model_dim // 2
    halves = (last - first) // span
    got = pl.pallas_call(
        functools.partial(
            conv_kernel, chips, bits, taps, 256, wanted, first, count * halves
        ),
        name="conv",
        out_shape=[array((rows, span), d) for d in dtypes for _ in range(halves)],
        in_specs=[anywhere()] + [whole_vmem()] * (count + 2) + [anywhere()] * len(after),
        out_specs=[whole_vmem()] * (count * halves),
        scratch_shapes=[
            pltpu.VMEM((count * rows, depth), bf16),
            pltpu.VMEM(features.shape, bf16),
            pltpu.SemaphoreType.DMA,
        ],
        compiler_params=pltpu.CompilerParams(vmem_limit_bytes=(5 + 2 * count) * MIB),
    )(in_hbm(features), edges, *blocks, weight, *after)
    return [got[j * halves : (j + 1) * halves] for j in range(count)]


def sum_kernel(count, *refs):
    out_ref = refs[-1]
    out_ref[...] = tree_sum([r[...].astype(f32) for r in refs[:count][::-1]]).astype(out_ref.dtype)


def add_up(terms, dtype, after=()):
    return pl.pallas_call(
        functools.partial(sum_kernel, len(terms)),
        name="add_up",
        out_shape=array(terms[0].shape, dtype),
        in_specs=[whole_vmem()] * len(terms) + [anywhere()] * len(after),
        out_specs=whole_vmem(),
        compiler_params=pltpu.CompilerParams(vmem_limit_bytes=4 * MIB),
    )(*terms[::-1], *after)


def encode_kernel(pieces, arrivals, pair_weight_ref, *rest):
    own_refs = rest[:pieces]
    come_refs = rest[pieces : pieces + arrivals * pieces]
    encoded_ref, feats_ref = rest[-2:]
    rows, span = own_refs[0].shape
    half = rows // 2
    pairs = half // PAIR_POOL
    at = lax.broadcasted_iota(jnp.int32, (pairs, half), 0)
    of = lax.broadcasted_iota(jnp.int32, (pairs, half), 1) // PAIR_POOL
    spread = jnp.where(at == of, 1.0 / PAIR_POOL, 0.0).astype(bf16)
    feats = jnp.zeros(feats_ref.shape, f32)
    for h in range(pieces):
        total = own_refs[h][...]
        for a in range(arrivals):
            total = total + come_refs[a * pieces + h][...].astype(f32)
        encoded = jnp.maximum(total[:half], total[half:]).astype(bf16)
        encoded_ref[:, h * span : (h + 1) * span] = encoded
        pooled = jnp.dot(spread, encoded, preferred_element_type=f32).astype(bf16)
        feats = feats + jnp.dot(
            pooled, pair_weight_ref[h * span : (h + 1) * span, :], preferred_element_type=f32
        )
    feats_ref[...] = feats.astype(bf16).astype(f32)


def encode(own, come, pair_weight, after):
    rows, span = own[0].shape
    pieces = len(own)
    half = rows // 2
    return pl.pallas_call(
        functools.partial(encode_kernel, pieces, len(come)),
        name="encode",
        out_shape=[
            array((half, span * pieces), bf16),
            array((half // PAIR_POOL, pair_weight.shape[1]), f32),
        ],
        in_specs=[whole_vmem()] * (1 + pieces * (1 + len(come))) + [anywhere()] * len(after),
        out_specs=[whole_vmem()] * 2,
        compiler_params=pltpu.CompilerParams(vmem_limit_bytes=8 * MIB),
    )(pair_weight, *own, *sum(come, []), *after)


def normalised(encoded_ref, gain_ref):
    wide = encoded_ref[...].astype(f32)
    scale = lax.rsqrt(jnp.mean(wide * wide, axis=-1, keepdims=True) + norm_eps)
    return (wide * scale * gain_ref[...][None]).astype(bf16)


def bundle_kernel(encoded_ref, gain_ref, weight_ref, mine_ref, other_ref, out_ref):
    keyval = lax.dot_general(
        normalised(encoded_ref, gain_ref),
        weight_ref[...],
        (((1,), (1,)), ((), ())),
        preferred_element_type=f32,
    )
    rows, columns = keyval.shape
    spare = out_ref.shape[1] - columns
    pieces = []
    for ref in (mine_ref, other_ref):
        feats = ref[...]
        pieces += [feats[:, g : g + spare] for g in range(0, feats.shape[1], spare)]
    used = sum(p.shape[0] for p in pieces)
    pieces.append(jnp.zeros((rows - used, spare), f32))
    out_ref[...] = jnp.concatenate(
        [keyval, jnp.concatenate(pieces, axis=0)], axis=1
    ).astype(bf16)


def bundle(encoded, gain, weight_t, mine, other):
    return pl.pallas_call(
        bundle_kernel,
        name="bundle",
        out_shape=array((encoded.shape[0], lane_pad(weight_t.shape[0])), bf16),
        in_specs=[whole_vmem()] * 5,
        out_specs=whole_vmem(),
        compiler_params=pltpu.CompilerParams(vmem_limit_bytes=4 * MIB),
    )(encoded, gain, weight_t, mine, other)


def attend_kernel(
    parts,
    heads,
    first,
    last,
    group,
    scale_ref,
    encoded_ref,
    gain_ref,
    query_weight_ref,
    start_ref,
    weight_ref,
    *rest,
):
    part_refs = rest[:parts]
    out_ref, done_ref, keys, values = rest[-4:]
    rows = encoded_ref.shape[0]
    key_dim = query_weight_ref.shape[1] // heads
    normed = normalised(encoded_ref, gain_ref)
    span = part_refs[0].shape[0]
    value_dim = values.shape[1]
    for k in range(parts):
        got = part_refs[k][...]
        keys[k * span : (k + 1) * span, :] = got[:, :key_dim]
        values[k * span : (k + 1) * span, :] = got[:, key_dim : key_dim + value_dim]
    total = start_ref[...].astype(f32)
    for n in range(first, last, group):
        got = jnp.dot(
            normed,
            query_weight_ref[:, n * key_dim : (n + group) * key_dim],
            preferred_element_type=f32,
        )
        queries = jnp.concatenate(
            [
                got[:, h * key_dim : (h + 1) * key_dim]
                * (scale_ref[n + h] / math.sqrt(key_dim))
                for h in range(group)
            ],
            axis=0,
        ).astype(bf16)
        scores = lax.dot_general(
            queries, keys[...], (((1,), (1,)), ((), ())), preferred_element_type=f32
        )
        weights = jnp.exp(logit_cap * jnp.tanh(scores * (1.0 / logit_cap)))
        sums = jnp.sum(weights, axis=-1, keepdims=True)
        mixed = jnp.dot(weights.astype(bf16), values[...], preferred_element_type=f32) / sums
        mixed = mixed.astype(bf16)
        for h in range(group):
            at = (n + h) * value_dim
            total = total + jnp.dot(
                mixed[h * rows : (h + 1) * rows],
                weight_ref[at : at + value_dim, :],
                preferred_element_type=f32,
            )
    out_ref[...] = total.astype(out_ref.dtype)
    done_ref[...] = total[0:8, 0:128]


def attend(
    encoded, gain, query_weight, scale, start, output_weight, parts, first, last, dtype, after
):
    rows, model_dim = start.shape
    heads = scale.shape[0]
    key_dim = query_weight.shape[1] // heads
    value_dim = output_weight.shape[0] // heads
    total_keys = parts[0].shape[0] * len(parts)
    group = 2
    return pl.pallas_call(
        functools.partial(attend_kernel, len(parts), heads, first, last, group),
        name="attend",
        out_shape=[array((rows, model_dim), dtype), array((8, 128), f32)],
        in_specs=[smem()] + [whole_vmem()] * (5 + len(parts)) + [anywhere()] * len(after),
        out_specs=[whole_vmem()] * 2,
        scratch_shapes=[
            pltpu.VMEM((total_keys, key_dim), bf16),
            pltpu.VMEM((total_keys, value_dim), bf16),
        ],
        compiler_params=pltpu.CompilerParams(
            vmem_limit_bytes=8 * MIB if total_keys <= 1024 else 32 * MIB
        ),
    )(scale, encoded, gain, query_weight, start, output_weight, *parts, *after)


def unpack_kernel(chips, pairs, rows, width, *refs):
    message_refs = refs[:chips][::-1]
    out_ref = refs[-1]
    dim = out_ref.shape[2]
    padded = message_refs[0].shape[1]
    for k in range(chips):
        spare = dim * SPARE_ROWS // rows
        first = jnp.concatenate(
            [
                message_refs[k][
                    g * SPARE_ROWS : (g + 1) * SPARE_ROWS, width + 8 : width + 8 + spare
                ]
                for g in range(dim // spare)
            ],
            axis=1,
        )
        piece = message_refs[k][rows:, :]
        piece = [piece[:, g : g + dim] for g in range(0, padded, dim)]
        piece = jnp.concatenate([first] + piece, axis=0)
        piece = piece[: 2 * pairs * pairs].reshape(pairs, 2 * pairs, dim)
        out_ref[k * pairs : (k + 1) * pairs] = piece


def unpack_pairs(messages, pairs, dim, rows, width, after):
    chips = len(messages)
    return pl.pallas_call(
        functools.partial(unpack_kernel, chips, pairs, rows, width),
        name="unpack_pairs",
        out_shape=array((chips * pairs, 2 * pairs, dim), bf16),
        in_specs=[whole_vmem()] * chips + [anywhere()] * len(after),
        out_specs=whole_vmem(),
        compiler_params=pltpu.CompilerParams(vmem_limit_bytes=4 * MIB),
    )(*messages[::-1], *after)


def pair_kernel(
    chips, columns_used, input_ref, cotangent_ref, other_cotangent_ref, flip_ref, turned_ref, other_ref, *rest
):
    bundle_refs = rest[:chips][::-1]
    out_ref, grad_ref, stacked, mirror, summed, flipped, cotangent = rest[-7:]
    rows, columns, dim = input_ref.shape
    parts = 2 * chips
    wide = 2 * rows
    chip, core = here()
    me = chip * 2 + core
    for k in range(chips):
        got = bundle_refs[k][:, columns_used:].astype(f32)
        count = 2 * dim // got.shape[1]
        for f in range(2):
            at = f * count * rows
            stacked[2 * k + f] = jnp.concatenate(
                [got[at + g * rows : at + (g + 1) * rows] for g in range(count)], axis=1
            )
    own, other = stacked[0], stacked[1]
    both_k = jnp.concatenate(
        [jnp.where(core == 0, own, other), jnp.where(core == 0, other, own)], axis=0
    )[:, dim:][None]
    for k in range(parts):
        source = turned_ref if k % 2 == 0 else other_ref
        value = source[k // 2 * rows : (k // 2 + 1) * rows].astype(f32)
        value = value + stacked[k][:, None, :dim] * both_k
        mirror[k] = value.reshape(rows * wide, dim).astype(bf16)
    target = lax.broadcasted_iota(jnp.int32, (rows * wide, rows * wide), 0)
    origin = lax.broadcasted_iota(jnp.int32, (rows * wide, rows * wide), 1)
    swap = jnp.where(origin == (target % rows) * wide + target // rows, 1.0, 0.0).astype(bf16)
    for b in range(parts):
        turned = jnp.dot(swap, mirror[b ^ me], preferred_element_type=f32)
        flipped[:, b * rows : (b + 1) * rows, :] = turned.reshape(wide, rows, dim)
    every = jnp.concatenate([stacked[b ^ me] for b in range(parts)], axis=0)[:, dim:]
    for i in range(rows):
        at = pl.ds(i * columns, columns)
        value = input_ref[i].astype(f32) + own[i : i + 1, :dim] * every
        summed[at, :] = value.astype(bf16)
    facing = flipped[pl.ds(core * rows, rows)].reshape(rows * columns, dim).astype(bf16)
    update = jnp.dot(facing, flip_ref[...], preferred_element_type=f32)
    update = update + summed[...].astype(f32)
    out_ref[...] = update.astype(bf16).reshape(rows, columns, dim)
    cotangent[pl.ds(core * rows, rows)] = cotangent_ref[...]
    cotangent[pl.ds((1 - core) * rows, rows)] = other_cotangent_ref[...]
    grad = lax.dot_general(
        flipped[...].reshape(wide * columns, dim).astype(bf16),
        cotangent[...].reshape(wide * columns, dim),
        (((0,), (0,)), ((), ())),
        preferred_element_type=f32,
    )
    grad_ref[...] = grad.astype(bf16)


def pair_update(pair_input, cotangents, flip_weight, turned, bundles, columns_used):
    rows, columns, dim = pair_input.shape
    chips = len(bundles)
    return pl.pallas_call(
        functools.partial(pair_kernel, chips, columns_used),
        name="pair",
        out_shape=[array((rows, columns, dim), bf16), array((dim, dim), bf16)],
        in_specs=[whole_vmem()] * (6 + chips),
        out_specs=[whole_vmem()] * 2,
        scratch_shapes=[
            pltpu.VMEM((2 * chips, rows, 2 * dim), f32),
            pltpu.VMEM((2 * chips, 2 * rows * rows, dim), bf16),
            pltpu.VMEM((rows * columns, dim), bf16),
            pltpu.VMEM((2 * rows, columns, dim), f32),
            pltpu.VMEM((2 * rows, columns, dim), bf16),
        ],
        compiler_params=pltpu.CompilerParams(
            vmem_limit_bytes=6 * MIB if chips <= 4 else 32 * MIB
        ),
    )(pair_input, *cotangents, flip_weight, *turned, *bundles[::-1])


def per_device(
    features,
    conv_weight,
    norm_gain,
    query_weight,
    keyval_weight,
    head_scale,
    output_weight,
    pair_weight,
    pair_input,
    flip_weight,
    pair_cotangent,
):
    chips = lax.axis_size("seq")
    bits = chips.bit_length() - 1
    windows = lax.axis_size("dp")
    taps = conv_weight.shape[0]
    model_dim = output_weight.shape[1]
    heads = head_scale.shape[0]
    features = features[0]

    masks = [(k, flipped_bits(k, bits)) for k in range(chips)]

    def send(value, mask, flip=0):
        cores = mask if isinstance(mask, tuple) else (mask, mask)
        return lax.ppermute(value, GROUP, hop_pairs(chips, cores, flip))

    own_weight = conv_weight.reshape(-1, model_dim)
    peer_weight = send(own_weight, 0, 1)

    rows, channels = features.shape
    width = channels // chips
    blocks = prep(features, pair_input[0], chips)
    messages = [blocks[0]] + [None] * (chips - 1)
    for k in range(chips - 1, 0, -1):
        messages[k] = send(blocks[k], k)
    weight = pack_filter(own_weight, peer_weight, taps, blocks[0].shape[1])
    cotangent, weight = lax.optimization_barrier((pair_cotangent[0], weight))
    cotangents = (pair_cotangent[0], send(cotangent, 0, 1))

    last = chips - 1
    rest = sorted(range(last), key=lambda k: (1 - (k & 1), -k))

    prepared = {}

    def active(k):
        if k not in prepared:
            sources = [messages[j] for j in dict.fromkeys(masks[k])]
            after = [] if k == last else partial[last]
            prepared[k] = activate(sources, width, rows, after)
        return prepared[k]

    edges = send(edge_rows(messages, width, rows, [active(last)]), 0, 1)

    def partials(ks, columns, after):
        dtypes = [bf16 if k & 1 else f32 for k in ks]
        got = conv(
            [active(k) for k in ks], edges, features, weight, taps, ks, dtypes, columns, after
        )
        return dict(zip(ks, got))

    partial = partials([last], (0, model_dim // 2), [])
    partial[last] += partials([last], (model_dim // 2, model_dim), [cotangents[1]])[last]
    pairs, _, pair_dim = pair_input.shape[1:]
    turned = unpack_pairs(
        messages, pairs, pair_dim, rows, width, partial[last]
    )
    turned = (turned, send(turned, 0, 1))
    for ks in ([k for k in rest if k & 1], [k for k in rest if k and not k & 1], [0]):
        partial.update(partials(ks, (0, model_dim), []))
    arrived = []
    for b in range(bits):
        bit = 1 << b
        leaving = [k for k in [last] + rest if k in partial and k & bit]
        got = {k ^ bit: [send(v, masks[bit]) for v in partial.pop(k)] for k in leaving}
        for k, values in got.items():
            if k == 0:
                arrived.append(values)
            else:
                dtype = bf16 if k & (2 * bit) else f32
                partial[k] = [
                    add_up([p, v], dtype, [turned[1]]) for p, v in zip(partial[k], values)
                ]

    encoded, feats = encode(partial[0], arrived, pair_weight, [])
    own_bundle = bundle(encoded, norm_gain, keyval_weight.T, feats, send(feats, 0, 1))
    bundles = [own_bundle] + [send(own_bundle, k) for k in range(chips - 1, 0, -1)][::-1]
    pair_out, grad = pair_update(
        pair_input[0], cotangents, flip_weight, turned, bundles, keyval_weight.shape[1]
    )
    keyvals = bundles + [send(v, 0, 1) for v in bundles]

    def attend_heads(start, first, end, dtype, after):
        return attend(
            encoded,
            norm_gain,
            query_weight,
            head_scale,
            start,
            output_weight,
            keyvals,
            first,
            end,
            dtype,
            after,
        )

    halfway = heads // 2
    first_half, done = attend_heads(encoded, 0, halfway, f32, [])
    grad = add_up([grad] + [send(grad, k) for k in range(1, chips)], bf16, [done])
    block_out, done = attend_heads(first_half, halfway, heads, bf16, [grad])
    grad = add_up(
        [grad]
        + [
            lax.ppermute(grad, "dp", [(w, w ^ k) for w in range(windows)])
            for k in range(1, windows)
        ],
        f32,
        [done],
    )
    return (block_out[None], pair_out[None], grad)


def solution(mesh):
    placed = (
        P("dp", ("seq", "mp"), None),
        P(None, ("seq", "mp"), None),
        P(),
        P(),
        P(),
        P(),
        P(),
        P(),
        P("dp", ("seq", "mp"), None, None),
        P(),
        P("dp", ("seq", "mp"), None, None),
    )
    return jax.shard_map(
        per_device,
        mesh=mesh,
        in_specs=placed,
        out_specs=(P("dp", ("seq", "mp"), None), P("dp", ("seq", "mp"), None, None), P()),
        check_vma=False,
    )
```

```python
import functools
import math

import jax
import jax.numpy as jnp
from jax import lax
from jax.experimental import pallas as pl
from jax.experimental.pallas import tpu as pltpu
from jax.sharding import PartitionSpec as P

PAIR_POOL = 16
SPARE_ROWS = 32
norm_eps = 1e-06
logit_cap = 50.0
MIB = 1 << 20
GROUP = ("seq", "mp")
f32, bf16 = jnp.float32, jnp.bfloat16


def whole_vmem():
    return pl.BlockSpec(memory_space=pltpu.VMEM)


def anywhere():
    return pl.BlockSpec(memory_space=pl.ANY)


def smem():
    return pl.BlockSpec(memory_space=pltpu.SMEM)


def in_hbm(value):
    return pltpu.with_memory_space_constraint(value, pltpu.HBM)


def array(shape, dtype):
    return jax.ShapeDtypeStruct(shape, dtype)


def lane_pad(width):
    return (width + 127) // 128 * 128


def tree_sum(terms):
    while len(terms) > 1:
        terms = [terms[i] + terms[i + 1] for i in range(0, len(terms), 2)]
    return terms[0]


def flipped_bits(mask, bits):
    return sum(((mask >> b) & 1) << (bits - 1 - b) for b in range(bits))


def here():
    return lax.axis_index("seq"), lax.axis_index("mp")


def hop_pairs(chips, core_masks, core_flip):
    pairs = []
    for chip in range(chips):
        for core in range(2):
            target = (chip ^ core_masks[core]) * 2 + (core ^ core_flip)
            pairs.append((chip * 2 + core, target))
    return pairs


def pick_rows(rows):
    half = rows // 2
    target = lax.broadcasted_iota(jnp.int32, (rows, rows), 0)
    source = lax.broadcasted_iota(jnp.int32, (rows, rows), 1)
    wanted = jnp.where(target < half, 2 * target, 2 * (target - half) + 1)
    return jnp.where(source == wanted, 1.0, 0.0).astype(bf16)


def prep_kernel(chips, width, feat_hbm, pair_hbm, *rest):
    block_refs = rest[:chips]
    feat, pair, split, sems = rest[chips:]
    rows = feat.shape[0]
    chip, _ = here()
    chunks = sems.shape[0] - 1
    step = rows // chunks

    def copy(n):
        at = pl.ds(n * step, step)
        return pltpu.make_async_copy(feat_hbm.at[at, :], feat.at[at, :], sems.at[n])

    pair_copy = pltpu.make_async_copy(pair_hbm, pair, sems.at[chunks])
    for n in range(chunks):
        copy(n).start()
    pair_copy.start()
    for n in range(chunks):
        copy(n).wait()
        fill_rows(chips, width, n * step, step, feat, split)
    pair_copy.wait()
    pairs, _, dim = pair.shape
    lanes = split.shape[2] // dim
    extra = block_refs[0].shape[0] - rows
    spare = dim * SPARE_ROWS // rows
    for k in range(chips):
        at = pl.ds(pl.multiple_of((chip ^ k) * 2 * pairs, 16), 2 * pairs)
        piece = pair[:, at, :].reshape(2 * pairs * pairs, dim)
        block_refs[k][0:rows, :] = split[chip ^ k]
        for g in range(dim // spare):
            block_refs[k][
                g * SPARE_ROWS : (g + 1) * SPARE_ROWS, width + 8 : width + 8 + spare
            ] = piece[:SPARE_ROWS, g * spare : (g + 1) * spare]
        for g in range(lanes):
            part = piece[SPARE_ROWS + g * extra : SPARE_ROWS + (g + 1) * extra]
            block_refs[k][rows : rows + part.shape[0], g * dim : (g + 1) * dim] = part


def fill_rows(chips, width, start, step, feat, split):
    at = slice(start, start + step)
    x = feat[at, :].astype(f32)
    scale = lax.rsqrt(jnp.mean(x * x, axis=-1, keepdims=True) + norm_eps)
    high = scale.astype(bf16)
    middle = (scale - high.astype(f32)).astype(bf16)
    low = (scale - high.astype(f32) - middle.astype(f32)).astype(bf16)
    lane = lax.broadcasted_iota(jnp.int32, (step, split.shape[2] - width), 1)
    tail = jnp.where(
        lane == 0,
        high.astype(f32),
        jnp.where(
            lane == 1, middle.astype(f32), jnp.where(lane == 2, low.astype(f32), 0.0)
        ),
    ).astype(bf16)
    for q in range(chips):
        split[q, at, 0:width] = feat[at, q * width : (q + 1) * width]
        split[q, at, width:] = tail


def prep(features, pair_input, chips):
    rows, channels = features.shape
    width = channels // chips
    padded = lane_pad(width)
    pairs, _, dim = pair_input.shape
    extra = -(-(2 * pairs * pairs - SPARE_ROWS) // (16 * (padded // dim))) * 16
    return pl.pallas_call(
        functools.partial(prep_kernel, chips, width),
        name="prep",
        out_shape=[array((rows + extra, padded), bf16)] * chips,
        in_specs=[anywhere()] * 2,
        out_specs=[whole_vmem()] * chips,
        scratch_shapes=[
            pltpu.VMEM((rows, channels), bf16),
            pltpu.VMEM(pair_input.shape, bf16),
            pltpu.VMEM((chips, rows, padded), bf16),
            pltpu.SemaphoreType.DMA((2,)),
        ],
        compiler_params=pltpu.CompilerParams(vmem_limit_bytes=10 * MIB),
    )(in_hbm(features), in_hbm(pair_input))


def gelu_of(block, width):
    scale = block[:, width : width + 1] + block[:, width + 1 : width + 2]
    scale = scale + block[:, width + 2 : width + 3]
    v = block * scale
    g = (0.5 * v) * (1.0 + lax.erf(v * math.sqrt(0.5)))
    lane = lax.broadcasted_iota(jnp.int32, block.shape, 1)
    return jnp.where(lane < width, g, 0.0)


def edges_kernel(chips, width, rows, *refs):
    message_refs = refs[:chips][::-1]
    out_ref = refs[-1]
    strips = []
    for ref in message_refs:
        for start, row in ((0, 0), (0, 1), (rows - 16, 14), (rows - 16, 15)):
            strips.append(ref[start : start + 16, :].astype(f32)[row : row + 1])
    prepared = gelu_of(jnp.concatenate(strips, axis=0), width)
    for k in range(chips):
        out_ref[k, 0:4] = prepared[4 * k : 4 * k + 4]
        out_ref[k, 4:8] = jnp.zeros((4, prepared.shape[1]), f32)


def edge_rows(messages, width, rows, after):
    chips = len(messages)
    padded = messages[0].shape[1]
    return pl.pallas_call(
        functools.partial(edges_kernel, chips, width, rows),
        name="edge_rows",
        out_shape=array((chips, 8, padded), f32),
        in_specs=[whole_vmem()] * chips + [anywhere()] * len(after),
        out_specs=whole_vmem(),
        compiler_params=pltpu.CompilerParams(vmem_limit_bytes=2 * MIB),
    )(*messages[::-1], *after)


def activate_kernel(width, count, *refs):
    message_refs, out_ref, wide = refs[:count], refs[-2], refs[-1]
    _, core = here()
    step = 32
    rows = out_ref.shape[0]
    pick = pick_rows(rows)
    if count == 1:
        wide[...] = jnp.dot(pick, message_refs[0][0:rows, :], preferred_element_type=f32)
    else:

        @pl.when(core == 0)
        def _():
            wide[...] = jnp.dot(pick, message_refs[0][0:rows, :], preferred_element_type=f32)

        @pl.when(core != 0)
        def _():
            wide[...] = jnp.dot(pick, message_refs[1][0:rows, :], preferred_element_type=f32)

    def body(i, carry):
        at = pl.ds(pl.multiple_of(i * step, step), step)
        out_ref[at, :] = gelu_of(wide[at, :], width).astype(bf16)
        return carry

    lax.fori_loop(0, out_ref.shape[0] // step, body, 0)


def activate(messages, width, rows, after):
    return pl.pallas_call(
        functools.partial(activate_kernel, width, len(messages)),
        name="activate",
        out_shape=array((rows, messages[0].shape[1]), bf16),
        in_specs=[whole_vmem()] * len(messages) + [anywhere()] * len(after),
        out_specs=whole_vmem(),
        scratch_shapes=[pltpu.VMEM((rows, messages[0].shape[1]), f32)],
        compiler_params=pltpu.CompilerParams(vmem_limit_bytes=3 * MIB),
    )(*messages, *after)


def pack_kernel(taps, padded, own_hbm, peer_hbm, out_ref, sems):
    part = own_hbm.shape[0] // taps
    _, core = here()
    copies = []
    for p, source in enumerate((own_hbm, peer_hbm)):
        place = core if p == 0 else 1 - core
        for k in range(taps):
            to = pl.ds(pl.multiple_of(k * padded + place * part, 16), part)
            copies.append(
                pltpu.make_async_copy(
                    source.at[k * part : (k + 1) * part, :], out_ref.at[to, :], sems.at[p, k]
                )
            )
    for c in copies:
        c.start()
    if padded > 2 * part:
        for k in range(taps):
            out_ref[k * padded + 2 * part : (k + 1) * padded, :] = jnp.zeros(
                (padded - 2 * part, out_ref.shape[1]), bf16
            )
    for c in copies:
        c.wait()


def pack_filter(own, peer, taps, padded):
    model_dim = own.shape[1]
    part = own.shape[0] // taps
    if part % 16:
        own, peer = (w.reshape(taps, part, model_dim) for w in (own, peer))
        first = lax.axis_index("mp") == 0
        low, high = jnp.where(first, own, peer), jnp.where(first, peer, own)
        both = jnp.concatenate([low, high], axis=1)
        both = jnp.pad(both, ((0, 0), (0, padded - 2 * part), (0, 0)))
        return both.reshape(taps * padded, model_dim)
    return pl.pallas_call(
        functools.partial(pack_kernel, taps, padded),
        name="pack_filter",
        out_shape=array((taps * padded, model_dim), bf16),
        in_specs=[anywhere()] * 2,
        out_specs=whole_vmem(),
        scratch_shapes=[pltpu.SemaphoreType.DMA((2, taps))],
        compiler_params=pltpu.CompilerParams(vmem_limit_bytes=2 * MIB),
    )(in_hbm(own), peer)


def conv_kernel(
    chips, bits, taps, tile, wanted, columns, outs, edged, feat_hbm, edge_ref, *rest
):
    count = len(wanted)
    block_refs = rest[:count]
    weight_ref = rest[count]
    cols, feat, sem = rest[-3:]
    out_refs = rest[-3 - outs : -3]
    rows, padded = block_refs[0].shape
    half = rows // 2
    chip, core = here()
    if 0 in wanted:
        copy = pltpu.make_async_copy(feat_hbm, feat, sem)
        copy.start()
    row = lax.broadcasted_iota(jnp.int32, (half, padded), 0)
    for j, k in enumerate(wanted):
        mask = jnp.where(core == 0, k, flipped_bits(k, bits))
        left = (chip ^ mask) - (1 - core)
        right = (chip ^ mask) + core
        block = block_refs[j][...]
        if edged:
            before = edge_ref[jnp.where(left >= 0, left ^ chip, 0)]
            before = jnp.where(left >= 0, before, 0.0)
            after = edge_ref[jnp.where(right < chips, right ^ chip, 0)]
            after = jnp.where(right < chips, after, 0.0)
        else:
            before = after = jnp.zeros((8, padded), f32)
        even = block[0:half].astype(f32)
        odd = block[half:rows].astype(f32)

        def back(v, strip_row):
            return jnp.where(row == 0, before[strip_row : strip_row + 1], pltpu.roll(v, 1, 0))

        def ahead(v, strip_row):
            return jnp.where(
                row == half - 1, after[strip_row : strip_row + 1], pltpu.roll(v, half - 1, 0)
            )

        lagged = [back(even, 2), back(odd, 3), even, odd, ahead(even, 0), ahead(odd, 1)]
        for i, v in enumerate(lagged):
            piece = v.astype(bf16)
            if i < taps:
                cols[j * rows : j * rows + half, i * padded : (i + 1) * padded] = piece
            if i > 0:
                cols[j * rows + half : (j + 1) * rows, (i - 1) * padded : i * padded] = piece
    pick = pick_rows(rows)
    if 0 in wanted:
        copy.wait()
    for j, k in enumerate(wanted):
        for h, (first, last) in enumerate(columns):
            out_ref = out_refs[j * len(columns) + h]
            for at in range(first, last, tile):
                got = jnp.dot(
                    cols[j * rows : (j + 1) * rows],
                    weight_ref[:, at : at + tile],
                    preferred_element_type=f32,
                )
                if k == 0 and at < feat.shape[1]:
                    width = min(tile, feat.shape[1] - at)
                    skip = jnp.dot(
                        pick, feat[:, at : at + width], preferred_element_type=f32
                    )
                    if width < tile:
                        skip = jnp.concatenate(
                            [skip, jnp.zeros((rows, tile - width), f32)], axis=1
                        )
                    got = got + skip
                out_ref[:, at - first : at - first + tile] = got.astype(out_ref.dtype)


def edge_terms_kernel(chips, taps, edge_ref, weight_ref, *rest):
    out_ref, cols = rest[-2:]
    padded = edge_ref.shape[2]
    chip, core = here()
    left = (chip ^ (chips - 1)) - (1 - core)
    right = (chip ^ (chips - 1)) + core
    before = edge_ref[jnp.where(left >= 0, left ^ chip, 0)]
    before = jnp.where(left >= 0, before, 0.0)
    after = edge_ref[jnp.where(right < chips, right ^ chip, 0)]
    after = jnp.where(right < chips, after, 0.0)
    none = jnp.zeros((1, padded), f32)
    blank = jnp.zeros((12, padded), f32)
    terms = {
        0: (before[2:3], before[3:4], none, none),
        1: (before[3:4], none, none, none),
        3: (none, none, none, after[0:1]),
        4: (none, none, after[0:1], after[1:2]),
    }
    for k in range(taps):
        rows = terms.get(k, (none,) * 4)
        cols[:, k * padded : (k + 1) * padded] = jnp.concatenate(
            [*rows, blank], axis=0
        ).astype(bf16)
    span = out_ref.shape[1]
    quarters = [
        jnp.dot(cols[...], weight_ref[:, at : at + span], preferred_element_type=f32)[0:4]
        for at in range(0, 4 * span, span)
    ]
    out_ref[...] = jnp.concatenate(quarters, axis=0).astype(bf16)


def edge_terms(edges, weight, taps, after):
    chips = edges.shape[0]
    depth, model_dim = weight.shape
    return pl.pallas_call(
        functools.partial(edge_terms_kernel, chips, taps),
        name="edge_terms",
        out_shape=array((16, model_dim // 4), bf16),
        in_specs=[whole_vmem()] * 2 + [anywhere()] * len(after),
        out_specs=whole_vmem(),
        scratch_shapes=[pltpu.VMEM((16, depth), bf16)],
        compiler_params=pltpu.CompilerParams(vmem_limit_bytes=2 * MIB),
    )(edges, weight, *after)


def conv(blocks, edges, features, weight, taps, wanted, dtypes, columns, after):
    chips = lax.axis_size("seq")
    bits = chips.bit_length() - 1
    rows = features.shape[0]
    edged = edges is not None
    depth, model_dim = weight.shape
    count = len(wanted)
    pieces = len(columns)
    got = pl.pallas_call(
        functools.partial(
            conv_kernel, chips, bits, taps, 256, wanted, columns, count * pieces, edged
        ),
        name="conv",
        out_shape=[array((rows, b - a), d) for d in dtypes for a, b in columns],
        in_specs=[anywhere()] + [whole_vmem()] * (count + 2) + [anywhere()] * len(after),
        out_specs=[whole_vmem()] * (count * pieces),
        scratch_shapes=[
            pltpu.VMEM((count * rows, depth), bf16),
            pltpu.VMEM(features.shape, bf16),
            pltpu.SemaphoreType.DMA,
        ],
        compiler_params=pltpu.CompilerParams(vmem_limit_bytes=(5 + 2 * count) * MIB),
    )(in_hbm(features), edges if edged else blocks[0], *blocks, weight, *after)
    return [got[j * pieces : (j + 1) * pieces] for j in range(count)]


def sum_kernel(count, *refs):
    out_ref = refs[-1]
    out_ref[...] = tree_sum([r[...].astype(f32) for r in refs[:count]]).astype(out_ref.dtype)


def add_up(terms, dtype, after=()):
    return pl.pallas_call(
        functools.partial(sum_kernel, len(terms)),
        name="add_up",
        out_shape=array(terms[0].shape, dtype),
        in_specs=[whole_vmem()] * len(terms) + [anywhere()] * len(after),
        out_specs=whole_vmem(),
        compiler_params=pltpu.CompilerParams(vmem_limit_bytes=4 * MIB),
    )(*terms, *after)


def encode_kernel(pieces, arrivals, pair_weight_ref, term_ref, *rest):
    own_refs = rest[:pieces]
    come_refs = rest[pieces : pieces + arrivals * pieces]
    encoded_ref, feats_ref = rest[-2:]
    rows = own_refs[0].shape[0]
    half = rows // 2
    pairs = half // PAIR_POOL
    at = lax.broadcasted_iota(jnp.int32, (pairs, half), 0)
    of = lax.broadcasted_iota(jnp.int32, (pairs, half), 1) // PAIR_POOL
    spread = jnp.where(at == of, 1.0 / PAIR_POOL, 0.0).astype(bf16)
    feats = jnp.zeros(feats_ref.shape, f32)
    quarters = term_ref[...].astype(f32)
    all_terms = jnp.concatenate([quarters[q : q + 4] for q in range(0, 16, 4)], axis=1)
    first = 0
    for h in range(pieces):
        last = first + own_refs[h].shape[1]
        total = own_refs[h][...]
        for a in range(arrivals):
            total = total + come_refs[a * pieces + h][...].astype(f32)
        terms = all_terms[:, first:last]
        row = lax.broadcasted_iota(jnp.int32, (half, last - first), 0)
        even, odd = (
            part
            + jnp.where(row == 0, terms[i : i + 1], 0.0)
            + jnp.where(row == half - 1, terms[i + 2 : i + 3], 0.0)
            for i, part in enumerate((total[:half], total[half:]))
        )
        encoded = jnp.maximum(even, odd).astype(bf16)
        encoded_ref[:, first:last] = encoded
        pooled = jnp.dot(spread, encoded, preferred_element_type=f32).astype(bf16)
        feats = feats + jnp.dot(
            pooled, pair_weight_ref[first:last, :], preferred_element_type=f32
        )
        first = last
    feats_ref[...] = feats.astype(bf16).astype(f32)


def encode(own, come, terms, pair_weight, after):
    rows = own[0].shape[0]
    pieces = len(own)
    half = rows // 2
    return pl.pallas_call(
        functools.partial(encode_kernel, pieces, len(come)),
        name="encode",
        out_shape=[
            array((half, sum(v.shape[1] for v in own)), bf16),
            array((half // PAIR_POOL, pair_weight.shape[1]), f32),
        ],
        in_specs=[whole_vmem()] * (2 + pieces * (1 + len(come))) + [anywhere()] * len(after),
        out_specs=[whole_vmem()] * 2,
        compiler_params=pltpu.CompilerParams(vmem_limit_bytes=8 * MIB),
    )(pair_weight, terms, *own, *sum(come, []), *after)


def normalised(encoded_ref, gain_ref):
    wide = encoded_ref[...].astype(f32)
    scale = lax.rsqrt(jnp.mean(wide * wide, axis=-1, keepdims=True) + norm_eps)
    return (wide * scale * gain_ref[...][None]).astype(bf16)


def keyval_kernel(encoded_ref, gain_ref, weight_ref, out_ref):
    out_ref[...] = lax.dot_general(
        normalised(encoded_ref, gain_ref),
        weight_ref[...],
        (((1,), (1,)), ((), ())),
        preferred_element_type=f32,
    ).astype(bf16)


def project_keyvals(encoded, gain, weight_t):
    return pl.pallas_call(
        keyval_kernel,
        name="keyvals",
        out_shape=array((encoded.shape[0], weight_t.shape[0]), bf16),
        in_specs=[whole_vmem()] * 3,
        out_specs=whole_vmem(),
        compiler_params=pltpu.CompilerParams(vmem_limit_bytes=4 * MIB),
    )(encoded, gain, weight_t)


def bundle_kernel(keyval_ref, mine_ref, other_ref, out_ref):
    rows, columns = keyval_ref.shape
    spare = out_ref.shape[1] - columns
    pieces = []
    for ref in (mine_ref, other_ref):
        feats = ref[...]
        pieces += [feats[:, g : g + spare] for g in range(0, feats.shape[1], spare)]
    used = sum(p.shape[0] for p in pieces)
    pieces.append(jnp.zeros((rows - used, spare), f32))
    out_ref[:, :columns] = keyval_ref[...]
    out_ref[:, columns:] = jnp.concatenate(pieces, axis=0).astype(bf16)


def bundle(keyval, mine, other):
    return pl.pallas_call(
        bundle_kernel,
        name="bundle",
        out_shape=array((keyval.shape[0], lane_pad(keyval.shape[1])), bf16),
        in_specs=[whole_vmem()] * 3,
        out_specs=whole_vmem(),
        compiler_params=pltpu.CompilerParams(vmem_limit_bytes=4 * MIB),
    )(keyval, mine, other)


def attend_kernel(
    parts,
    heads,
    first,
    last,
    group,
    scale_ref,
    encoded_ref,
    gain_ref,
    query_weight_ref,
    start_ref,
    weight_ref,
    *rest,
):
    part_refs = rest[:parts]
    out_ref, done_ref, keys, values = rest[-4:]
    rows = encoded_ref.shape[0]
    key_dim = query_weight_ref.shape[1] // heads
    normed = normalised(encoded_ref, gain_ref)
    span = part_refs[0].shape[0]
    value_dim = values.shape[1]
    for k in range(parts):
        got = part_refs[k][...]
        keys[k * span : (k + 1) * span, :] = got[:, :key_dim]
        values[k * span : (k + 1) * span, :] = got[:, key_dim : key_dim + value_dim]
    total = start_ref[...].astype(f32)
    for n in range(first, last, group):
        got = jnp.dot(
            normed,
            query_weight_ref[:, n * key_dim : (n + group) * key_dim],
            preferred_element_type=f32,
        )
        queries = jnp.concatenate(
            [
                got[:, h * key_dim : (h + 1) * key_dim]
                * (scale_ref[n + h] / math.sqrt(key_dim))
                for h in range(group)
            ],
            axis=0,
        ).astype(bf16)
        scores = lax.dot_general(
            queries, keys[...], (((1,), (1,)), ((), ())), preferred_element_type=f32
        )
        weights = jnp.exp(logit_cap * jnp.tanh(scores * (1.0 / logit_cap)))
        sums = jnp.sum(weights, axis=-1, keepdims=True)
        mixed = jnp.dot(weights.astype(bf16), values[...], preferred_element_type=f32) / sums
        mixed = mixed.astype(bf16)
        for h in range(group):
            at = (n + h) * value_dim
            total = total + jnp.dot(
                mixed[h * rows : (h + 1) * rows],
                weight_ref[at : at + value_dim, :],
                preferred_element_type=f32,
            )
    out_ref[...] = total.astype(out_ref.dtype)
    done_ref[...] = total[0:8, 0:128]


def attend(
    encoded, gain, query_weight, scale, start, output_weight, parts, first, last, dtype, after
):
    rows, model_dim = start.shape
    heads = scale.shape[0]
    key_dim = query_weight.shape[1] // heads
    value_dim = output_weight.shape[0] // heads
    total_keys = parts[0].shape[0] * len(parts)
    group = 2
    return pl.pallas_call(
        functools.partial(attend_kernel, len(parts), heads, first, last, group),
        name="attend",
        out_shape=[array((rows, model_dim), dtype), array((8, 128), f32)],
        in_specs=[smem()] + [whole_vmem()] * (5 + len(parts)) + [anywhere()] * len(after),
        out_specs=[whole_vmem()] * 2,
        scratch_shapes=[
            pltpu.VMEM((total_keys, key_dim), bf16),
            pltpu.VMEM((total_keys, value_dim), bf16),
        ],
        compiler_params=pltpu.CompilerParams(
            vmem_limit_bytes=8 * MIB if total_keys <= 1024 else 32 * MIB
        ),
    )(scale, encoded, gain, query_weight, start, output_weight, *parts, *after)


def unpack_kernel(chips, pairs, rows, width, *refs):
    message_refs = refs[:chips][::-1]
    out_ref = refs[-1]
    dim = out_ref.shape[2]
    padded = message_refs[0].shape[1]
    for k in range(chips):
        spare = dim * SPARE_ROWS // rows
        first = jnp.concatenate(
            [
                message_refs[k][
                    g * SPARE_ROWS : (g + 1) * SPARE_ROWS, width + 8 : width + 8 + spare
                ]
                for g in range(dim // spare)
            ],
            axis=1,
        )
        piece = message_refs[k][rows:, :]
        piece = [piece[:, g : g + dim] for g in range(0, padded, dim)]
        piece = jnp.concatenate([first] + piece, axis=0)
        piece = piece[: 2 * pairs * pairs].reshape(pairs, 2 * pairs, dim)
        out_ref[k * pairs : (k + 1) * pairs] = piece


def unpack_pairs(messages, pairs, dim, rows, width, after):
    chips = len(messages)
    return pl.pallas_call(
        functools.partial(unpack_kernel, chips, pairs, rows, width),
        name="unpack_pairs",
        out_shape=array((chips * pairs, 2 * pairs, dim), bf16),
        in_specs=[whole_vmem()] * chips + [anywhere()] * len(after),
        out_specs=whole_vmem(),
        compiler_params=pltpu.CompilerParams(vmem_limit_bytes=4 * MIB),
    )(*messages[::-1], *after)


def pair_kernel(
    chips, columns_used, input_ref, cotangent_ref, other_cotangent_ref, flip_ref, turned_ref, other_ref, *rest
):
    bundle_refs = rest[:chips]
    out_ref, grad_ref, stacked, mirror, summed, flipped, cotangent = rest[-7:]
    rows, columns, dim = input_ref.shape
    parts = 2 * chips
    wide = 2 * rows
    chip, core = here()
    me = chip * 2 + core
    for k in range(chips):
        got = bundle_refs[k][:, columns_used:].astype(f32)
        count = 2 * dim // got.shape[1]
        for f in range(2):
            at = f * count * rows
            stacked[2 * k + f] = jnp.concatenate(
                [got[at + g * rows : at + (g + 1) * rows] for g in range(count)], axis=1
            )
    own, other = stacked[0], stacked[1]
    both_k = jnp.concatenate(
        [jnp.where(core == 0, own, other), jnp.where(core == 0, other, own)], axis=0
    )[:, dim:][None]
    for k in range(parts):
        source = turned_ref if k % 2 == 0 else other_ref
        value = source[k // 2 * rows : (k // 2 + 1) * rows].astype(f32)
        value = value + stacked[k][:, None, :dim] * both_k
        mirror[k] = value.reshape(rows * wide, dim).astype(bf16)
    target = lax.broadcasted_iota(jnp.int32, (rows * wide, rows * wide), 0)
    origin = lax.broadcasted_iota(jnp.int32, (rows * wide, rows * wide), 1)
    swap = jnp.where(origin == (target % rows) * wide + target // rows, 1.0, 0.0).astype(bf16)
    for b in range(parts):
        turned = jnp.dot(swap, mirror[b ^ me], preferred_element_type=f32)
        flipped[:, b * rows : (b + 1) * rows, :] = turned.reshape(wide, rows, dim)
    every = jnp.concatenate([stacked[b ^ me] for b in range(parts)], axis=0)[:, dim:]
    for i in range(rows):
        at = pl.ds(i * columns, columns)
        value = input_ref[i].astype(f32) + own[i : i + 1, :dim] * every
        summed[at, :] = value.astype(bf16)
    facing = flipped[pl.ds(core * rows, rows)].reshape(rows * columns, dim).astype(bf16)
    update = jnp.dot(facing, flip_ref[...], preferred_element_type=f32)
    update = update + summed[...].astype(f32)
    out_ref[...] = update.astype(bf16).reshape(rows, columns, dim)
    cotangent[pl.ds(core * rows, rows)] = cotangent_ref[...]
    cotangent[pl.ds((1 - core) * rows, rows)] = other_cotangent_ref[...]
    grad = lax.dot_general(
        flipped[...].reshape(wide * columns, dim).astype(bf16),
        cotangent[...].reshape(wide * columns, dim),
        (((0,), (0,)), ((), ())),
        preferred_element_type=f32,
    )
    grad_ref[...] = grad.astype(bf16)


def pair_update(pair_input, cotangents, flip_weight, turned, bundles, columns_used):
    rows, columns, dim = pair_input.shape
    chips = len(bundles)
    return pl.pallas_call(
        functools.partial(pair_kernel, chips, columns_used),
        name="pair",
        out_shape=[array((rows, columns, dim), bf16), array((dim, dim), bf16)],
        in_specs=[whole_vmem()] * (6 + chips),
        out_specs=[whole_vmem()] * 2,
        scratch_shapes=[
            pltpu.VMEM((2 * chips, rows, 2 * dim), f32),
            pltpu.VMEM((2 * chips, 2 * rows * rows, dim), bf16),
            pltpu.VMEM((rows * columns, dim), bf16),
            pltpu.VMEM((2 * rows, columns, dim), f32),
            pltpu.VMEM((2 * rows, columns, dim), bf16),
        ],
        compiler_params=pltpu.CompilerParams(
            vmem_limit_bytes=6 * MIB if chips <= 4 else 32 * MIB
        ),
    )(pair_input, *cotangents, flip_weight, *turned, *bundles)


def per_device(
    features,
    conv_weight,
    norm_gain,
    query_weight,
    keyval_weight,
    head_scale,
    output_weight,
    pair_weight,
    pair_input,
    flip_weight,
    pair_cotangent,
):
    chips = lax.axis_size("seq")
    bits = chips.bit_length() - 1
    windows = lax.axis_size("dp")
    taps = conv_weight.shape[0]
    model_dim = output_weight.shape[1]
    heads = head_scale.shape[0]
    features = features[0]

    masks = [(k, flipped_bits(k, bits)) for k in range(chips)]

    def send(value, mask, flip=0):
        cores = mask if isinstance(mask, tuple) else (mask, mask)
        return lax.ppermute(value, GROUP, hop_pairs(chips, cores, flip))

    rows, channels = features.shape
    width = channels // chips
    own_weight = conv_weight.reshape(-1, model_dim)
    peer_weight = send(own_weight, 0, 1)
    blocks = prep(features, pair_input[0], chips)

    messages = [blocks[0]] + [None] * (chips - 1)
    for k in range(chips - 1, 0, -1):
        messages[k] = send(blocks[k], k)
    weight = pack_filter(own_weight, peer_weight, taps, blocks[0].shape[1])
    cotangent, weight = lax.optimization_barrier((pair_cotangent[0], weight))
    cotangents = (pair_cotangent[0], send(cotangent, 0, 1))

    last = chips - 1
    rest = sorted(range(last), key=lambda k: (1 - (k & 1), -k))

    prepared = {}

    def active(k):
        if k not in prepared:
            sources = [messages[j] for j in dict.fromkeys(masks[k])]
            after = [] if k == last else partial[last] if k & 1 else partial[1]
            prepared[k] = activate(sources, width, rows, after)
        return prepared[k]

    def partials(ks, columns, edges, after):
        dtypes = [bf16 if k & 1 else f32 for k in ks]
        got = conv(
            [active(k) for k in ks], edges, features, weight, taps, ks, dtypes, columns, after
        )
        return dict(zip(ks, got))

    columns = [(0, model_dim // 2), (model_dim // 2, model_dim)]
    partial = partials([last], columns[:1], None, [])
    partial[last] += partials([last], columns[1:], None, [cotangents[1]])[last]
    edges = send(edge_rows(messages, width, rows, partial[last]), 0, 1)
    arrivals = [messages[k] for k in range(1, last)]
    partial[last] = [lax.optimization_barrier((v, *arrivals))[0] for v in partial[last]]
    pairs, _, pair_dim = pair_input.shape[1:]
    turned = unpack_pairs(
        messages, pairs, pair_dim, rows, width, partial[last]
    )
    turned = (turned, send(turned, 0, 1))
    for ks in ([k for k in rest if k & 1], [k for k in rest if k and not k & 1], [0]):
        partial.update(partials(ks, columns, edges, [turned[1]]))
    terms = send(edge_terms(edges, weight, taps, partial[last ^ 1]), last)
    arrived = []
    for b in range(bits):
        bit = 1 << b
        leaving = [k for k in [last] + rest if k in partial and k & bit]
        got = {k ^ bit: [send(v, masks[bit]) for v in partial.pop(k)] for k in leaving}
        for k, values in got.items():
            if k == 0:
                arrived.append(values)
            else:
                dtype = bf16 if k & (2 * bit) else f32
                partial[k] = [
                    add_up([p, v], dtype, [turned[1]]) for p, v in zip(partial[k], values)
                ]

    encoded, feats = encode(partial[0], arrived, terms, pair_weight, [])
    keyval = project_keyvals(encoded, norm_gain, keyval_weight.T)
    own_bundle = bundle(keyval, feats, send(feats, 0, 1))
    bundles = [own_bundle] + [send(own_bundle, k) for k in range(1, chips)]
    pair_out, grad = pair_update(
        pair_input[0], cotangents, flip_weight, turned, bundles, keyval_weight.shape[1]
    )
    keyvals = bundles + [send(v, 0, 1) for v in bundles]

    def attend_heads(start, first, end, dtype, after):
        return attend(
            encoded,
            norm_gain,
            query_weight,
            head_scale,
            start,
            output_weight,
            keyvals,
            first,
            end,
            dtype,
            after,
        )

    halfway = heads // 2
    first_half, done = attend_heads(encoded, 0, halfway, f32, [])
    grad = add_up([grad] + [send(grad, k) for k in range(1, chips)], bf16, [done])
    block_out, done = attend_heads(first_half, halfway, heads, bf16, [grad])
    grad = add_up(
        [grad]
        + [
            lax.ppermute(grad, "dp", [(w, w ^ k) for w in range(windows)])
            for k in range(1, windows)
        ],
        f32,
        [done],
    )
    return (block_out[None], pair_out[None], grad)


def solution(mesh):
    placed = (
        P("dp", ("seq", "mp"), None),
        P(None, ("seq", "mp"), None),
        P(),
        P(),
        P(),
        P(),
        P(),
        P(),
        P("dp", ("seq", "mp"), None, None),
        P(),
        P("dp", ("seq", "mp"), None, None),
    )
    return jax.shard_map(
        per_device,
        mesh=mesh,
        in_specs=placed,
        out_specs=(P("dp", ("seq", "mp"), None), P("dp", ("seq", "mp"), None, None), P()),
        check_vma=False,
    )
```

```python
import functools
import math

import jax
import jax.numpy as jnp
from jax import lax
from jax.experimental import pallas as pl
from jax.experimental.pallas import tpu as pltpu
from jax.sharding import PartitionSpec as P

PAIR_POOL = 16
SPARE_ROWS = 32
norm_eps = 1e-06
logit_cap = 50.0
MIB = 1 << 20
GROUP = ("seq", "mp")
f32, bf16 = jnp.float32, jnp.bfloat16


def whole_vmem():
    return pl.BlockSpec(memory_space=pltpu.VMEM)


def anywhere():
    return pl.BlockSpec(memory_space=pl.ANY)


def smem():
    return pl.BlockSpec(memory_space=pltpu.SMEM)


def in_hbm(value):
    return pltpu.with_memory_space_constraint(value, pltpu.HBM)


def array(shape, dtype):
    return jax.ShapeDtypeStruct(shape, dtype)


def lane_pad(width):
    return (width + 127) // 128 * 128


def tree_sum(terms):
    while len(terms) > 1:
        terms = [terms[i] + terms[i + 1] for i in range(0, len(terms), 2)]
    return terms[0]


def flipped_bits(mask, bits):
    return sum(((mask >> b) & 1) << (bits - 1 - b) for b in range(bits))


def here():
    return lax.axis_index("seq"), lax.axis_index("mp")


def hop_pairs(chips, core_masks, core_flip):
    pairs = []
    for chip in range(chips):
        for core in range(2):
            target = (chip ^ core_masks[core]) * 2 + (core ^ core_flip)
            pairs.append((chip * 2 + core, target))
    return pairs


def pick_rows(rows):
    half = rows // 2
    target = lax.broadcasted_iota(jnp.int32, (rows, rows), 0)
    source = lax.broadcasted_iota(jnp.int32, (rows, rows), 1)
    wanted = jnp.where(target < half, 2 * target, 2 * (target - half) + 1)
    return jnp.where(source == wanted, 1.0, 0.0).astype(bf16)


def prep_kernel(chips, width, feat_hbm, pair_hbm, *rest):
    block_refs = rest[:chips]
    feat, pair, split, sems = rest[chips:]
    rows = feat.shape[0]
    chip, _ = here()
    chunks = sems.shape[0] - 1
    step = rows // chunks

    def copy(n):
        at = pl.ds(n * step, step)
        return pltpu.make_async_copy(feat_hbm.at[at, :], feat.at[at, :], sems.at[n])

    pair_copy = pltpu.make_async_copy(pair_hbm, pair, sems.at[chunks])
    for n in range(chunks):
        copy(n).start()
    pair_copy.start()
    for n in range(chunks):
        copy(n).wait()
        fill_rows(chips, width, n * step, step, feat, split)
    pair_copy.wait()
    pairs, _, dim = pair.shape
    lanes = split.shape[2] // dim
    extra = block_refs[0].shape[0] - rows
    spare = dim * SPARE_ROWS // rows
    for k in range(chips):
        at = pl.ds(pl.multiple_of((chip ^ k) * 2 * pairs, 16), 2 * pairs)
        piece = pair[:, at, :].reshape(2 * pairs * pairs, dim)
        block_refs[k][0:rows, :] = split[chip ^ k]
        for g in range(dim // spare):
            block_refs[k][
                g * SPARE_ROWS : (g + 1) * SPARE_ROWS, width + 8 : width + 8 + spare
            ] = piece[:SPARE_ROWS, g * spare : (g + 1) * spare]
        for g in range(lanes):
            part = piece[SPARE_ROWS + g * extra : SPARE_ROWS + (g + 1) * extra]
            block_refs[k][rows : rows + part.shape[0], g * dim : (g + 1) * dim] = part


def fill_rows(chips, width, start, step, feat, split):
    at = slice(start, start + step)
    x = feat[at, :].astype(f32)
    scale = lax.rsqrt(jnp.mean(x * x, axis=-1, keepdims=True) + norm_eps)
    high = scale.astype(bf16)
    middle = (scale - high.astype(f32)).astype(bf16)
    low = (scale - high.astype(f32) - middle.astype(f32)).astype(bf16)
    lane = lax.broadcasted_iota(jnp.int32, (step, split.shape[2] - width), 1)
    tail = jnp.where(
        lane == 0,
        high.astype(f32),
        jnp.where(
            lane == 1, middle.astype(f32), jnp.where(lane == 2, low.astype(f32), 0.0)
        ),
    ).astype(bf16)
    for q in range(chips):
        split[q, at, 0:width] = feat[at, q * width : (q + 1) * width]
        split[q, at, width:] = tail


def prep(features, pair_input, chips):
    rows, channels = features.shape
    width = channels // chips
    padded = lane_pad(width)
    pairs, _, dim = pair_input.shape
    extra = -(-(2 * pairs * pairs - SPARE_ROWS) // (16 * (padded // dim))) * 16
    return pl.pallas_call(
        functools.partial(prep_kernel, chips, width),
        name="prep",
        out_shape=[array((rows + extra, padded), bf16)] * chips,
        in_specs=[anywhere()] * 2,
        out_specs=[whole_vmem()] * chips,
        scratch_shapes=[
            pltpu.VMEM((rows, channels), bf16),
            pltpu.VMEM(pair_input.shape, bf16),
            pltpu.VMEM((chips, rows, padded), bf16),
            pltpu.SemaphoreType.DMA((2,)),
        ],
        compiler_params=pltpu.CompilerParams(vmem_limit_bytes=10 * MIB),
    )(in_hbm(features), in_hbm(pair_input))


def gelu_of(block, width):
    scale = block[:, width : width + 1] + block[:, width + 1 : width + 2]
    scale = scale + block[:, width + 2 : width + 3]
    v = block * scale
    g = (0.5 * v) * (1.0 + lax.erf(v * math.sqrt(0.5)))
    lane = lax.broadcasted_iota(jnp.int32, block.shape, 1)
    return jnp.where(lane < width, g, 0.0)


def edges_kernel(chips, width, rows, *refs):
    message_refs = refs[:chips][::-1]
    out_ref = refs[-1]
    strips = []
    for ref in message_refs:
        for start, row in ((0, 0), (0, 1), (rows - 16, 14), (rows - 16, 15)):
            strips.append(ref[start : start + 16, :].astype(f32)[row : row + 1])
    prepared = gelu_of(jnp.concatenate(strips, axis=0), width)
    for k in range(chips):
        out_ref[k, 0:4] = prepared[4 * k : 4 * k + 4]
        out_ref[k, 4:8] = jnp.zeros((4, prepared.shape[1]), f32)


def edge_rows(messages, width, rows, after):
    chips = len(messages)
    padded = messages[0].shape[1]
    return pl.pallas_call(
        functools.partial(edges_kernel, chips, width, rows),
        name="edge_rows",
        out_shape=array((chips, 8, padded), f32),
        in_specs=[whole_vmem()] * chips + [anywhere()] * len(after),
        out_specs=whole_vmem(),
        compiler_params=pltpu.CompilerParams(vmem_limit_bytes=2 * MIB),
    )(*messages[::-1], *after)


def activate_kernel(width, count, *refs):
    message_refs, out_ref, wide = refs[:count], refs[-2], refs[-1]
    _, core = here()
    step = 32
    rows = out_ref.shape[0]
    pick = pick_rows(rows)
    if count == 1:
        wide[...] = jnp.dot(pick, message_refs[0][0:rows, :], preferred_element_type=f32)
    else:

        @pl.when(core == 0)
        def _():
            wide[...] = jnp.dot(pick, message_refs[0][0:rows, :], preferred_element_type=f32)

        @pl.when(core != 0)
        def _():
            wide[...] = jnp.dot(pick, message_refs[1][0:rows, :], preferred_element_type=f32)

    def body(i, carry):
        at = pl.ds(pl.multiple_of(i * step, step), step)
        out_ref[at, :] = gelu_of(wide[at, :], width).astype(bf16)
        return carry

    lax.fori_loop(0, out_ref.shape[0] // step, body, 0)


def activate(messages, width, rows, after):
    return pl.pallas_call(
        functools.partial(activate_kernel, width, len(messages)),
        name="activate",
        out_shape=array((rows, messages[0].shape[1]), bf16),
        in_specs=[whole_vmem()] * len(messages) + [anywhere()] * len(after),
        out_specs=whole_vmem(),
        scratch_shapes=[pltpu.VMEM((rows, messages[0].shape[1]), f32)],
        compiler_params=pltpu.CompilerParams(vmem_limit_bytes=3 * MIB),
    )(*messages, *after)


def pack_kernel(taps, padded, own_hbm, peer_hbm, out_ref, sems):
    part = own_hbm.shape[0] // taps
    _, core = here()
    copies = []
    for p, source in enumerate((own_hbm, peer_hbm)):
        place = core if p == 0 else 1 - core
        for k in range(taps):
            to = pl.ds(pl.multiple_of(k * padded + place * part, 16), part)
            copies.append(
                pltpu.make_async_copy(
                    source.at[k * part : (k + 1) * part, :], out_ref.at[to, :], sems.at[p, k]
                )
            )
    for c in copies:
        c.start()
    if padded > 2 * part:
        for k in range(taps):
            out_ref[k * padded + 2 * part : (k + 1) * padded, :] = jnp.zeros(
                (padded - 2 * part, out_ref.shape[1]), bf16
            )
    for c in copies:
        c.wait()


def pack_filter(own, peer, taps, padded):
    model_dim = own.shape[1]
    part = own.shape[0] // taps
    if part % 16:
        own, peer = (w.reshape(taps, part, model_dim) for w in (own, peer))
        first = lax.axis_index("mp") == 0
        low, high = jnp.where(first, own, peer), jnp.where(first, peer, own)
        both = jnp.concatenate([low, high], axis=1)
        both = jnp.pad(both, ((0, 0), (0, padded - 2 * part), (0, 0)))
        return both.reshape(taps * padded, model_dim)
    return pl.pallas_call(
        functools.partial(pack_kernel, taps, padded),
        name="pack_filter",
        out_shape=array((taps * padded, model_dim), bf16),
        in_specs=[anywhere()] * 2,
        out_specs=whole_vmem(),
        scratch_shapes=[pltpu.SemaphoreType.DMA((2, taps))],
        compiler_params=pltpu.CompilerParams(vmem_limit_bytes=2 * MIB),
    )(in_hbm(own), peer)


def conv_kernel(
    chips, bits, taps, tile, wanted, columns, outs, edged, feat_hbm, edge_ref, *rest
):
    count = len(wanted)
    block_refs = rest[:count]
    weight_ref = rest[count]
    cols, feat, sem = rest[-3:]
    out_refs = rest[-3 - outs : -3]
    rows, padded = block_refs[0].shape
    half = rows // 2
    chip, core = here()
    if 0 in wanted:
        copy = pltpu.make_async_copy(feat_hbm, feat, sem)
        copy.start()
    row = lax.broadcasted_iota(jnp.int32, (half, padded), 0)
    for j, k in enumerate(wanted):
        mask = jnp.where(core == 0, k, flipped_bits(k, bits))
        left = (chip ^ mask) - (1 - core)
        right = (chip ^ mask) + core
        block = block_refs[j][...]
        if edged:
            before = edge_ref[jnp.where(left >= 0, left ^ chip, 0)]
            before = jnp.where(left >= 0, before, 0.0)
            after = edge_ref[jnp.where(right < chips, right ^ chip, 0)]
            after = jnp.where(right < chips, after, 0.0)
        else:
            before = after = jnp.zeros((8, padded), f32)
        even = block[0:half].astype(f32)
        odd = block[half:rows].astype(f32)

        def back(v, strip_row):
            return jnp.where(row == 0, before[strip_row : strip_row + 1], pltpu.roll(v, 1, 0))

        def ahead(v, strip_row):
            return jnp.where(
                row == half - 1, after[strip_row : strip_row + 1], pltpu.roll(v, half - 1, 0)
            )

        lagged = [back(even, 2), back(odd, 3), even, odd, ahead(even, 0), ahead(odd, 1)]
        for i, v in enumerate(lagged):
            piece = v.astype(bf16)
            if i < taps:
                cols[j * rows : j * rows + half, i * padded : (i + 1) * padded] = piece
            if i > 0:
                cols[j * rows + half : (j + 1) * rows, (i - 1) * padded : i * padded] = piece
    pick = pick_rows(rows)
    if 0 in wanted:
        copy.wait()
    for j, k in enumerate(wanted):
        for h, (first, last) in enumerate(columns):
            out_ref = out_refs[j * len(columns) + h]
            for at in range(first, last, tile):
                got = jnp.dot(
                    cols[j * rows : (j + 1) * rows],
                    weight_ref[:, at : at + tile],
                    preferred_element_type=f32,
                )
                if k == 0 and at < feat.shape[1]:
                    width = min(tile, feat.shape[1] - at)
                    skip = jnp.dot(
                        pick, feat[:, at : at + width], preferred_element_type=f32
                    )
                    if width < tile:
                        skip = jnp.concatenate(
                            [skip, jnp.zeros((rows, tile - width), f32)], axis=1
                        )
                    got = got + skip
                out_ref[:, at - first : at - first + tile] = got.astype(out_ref.dtype)


def edge_terms_kernel(chips, taps, edge_ref, weight_ref, *rest):
    out_ref, cols = rest[-2:]
    padded = edge_ref.shape[2]
    chip, core = here()
    left = (chip ^ (chips - 1)) - (1 - core)
    right = (chip ^ (chips - 1)) + core
    before = edge_ref[jnp.where(left >= 0, left ^ chip, 0)]
    before = jnp.where(left >= 0, before, 0.0)
    after = edge_ref[jnp.where(right < chips, right ^ chip, 0)]
    after = jnp.where(right < chips, after, 0.0)
    none = jnp.zeros((1, padded), f32)
    blank = jnp.zeros((12, padded), f32)
    terms = {
        0: (before[2:3], before[3:4], none, none),
        1: (before[3:4], none, none, none),
        3: (none, none, none, after[0:1]),
        4: (none, none, after[0:1], after[1:2]),
    }
    for k in range(taps):
        rows = terms.get(k, (none,) * 4)
        cols[:, k * padded : (k + 1) * padded] = jnp.concatenate(
            [*rows, blank], axis=0
        ).astype(bf16)
    span = out_ref.shape[1]
    quarters = [
        jnp.dot(cols[...], weight_ref[:, at : at + span], preferred_element_type=f32)[0:4]
        for at in range(0, 4 * span, span)
    ]
    out_ref[...] = jnp.concatenate(quarters, axis=0).astype(bf16)


def edge_terms(edges, weight, taps, after):
    chips = edges.shape[0]
    depth, model_dim = weight.shape
    return pl.pallas_call(
        functools.partial(edge_terms_kernel, chips, taps),
        name="edge_terms",
        out_shape=array((16, model_dim // 4), bf16),
        in_specs=[whole_vmem()] * 2 + [anywhere()] * len(after),
        out_specs=whole_vmem(),
        scratch_shapes=[pltpu.VMEM((16, depth), bf16)],
        compiler_params=pltpu.CompilerParams(vmem_limit_bytes=2 * MIB),
    )(edges, weight, *after)


def conv(blocks, edges, features, weight, taps, wanted, dtypes, columns, after):
    chips = lax.axis_size("seq")
    bits = chips.bit_length() - 1
    rows = features.shape[0]
    edged = edges is not None
    depth, model_dim = weight.shape
    count = len(wanted)
    pieces = len(columns)
    got = pl.pallas_call(
        functools.partial(
            conv_kernel, chips, bits, taps, 256, wanted, columns, count * pieces, edged
        ),
        name="conv",
        out_shape=[array((rows, b - a), d) for d in dtypes for a, b in columns],
        in_specs=[anywhere()] + [whole_vmem()] * (count + 2) + [anywhere()] * len(after),
        out_specs=[whole_vmem()] * (count * pieces),
        scratch_shapes=[
            pltpu.VMEM((count * rows, depth), bf16),
            pltpu.VMEM(features.shape, bf16),
            pltpu.SemaphoreType.DMA,
        ],
        compiler_params=pltpu.CompilerParams(vmem_limit_bytes=(5 + 2 * count) * MIB),
    )(in_hbm(features), edges if edged else blocks[0], *blocks, weight, *after)
    return [got[j * pieces : (j + 1) * pieces] for j in range(count)]


def sum_kernel(count, backwards, *refs):
    out_ref = refs[-1]
    terms = [r[...].astype(f32) for r in refs[:count]]
    out_ref[...] = tree_sum(terms[::-1] if backwards else terms).astype(out_ref.dtype)


def add_up(terms, dtype, after=(), backwards=False):
    terms = terms[::-1] if backwards else terms
    return pl.pallas_call(
        functools.partial(sum_kernel, len(terms), backwards),
        name="add_up",
        out_shape=array(terms[0].shape, dtype),
        in_specs=[whole_vmem()] * len(terms) + [anywhere()] * len(after),
        out_specs=whole_vmem(),
        compiler_params=pltpu.CompilerParams(vmem_limit_bytes=4 * MIB),
    )(*terms, *after)


def encode_kernel(pieces, arrivals, pair_weight_ref, term_ref, *rest):
    own_refs = rest[:pieces]
    come_refs = rest[pieces : pieces + arrivals * pieces]
    encoded_ref, feats_ref = rest[-2:]
    rows = own_refs[0].shape[0]
    half = rows // 2
    pairs = half // PAIR_POOL
    at = lax.broadcasted_iota(jnp.int32, (pairs, half), 0)
    of = lax.broadcasted_iota(jnp.int32, (pairs, half), 1) // PAIR_POOL
    spread = jnp.where(at == of, 1.0 / PAIR_POOL, 0.0).astype(bf16)
    feats = jnp.zeros(feats_ref.shape, f32)
    quarters = term_ref[...].astype(f32)
    all_terms = jnp.concatenate([quarters[q : q + 4] for q in range(0, 16, 4)], axis=1)
    first = 0
    for h in range(pieces):
        last = first + own_refs[h].shape[1]
        total = own_refs[h][...]
        for a in range(arrivals):
            total = total + come_refs[a * pieces + h][...].astype(f32)
        terms = all_terms[:, first:last]
        row = lax.broadcasted_iota(jnp.int32, (half, last - first), 0)
        even, odd = (
            part
            + jnp.where(row == 0, terms[i : i + 1], 0.0)
            + jnp.where(row == half - 1, terms[i + 2 : i + 3], 0.0)
            for i, part in enumerate((total[:half], total[half:]))
        )
        encoded = jnp.maximum(even, odd).astype(bf16)
        encoded_ref[:, first:last] = encoded
        pooled = jnp.dot(spread, encoded, preferred_element_type=f32).astype(bf16)
        feats = feats + jnp.dot(
            pooled, pair_weight_ref[first:last, :], preferred_element_type=f32
        )
        first = last
    feats_ref[...] = feats.astype(bf16).astype(f32)


def encode(own, come, terms, pair_weight, after):
    rows = own[0].shape[0]
    pieces = len(own)
    half = rows // 2
    return pl.pallas_call(
        functools.partial(encode_kernel, pieces, len(come)),
        name="encode",
        out_shape=[
            array((half, sum(v.shape[1] for v in own)), bf16),
            array((half // PAIR_POOL, pair_weight.shape[1]), f32),
        ],
        in_specs=[whole_vmem()] * (2 + pieces * (1 + len(come))) + [anywhere()] * len(after),
        out_specs=[whole_vmem()] * 2,
        compiler_params=pltpu.CompilerParams(vmem_limit_bytes=8 * MIB),
    )(pair_weight, terms, *own, *sum(come, []), *after)


def normalised(encoded_ref, gain_ref):
    wide = encoded_ref[...].astype(f32)
    scale = lax.rsqrt(jnp.mean(wide * wide, axis=-1, keepdims=True) + norm_eps)
    return (wide * scale * gain_ref[...][None]).astype(bf16)


def keyval_kernel(encoded_ref, gain_ref, weight_ref, out_ref):
    out_ref[...] = lax.dot_general(
        normalised(encoded_ref, gain_ref),
        weight_ref[...],
        (((1,), (1,)), ((), ())),
        preferred_element_type=f32,
    ).astype(bf16)


def project_keyvals(encoded, gain, weight_t):
    return pl.pallas_call(
        keyval_kernel,
        name="keyvals",
        out_shape=array((encoded.shape[0], weight_t.shape[0]), bf16),
        in_specs=[whole_vmem()] * 3,
        out_specs=whole_vmem(),
        compiler_params=pltpu.CompilerParams(vmem_limit_bytes=4 * MIB),
    )(encoded, gain, weight_t)


def bundle_kernel(keyval_ref, mine_ref, other_ref, out_ref):
    rows, columns = keyval_ref.shape
    spare = out_ref.shape[1] - columns
    pieces = []
    for ref in (mine_ref, other_ref):
        feats = ref[...]
        pieces += [feats[:, g : g + spare] for g in range(0, feats.shape[1], spare)]
    used = sum(p.shape[0] for p in pieces)
    pieces.append(jnp.zeros((rows - used, spare), f32))
    out_ref[:, :columns] = keyval_ref[...]
    out_ref[:, columns:] = jnp.concatenate(pieces, axis=0).astype(bf16)


def bundle(keyval, mine, other):
    return pl.pallas_call(
        bundle_kernel,
        name="bundle",
        out_shape=array((keyval.shape[0], lane_pad(keyval.shape[1])), bf16),
        in_specs=[whole_vmem()] * 3,
        out_specs=whole_vmem(),
        compiler_params=pltpu.CompilerParams(vmem_limit_bytes=4 * MIB),
    )(keyval, mine, other)


def attend_kernel(
    parts,
    heads,
    first,
    last,
    group,
    scale_ref,
    encoded_ref,
    gain_ref,
    query_weight_ref,
    start_ref,
    weight_ref,
    *rest,
):
    part_refs = rest[:parts]
    out_ref, done_ref, keys, values = rest[-4:]
    rows = encoded_ref.shape[0]
    key_dim = query_weight_ref.shape[1] // heads
    normed = normalised(encoded_ref, gain_ref)
    span = part_refs[0].shape[0]
    value_dim = values.shape[1]
    for k in range(parts):
        got = part_refs[k][...]
        keys[k * span : (k + 1) * span, :] = got[:, :key_dim]
        values[k * span : (k + 1) * span, :] = got[:, key_dim : key_dim + value_dim]
    total = start_ref[...].astype(f32)
    for n in range(first, last, group):
        got = jnp.dot(
            normed,
            query_weight_ref[:, n * key_dim : (n + group) * key_dim],
            preferred_element_type=f32,
        )
        queries = jnp.concatenate(
            [
                got[:, h * key_dim : (h + 1) * key_dim]
                * (scale_ref[n + h] / math.sqrt(key_dim))
                for h in range(group)
            ],
            axis=0,
        ).astype(bf16)
        scores = lax.dot_general(
            queries, keys[...], (((1,), (1,)), ((), ())), preferred_element_type=f32
        )
        weights = jnp.exp(logit_cap * jnp.tanh(scores * (1.0 / logit_cap)))
        sums = jnp.sum(weights, axis=-1, keepdims=True)
        mixed = jnp.dot(weights.astype(bf16), values[...], preferred_element_type=f32) / sums
        mixed = mixed.astype(bf16)
        for h in range(group):
            at = (n + h) * value_dim
            total = total + jnp.dot(
                mixed[h * rows : (h + 1) * rows],
                weight_ref[at : at + value_dim, :],
                preferred_element_type=f32,
            )
    out_ref[...] = total.astype(out_ref.dtype)
    done_ref[...] = total[0:8, 0:128]


def attend(
    encoded, gain, query_weight, scale, start, output_weight, parts, first, last, dtype, after
):
    rows, model_dim = start.shape
    heads = scale.shape[0]
    key_dim = query_weight.shape[1] // heads
    value_dim = output_weight.shape[0] // heads
    total_keys = parts[0].shape[0] * len(parts)
    group = 2
    return pl.pallas_call(
        functools.partial(attend_kernel, len(parts), heads, first, last, group),
        name="attend",
        out_shape=[array((rows, model_dim), dtype), array((8, 128), f32)],
        in_specs=[smem()] + [whole_vmem()] * (5 + len(parts)) + [anywhere()] * len(after),
        out_specs=[whole_vmem()] * 2,
        scratch_shapes=[
            pltpu.VMEM((total_keys, key_dim), bf16),
            pltpu.VMEM((total_keys, value_dim), bf16),
        ],
        compiler_params=pltpu.CompilerParams(
            vmem_limit_bytes=8 * MIB if total_keys <= 1024 else 32 * MIB
        ),
    )(scale, encoded, gain, query_weight, start, output_weight, *parts, *after)


def unpack_kernel(chips, pairs, rows, width, *refs):
    message_refs = refs[:chips][::-1]
    out_ref = refs[-1]
    dim = out_ref.shape[2]
    padded = message_refs[0].shape[1]
    for k in range(chips):
        spare = dim * SPARE_ROWS // rows
        first = jnp.concatenate(
            [
                message_refs[k][
                    g * SPARE_ROWS : (g + 1) * SPARE_ROWS, width + 8 : width + 8 + spare
                ]
                for g in range(dim // spare)
            ],
            axis=1,
        )
        piece = message_refs[k][rows:, :]
        piece = [piece[:, g : g + dim] for g in range(0, padded, dim)]
        piece = jnp.concatenate([first] + piece, axis=0)
        piece = piece[: 2 * pairs * pairs].reshape(pairs, 2 * pairs, dim)
        out_ref[k * pairs : (k + 1) * pairs] = piece


def unpack_pairs(messages, pairs, dim, rows, width, after):
    chips = len(messages)
    return pl.pallas_call(
        functools.partial(unpack_kernel, chips, pairs, rows, width),
        name="unpack_pairs",
        out_shape=array((chips * pairs, 2 * pairs, dim), bf16),
        in_specs=[whole_vmem()] * chips + [anywhere()] * len(after),
        out_specs=whole_vmem(),
        compiler_params=pltpu.CompilerParams(vmem_limit_bytes=4 * MIB),
    )(*messages[::-1], *after)


def pair_kernel(
    chips, columns_used, input_ref, cotangent_ref, other_cotangent_ref, flip_ref, turned_ref, other_ref, *rest
):
    bundle_refs = rest[:chips]
    out_ref, grad_ref, stacked, mirror, summed, flipped, cotangent = rest[-7:]
    rows, columns, dim = input_ref.shape
    parts = 2 * chips
    wide = 2 * rows
    chip, core = here()
    me = chip * 2 + core
    for k in range(chips):
        got = bundle_refs[k][:, columns_used:].astype(f32)
        count = 2 * dim // got.shape[1]
        for f in range(2):
            at = f * count * rows
            stacked[2 * k + f] = jnp.concatenate(
                [got[at + g * rows : at + (g + 1) * rows] for g in range(count)], axis=1
            )
    own, other = stacked[0], stacked[1]
    both_k = jnp.concatenate(
        [jnp.where(core == 0, own, other), jnp.where(core == 0, other, own)], axis=0
    )[:, dim:][None]
    for k in range(parts):
        source = turned_ref if k % 2 == 0 else other_ref
        value = source[k // 2 * rows : (k // 2 + 1) * rows].astype(f32)
        value = value + stacked[k][:, None, :dim] * both_k
        mirror[k] = value.reshape(rows * wide, dim).astype(bf16)
    target = lax.broadcasted_iota(jnp.int32, (rows * wide, rows * wide), 0)
    origin = lax.broadcasted_iota(jnp.int32, (rows * wide, rows * wide), 1)
    swap = jnp.where(origin == (target % rows) * wide + target // rows, 1.0, 0.0).astype(bf16)
    for b in range(parts):
        turned = jnp.dot(swap, mirror[b ^ me], preferred_element_type=f32)
        flipped[:, b * rows : (b + 1) * rows, :] = turned.reshape(wide, rows, dim)
    every = jnp.concatenate([stacked[b ^ me] for b in range(parts)], axis=0)[:, dim:]
    for i in range(rows):
        at = pl.ds(i * columns, columns)
        value = input_ref[i].astype(f32) + own[i : i + 1, :dim] * every
        summed[at, :] = value.astype(bf16)
    facing = flipped[pl.ds(core * rows, rows)].reshape(rows * columns, dim).astype(bf16)
    update = jnp.dot(facing, flip_ref[...], preferred_element_type=f32)
    update = update + summed[...].astype(f32)
    out_ref[...] = update.astype(bf16).reshape(rows, columns, dim)
    cotangent[pl.ds(core * rows, rows)] = cotangent_ref[...]
    cotangent[pl.ds((1 - core) * rows, rows)] = other_cotangent_ref[...]
    grad = lax.dot_general(
        flipped[...].reshape(wide * columns, dim).astype(bf16),
        cotangent[...].reshape(wide * columns, dim),
        (((0,), (0,)), ((), ())),
        preferred_element_type=f32,
    )
    grad_ref[...] = grad.astype(bf16)


def pair_update(pair_input, cotangents, flip_weight, turned, bundles, columns_used):
    rows, columns, dim = pair_input.shape
    chips = len(bundles)
    return pl.pallas_call(
        functools.partial(pair_kernel, chips, columns_used),
        name="pair",
        out_shape=[array((rows, columns, dim), bf16), array((dim, dim), bf16)],
        in_specs=[whole_vmem()] * (6 + chips),
        out_specs=[whole_vmem()] * 2,
        scratch_shapes=[
            pltpu.VMEM((2 * chips, rows, 2 * dim), f32),
            pltpu.VMEM((2 * chips, 2 * rows * rows, dim), bf16),
            pltpu.VMEM((rows * columns, dim), bf16),
            pltpu.VMEM((2 * rows, columns, dim), f32),
            pltpu.VMEM((2 * rows, columns, dim), bf16),
        ],
        compiler_params=pltpu.CompilerParams(
            vmem_limit_bytes=6 * MIB if chips <= 4 else 32 * MIB
        ),
    )(pair_input, *cotangents, flip_weight, *turned, *bundles)


def per_device(
    features,
    conv_weight,
    norm_gain,
    query_weight,
    keyval_weight,
    head_scale,
    output_weight,
    pair_weight,
    pair_input,
    flip_weight,
    pair_cotangent,
):
    chips = lax.axis_size("seq")
    bits = chips.bit_length() - 1
    windows = lax.axis_size("dp")
    taps = conv_weight.shape[0]
    model_dim = output_weight.shape[1]
    heads = head_scale.shape[0]
    features = features[0]

    masks = [(k, flipped_bits(k, bits)) for k in range(chips)]

    def send(value, mask, flip=0):
        cores = mask if isinstance(mask, tuple) else (mask, mask)
        return lax.ppermute(value, GROUP, hop_pairs(chips, cores, flip))

    rows, channels = features.shape
    width = channels // chips
    own_weight = conv_weight.reshape(-1, model_dim)
    peer_weight = send(own_weight, 0, 1)
    blocks = prep(features, pair_input[0], chips)

    messages = [blocks[0]] + [None] * (chips - 1)
    for k in range(chips - 1, 0, -1):
        messages[k] = send(blocks[k], k)
    weight = pack_filter(own_weight, peer_weight, taps, blocks[0].shape[1])
    cotangent, weight = lax.optimization_barrier((pair_cotangent[0], weight))
    cotangents = (pair_cotangent[0], send(cotangent, 0, 1))

    last = chips - 1
    rest = sorted(range(last), key=lambda k: (1 - (k & 1), -k))

    prepared = {}

    def active(k, wait):
        if k not in prepared:
            sources = [messages[j] for j in dict.fromkeys(masks[k])]
            prepared[k] = activate(sources, width, rows, wait)
        return prepared[k]

    def partials(ks, columns, edges, after, wait):
        dtypes = [bf16 if k & 1 else f32 for k in ks]
        blocks = [active(k, wait) for k in ks]
        got = conv(blocks, edges, features, weight, taps, ks, dtypes, columns, after)
        return dict(zip(ks, got))

    columns = [(0, model_dim // 2), (model_dim // 2, model_dim)]
    partial = partials([last], columns[:1], None, [], [])
    partial[last] += partials([last], columns[1:], None, [cotangents[1]], [])[last]
    edges = send(edge_rows(messages, width, rows, partial[last]), 0, 1)
    arrivals = [messages[k] for k in range(1, last)]
    partial[last] = [lax.optimization_barrier((v, *arrivals))[0] for v in partial[last]]
    pairs, _, pair_dim = pair_input.shape[1:]
    turned = unpack_pairs(
        messages, pairs, pair_dim, rows, width, partial[last]
    )
    turned = (turned, send(turned, 0, 1))
    odd = [k for k in rest if k & 1]
    even = [k for k in rest if k and not k & 1]
    partial.update(partials(odd, columns, edges, [turned[1]], partial[last]))
    own_terms = edge_terms(edges, weight, taps, partial[1])
    terms = send(own_terms, last)
    for ks in (even, [0]):
        partial.update(partials(ks, columns, edges, [turned[1]], [own_terms]))
    arrived = []
    for b in range(bits):
        bit = 1 << b
        leaving = [k for k in [last] + rest if k in partial and k & bit]
        got = {k ^ bit: [send(v, masks[bit]) for v in partial.pop(k)] for k in leaving}
        for k, values in got.items():
            if k == 0:
                arrived.append(values)
            else:
                dtype = bf16 if k & (2 * bit) else f32
                partial[k] = [
                    add_up([p, v], dtype, [turned[1]]) for p, v in zip(partial[k], values)
                ]

    encoded, feats = encode(partial[0], arrived, terms, pair_weight, [])
    keyval = project_keyvals(encoded, norm_gain, keyval_weight.T)
    own_bundle = bundle(keyval, feats, send(feats, 0, 1))
    bundles = [own_bundle] + [send(own_bundle, k) for k in range(1, chips)]
    pair_out, grad = pair_update(
        pair_input[0], cotangents, flip_weight, turned, bundles, keyval_weight.shape[1]
    )
    keyvals = bundles + [send(v, 0, 1) for v in bundles]

    def attend_heads(start, first, end, dtype, after):
        return attend(
            encoded,
            norm_gain,
            query_weight,
            head_scale,
            start,
            output_weight,
            keyvals,
            first,
            end,
            dtype,
            after,
        )

    halfway = heads // 2
    first_half, done = attend_heads(encoded, 0, halfway, f32, [])
    grad = add_up([grad] + [send(grad, k) for k in range(1, chips)], bf16, [done])
    block_out, done = attend_heads(first_half, halfway, heads, bf16, [grad])
    planes = [
        lax.ppermute(grad, "dp", [(w, w ^ k) for w in range(windows)])
        for k in range(windows - 1, 0, -1)
    ]
    grad = add_up([grad] + planes[::-1], f32, [done], backwards=True)
    return (block_out[None], pair_out[None], grad)


def solution(mesh):
    placed = (
        P("dp", ("seq", "mp"), None),
        P(None, ("seq", "mp"), None),
        P(),
        P(),
        P(),
        P(),
        P(),
        P(),
        P("dp", ("seq", "mp"), None, None),
        P(),
        P("dp", ("seq", "mp"), None, None),
    )
    return jax.shard_map(
        per_device,
        mesh=mesh,
        in_specs=placed,
        out_specs=(P("dp", ("seq", "mp"), None), P("dp", ("seq", "mp"), None, None), P()),
        check_vma=False,
    )
```

```python
import functools
import math

import jax
import jax.numpy as jnp
from jax import lax
from jax.experimental import pallas as pl
from jax.experimental.pallas import tpu as pltpu
from jax.sharding import PartitionSpec as P

PAIR_POOL = 16
SPARE_ROWS = 32
norm_eps = 1e-06
logit_cap = 50.0
MIB = 1 << 20
GROUP = ("seq", "mp")
f32, bf16 = jnp.float32, jnp.bfloat16


def whole_vmem():
    return pl.BlockSpec(memory_space=pltpu.VMEM)


def anywhere():
    return pl.BlockSpec(memory_space=pl.ANY)


def smem():
    return pl.BlockSpec(memory_space=pltpu.SMEM)


def in_hbm(value):
    return pltpu.with_memory_space_constraint(value, pltpu.HBM)


def array(shape, dtype):
    return jax.ShapeDtypeStruct(shape, dtype)


def lane_pad(width):
    return (width + 127) // 128 * 128


def tree_sum(terms):
    while len(terms) > 1:
        terms = [terms[i] + terms[i + 1] for i in range(0, len(terms), 2)]
    return terms[0]


def flipped_bits(mask, bits):
    return sum(((mask >> b) & 1) << (bits - 1 - b) for b in range(bits))


def here():
    return lax.axis_index("seq"), lax.axis_index("mp")


def hop_pairs(chips, core_masks, core_flip):
    pairs = []
    for chip in range(chips):
        for core in range(2):
            target = (chip ^ core_masks[core]) * 2 + (core ^ core_flip)
            pairs.append((chip * 2 + core, target))
    return pairs


def pick_rows(rows):
    half = rows // 2
    target = lax.broadcasted_iota(jnp.int32, (rows, rows), 0)
    source = lax.broadcasted_iota(jnp.int32, (rows, rows), 1)
    wanted = jnp.where(target < half, 2 * target, 2 * (target - half) + 1)
    return jnp.where(source == wanted, 1.0, 0.0).astype(bf16)


def prep_kernel(chips, width, feat_hbm, pair_hbm, *rest):
    block_refs = rest[:chips]
    feat, pair, split, sems = rest[chips:]
    rows = feat.shape[0]
    chip, _ = here()
    chunks = sems.shape[0] - 1
    step = rows // chunks

    def copy(n):
        at = pl.ds(n * step, step)
        return pltpu.make_async_copy(feat_hbm.at[at, :], feat.at[at, :], sems.at[n])

    pair_copy = pltpu.make_async_copy(pair_hbm, pair, sems.at[chunks])
    for n in range(chunks):
        copy(n).start()
    pair_copy.start()
    for n in range(chunks):
        copy(n).wait()
        fill_rows(chips, width, n * step, step, feat, split)
    pair_copy.wait()
    pairs, _, dim = pair.shape
    lanes = split.shape[2] // dim
    extra = block_refs[0].shape[0] - rows
    spare = dim * SPARE_ROWS // rows
    for k in range(chips):
        at = pl.ds(pl.multiple_of((chip ^ k) * 2 * pairs, 16), 2 * pairs)
        piece = pair[:, at, :].reshape(2 * pairs * pairs, dim)
        block_refs[k][0:rows, :] = split[chip ^ k]
        for g in range(dim // spare):
            block_refs[k][
                g * SPARE_ROWS : (g + 1) * SPARE_ROWS, width + 8 : width + 8 + spare
            ] = piece[:SPARE_ROWS, g * spare : (g + 1) * spare]
        for g in range(lanes):
            part = piece[SPARE_ROWS + g * extra : SPARE_ROWS + (g + 1) * extra]
            block_refs[k][rows : rows + part.shape[0], g * dim : (g + 1) * dim] = part


def fill_rows(chips, width, start, step, feat, split):
    at = slice(start, start + step)
    x = feat[at, :].astype(f32)
    scale = lax.rsqrt(jnp.mean(x * x, axis=-1, keepdims=True) + norm_eps)
    high = scale.astype(bf16)
    middle = (scale - high.astype(f32)).astype(bf16)
    low = (scale - high.astype(f32) - middle.astype(f32)).astype(bf16)
    lane = lax.broadcasted_iota(jnp.int32, (step, split.shape[2] - width), 1)
    tail = jnp.where(
        lane == 0,
        high.astype(f32),
        jnp.where(
            lane == 1, middle.astype(f32), jnp.where(lane == 2, low.astype(f32), 0.0)
        ),
    ).astype(bf16)
    for q in range(chips):
        split[q, at, 0:width] = feat[at, q * width : (q + 1) * width]
        split[q, at, width:] = tail


def prep(features, pair_input, chips):
    rows, channels = features.shape
    width = channels // chips
    padded = lane_pad(width)
    pairs, _, dim = pair_input.shape
    extra = -(-(2 * pairs * pairs - SPARE_ROWS) // (16 * (padded // dim))) * 16
    return pl.pallas_call(
        functools.partial(prep_kernel, chips, width),
        name="prep",
        out_shape=[array((rows + extra, padded), bf16)] * chips,
        in_specs=[anywhere()] * 2,
        out_specs=[whole_vmem()] * chips,
        scratch_shapes=[
            pltpu.VMEM((rows, channels), bf16),
            pltpu.VMEM(pair_input.shape, bf16),
            pltpu.VMEM((chips, rows, padded), bf16),
            pltpu.SemaphoreType.DMA((2,)),
        ],
        compiler_params=pltpu.CompilerParams(vmem_limit_bytes=10 * MIB),
    )(in_hbm(features), in_hbm(pair_input))


def gelu_of(block, width):
    scale = block[:, width : width + 1] + block[:, width + 1 : width + 2]
    scale = scale + block[:, width + 2 : width + 3]
    v = block * scale
    g = (0.5 * v) * (1.0 + lax.erf(v * math.sqrt(0.5)))
    lane = lax.broadcasted_iota(jnp.int32, block.shape, 1)
    return jnp.where(lane < width, g, 0.0)


def edges_kernel(chips, width, rows, *refs):
    message_refs = refs[:chips][::-1]
    out_ref = refs[-1]
    strips = []
    for ref in message_refs:
        for start, row in ((0, 0), (0, 1), (rows - 16, 14), (rows - 16, 15)):
            strips.append(ref[start : start + 16, :].astype(f32)[row : row + 1])
    prepared = gelu_of(jnp.concatenate(strips, axis=0), width)
    for k in range(chips):
        out_ref[k, 0:4] = prepared[4 * k : 4 * k + 4]
        out_ref[k, 4:8] = jnp.zeros((4, prepared.shape[1]), f32)


def edge_rows(messages, width, rows, after):
    chips = len(messages)
    padded = messages[0].shape[1]
    return pl.pallas_call(
        functools.partial(edges_kernel, chips, width, rows),
        name="edge_rows",
        out_shape=array((chips, 8, padded), f32),
        in_specs=[whole_vmem()] * chips + [anywhere()] * len(after),
        out_specs=whole_vmem(),
        compiler_params=pltpu.CompilerParams(vmem_limit_bytes=2 * MIB),
    )(*messages[::-1], *after)


def activate_kernel(width, count, *refs):
    message_refs, out_ref, wide = refs[:count], refs[-2], refs[-1]
    _, core = here()
    step = 32
    rows = out_ref.shape[0]
    pick = pick_rows(rows)
    if count == 1:
        wide[...] = jnp.dot(pick, message_refs[0][0:rows, :], preferred_element_type=f32)
    else:

        @pl.when(core == 0)
        def _():
            wide[...] = jnp.dot(pick, message_refs[0][0:rows, :], preferred_element_type=f32)

        @pl.when(core != 0)
        def _():
            wide[...] = jnp.dot(pick, message_refs[1][0:rows, :], preferred_element_type=f32)

    def body(i, carry):
        at = pl.ds(pl.multiple_of(i * step, step), step)
        out_ref[at, :] = gelu_of(wide[at, :], width).astype(bf16)
        return carry

    lax.fori_loop(0, out_ref.shape[0] // step, body, 0)


def activate(messages, width, rows, after):
    return pl.pallas_call(
        functools.partial(activate_kernel, width, len(messages)),
        name="activate",
        out_shape=array((rows, messages[0].shape[1]), bf16),
        in_specs=[whole_vmem()] * len(messages) + [anywhere()] * len(after),
        out_specs=whole_vmem(),
        scratch_shapes=[pltpu.VMEM((rows, messages[0].shape[1]), f32)],
        compiler_params=pltpu.CompilerParams(vmem_limit_bytes=3 * MIB),
    )(*messages, *after)


def pack_kernel(taps, padded, own_hbm, peer_hbm, out_ref, sems):
    part = own_hbm.shape[0] // taps
    _, core = here()
    copies = []
    for p, source in enumerate((own_hbm, peer_hbm)):
        place = core if p == 0 else 1 - core
        for k in range(taps):
            to = pl.ds(pl.multiple_of(k * padded + place * part, 16), part)
            copies.append(
                pltpu.make_async_copy(
                    source.at[k * part : (k + 1) * part, :], out_ref.at[to, :], sems.at[p, k]
                )
            )
    for c in copies:
        c.start()
    if padded > 2 * part:
        for k in range(taps):
            out_ref[k * padded + 2 * part : (k + 1) * padded, :] = jnp.zeros(
                (padded - 2 * part, out_ref.shape[1]), bf16
            )
    for c in copies:
        c.wait()


def pack_filter(own, peer, taps, padded):
    model_dim = own.shape[1]
    part = own.shape[0] // taps
    if part % 16:
        own, peer = (w.reshape(taps, part, model_dim) for w in (own, peer))
        first = lax.axis_index("mp") == 0
        low, high = jnp.where(first, own, peer), jnp.where(first, peer, own)
        both = jnp.concatenate([low, high], axis=1)
        both = jnp.pad(both, ((0, 0), (0, padded - 2 * part), (0, 0)))
        return both.reshape(taps * padded, model_dim)
    return pl.pallas_call(
        functools.partial(pack_kernel, taps, padded),
        name="pack_filter",
        out_shape=array((taps * padded, model_dim), bf16),
        in_specs=[anywhere()] * 2,
        out_specs=whole_vmem(),
        scratch_shapes=[pltpu.SemaphoreType.DMA((2, taps))],
        compiler_params=pltpu.CompilerParams(vmem_limit_bytes=2 * MIB),
    )(in_hbm(own), peer)


def conv_kernel(
    chips, bits, taps, tile, wanted, columns, outs, edged, feat_hbm, edge_ref, *rest
):
    count = len(wanted)
    block_refs = rest[:count]
    weight_ref = rest[count]
    cols, feat, sem = rest[-3:]
    out_refs = rest[-3 - outs : -3]
    rows, padded = block_refs[0].shape
    half = rows // 2
    chip, core = here()
    if 0 in wanted:
        copy = pltpu.make_async_copy(feat_hbm, feat, sem)
        copy.start()
    row = lax.broadcasted_iota(jnp.int32, (half, padded), 0)
    for j, k in enumerate(wanted):
        mask = jnp.where(core == 0, k, flipped_bits(k, bits))
        left = (chip ^ mask) - (1 - core)
        right = (chip ^ mask) + core
        block = block_refs[j][...]
        if edged:
            before = edge_ref[jnp.where(left >= 0, left ^ chip, 0)]
            before = jnp.where(left >= 0, before, 0.0)
            after = edge_ref[jnp.where(right < chips, right ^ chip, 0)]
            after = jnp.where(right < chips, after, 0.0)
        else:
            before = after = jnp.zeros((8, padded), f32)
        even = block[0:half].astype(f32)
        odd = block[half:rows].astype(f32)

        def back(v, strip_row):
            return jnp.where(row == 0, before[strip_row : strip_row + 1], pltpu.roll(v, 1, 0))

        def ahead(v, strip_row):
            return jnp.where(
                row == half - 1, after[strip_row : strip_row + 1], pltpu.roll(v, half - 1, 0)
            )

        lagged = [back(even, 2), back(odd, 3), even, odd, ahead(even, 0), ahead(odd, 1)]
        for i, v in enumerate(lagged):
            piece = v.astype(bf16)
            if i < taps:
                cols[j * rows : j * rows + half, i * padded : (i + 1) * padded] = piece
            if i > 0:
                cols[j * rows + half : (j + 1) * rows, (i - 1) * padded : i * padded] = piece
    pick = pick_rows(rows)
    if 0 in wanted:
        copy.wait()
    for j, k in enumerate(wanted):
        for h, (first, last) in enumerate(columns):
            out_ref = out_refs[j * len(columns) + h]
            for at in range(first, last, tile):
                got = jnp.dot(
                    cols[j * rows : (j + 1) * rows],
                    weight_ref[:, at : at + tile],
                    preferred_element_type=f32,
                )
                if k == 0 and at < feat.shape[1]:
                    width = min(tile, feat.shape[1] - at)
                    skip = jnp.dot(
                        pick, feat[:, at : at + width], preferred_element_type=f32
                    )
                    if width < tile:
                        skip = jnp.concatenate(
                            [skip, jnp.zeros((rows, tile - width), f32)], axis=1
                        )
                    got = got + skip
                out_ref[:, at - first : at - first + tile] = got.astype(out_ref.dtype)


def edge_terms_kernel(chips, taps, edge_ref, weight_ref, *rest):
    out_ref, cols = rest[-2:]
    padded = edge_ref.shape[2]
    chip, core = here()
    left = (chip ^ (chips - 1)) - (1 - core)
    right = (chip ^ (chips - 1)) + core
    before = edge_ref[jnp.where(left >= 0, left ^ chip, 0)]
    before = jnp.where(left >= 0, before, 0.0)
    after = edge_ref[jnp.where(right < chips, right ^ chip, 0)]
    after = jnp.where(right < chips, after, 0.0)
    none = jnp.zeros((1, padded), f32)
    blank = jnp.zeros((12, padded), f32)
    terms = {
        0: (before[2:3], before[3:4], none, none),
        1: (before[3:4], none, none, none),
        3: (none, none, none, after[0:1]),
        4: (none, none, after[0:1], after[1:2]),
    }
    for k in range(taps):
        rows = terms.get(k, (none,) * 4)
        cols[:, k * padded : (k + 1) * padded] = jnp.concatenate(
            [*rows, blank], axis=0
        ).astype(bf16)
    span = out_ref.shape[1]
    quarters = [
        jnp.dot(cols[...], weight_ref[:, at : at + span], preferred_element_type=f32)[0:4]
        for at in range(0, 4 * span, span)
    ]
    out_ref[...] = jnp.concatenate(quarters, axis=0).astype(bf16)


def edge_terms(edges, weight, taps, after):
    chips = edges.shape[0]
    depth, model_dim = weight.shape
    return pl.pallas_call(
        functools.partial(edge_terms_kernel, chips, taps),
        name="edge_terms",
        out_shape=array((16, model_dim // 4), bf16),
        in_specs=[whole_vmem()] * 2 + [anywhere()] * len(after),
        out_specs=whole_vmem(),
        scratch_shapes=[pltpu.VMEM((16, depth), bf16)],
        compiler_params=pltpu.CompilerParams(vmem_limit_bytes=2 * MIB),
    )(edges, weight, *after)


def conv(blocks, edges, features, weight, taps, wanted, dtypes, columns, after):
    chips = lax.axis_size("seq")
    bits = chips.bit_length() - 1
    rows = features.shape[0]
    edged = edges is not None
    depth, model_dim = weight.shape
    count = len(wanted)
    pieces = len(columns)
    got = pl.pallas_call(
        functools.partial(
            conv_kernel, chips, bits, taps, 256, wanted, columns, count * pieces, edged
        ),
        name="conv",
        out_shape=[array((rows, b - a), d) for d in dtypes for a, b in columns],
        in_specs=[anywhere()] + [whole_vmem()] * (count + 2) + [anywhere()] * len(after),
        out_specs=[whole_vmem()] * (count * pieces),
        scratch_shapes=[
            pltpu.VMEM((count * rows, depth), bf16),
            pltpu.VMEM(features.shape, bf16),
            pltpu.SemaphoreType.DMA,
        ],
        compiler_params=pltpu.CompilerParams(vmem_limit_bytes=(5 + 2 * count) * MIB),
    )(in_hbm(features), edges if edged else blocks[0], *blocks, weight, *after)
    return [got[j * pieces : (j + 1) * pieces] for j in range(count)]


def sum_kernel(count, backwards, *refs):
    out_ref = refs[-1]
    terms = [r[...].astype(f32) for r in refs[:count]]
    out_ref[...] = tree_sum(terms[::-1] if backwards else terms).astype(out_ref.dtype)


def add_up(terms, dtype, after=(), backwards=False):
    terms = terms[::-1] if backwards else terms
    return pl.pallas_call(
        functools.partial(sum_kernel, len(terms), backwards),
        name="add_up",
        out_shape=array(terms[0].shape, dtype),
        in_specs=[whole_vmem()] * len(terms) + [anywhere()] * len(after),
        out_specs=whole_vmem(),
        compiler_params=pltpu.CompilerParams(vmem_limit_bytes=4 * MIB),
    )(*terms, *after)


def encode_kernel(pieces, arrivals, pair_weight_ref, term_ref, *rest):
    own_refs = rest[:pieces]
    come_refs = rest[pieces : pieces + arrivals * pieces]
    encoded_ref, feats_ref = rest[-2:]
    rows = own_refs[0].shape[0]
    half = rows // 2
    pairs = half // PAIR_POOL
    at = lax.broadcasted_iota(jnp.int32, (pairs, half), 0)
    of = lax.broadcasted_iota(jnp.int32, (pairs, half), 1) // PAIR_POOL
    spread = jnp.where(at == of, 1.0 / PAIR_POOL, 0.0).astype(bf16)
    feats = jnp.zeros(feats_ref.shape, f32)
    quarters = term_ref[...].astype(f32)
    all_terms = jnp.concatenate([quarters[q : q + 4] for q in range(0, 16, 4)], axis=1)
    first = 0
    for h in range(pieces):
        last = first + own_refs[h].shape[1]
        total = own_refs[h][...]
        for a in range(arrivals):
            total = total + come_refs[a * pieces + h][...].astype(f32)
        terms = all_terms[:, first:last]
        row = lax.broadcasted_iota(jnp.int32, (half, last - first), 0)
        even, odd = (
            part
            + jnp.where(row == 0, terms[i : i + 1], 0.0)
            + jnp.where(row == half - 1, terms[i + 2 : i + 3], 0.0)
            for i, part in enumerate((total[:half], total[half:]))
        )
        encoded = jnp.maximum(even, odd).astype(bf16)
        encoded_ref[:, first:last] = encoded
        pooled = jnp.dot(spread, encoded, preferred_element_type=f32).astype(bf16)
        feats = feats + jnp.dot(
            pooled, pair_weight_ref[first:last, :], preferred_element_type=f32
        )
        first = last
    feats_ref[...] = feats.astype(bf16).astype(f32)


def encode(own, come, terms, pair_weight, after):
    rows = own[0].shape[0]
    pieces = len(own)
    half = rows // 2
    return pl.pallas_call(
        functools.partial(encode_kernel, pieces, len(come)),
        name="encode",
        out_shape=[
            array((half, sum(v.shape[1] for v in own)), bf16),
            array((half // PAIR_POOL, pair_weight.shape[1]), f32),
        ],
        in_specs=[whole_vmem()] * (2 + pieces * (1 + len(come))) + [anywhere()] * len(after),
        out_specs=[whole_vmem()] * 2,
        compiler_params=pltpu.CompilerParams(vmem_limit_bytes=8 * MIB),
    )(pair_weight, terms, *own, *sum(come, []), *after)


def normalised(encoded_ref, gain_ref):
    wide = encoded_ref[...].astype(f32)
    scale = lax.rsqrt(jnp.mean(wide * wide, axis=-1, keepdims=True) + norm_eps)
    return (wide * scale * gain_ref[...][None]).astype(bf16)


def keyval_kernel(encoded_ref, gain_ref, weight_ref, out_ref):
    out_ref[...] = lax.dot_general(
        normalised(encoded_ref, gain_ref),
        weight_ref[...],
        (((1,), (1,)), ((), ())),
        preferred_element_type=f32,
    ).astype(bf16)


def project_keyvals(encoded, gain, weight_t):
    return pl.pallas_call(
        keyval_kernel,
        name="keyvals",
        out_shape=array((encoded.shape[0], weight_t.shape[0]), bf16),
        in_specs=[whole_vmem()] * 3,
        out_specs=whole_vmem(),
        compiler_params=pltpu.CompilerParams(vmem_limit_bytes=4 * MIB),
    )(encoded, gain, weight_t)


def bundle_kernel(keyval_ref, mine_ref, other_ref, out_ref):
    rows, columns = keyval_ref.shape
    spare = out_ref.shape[1] - columns
    pieces = []
    for ref in (mine_ref, other_ref):
        feats = ref[...]
        pieces += [feats[:, g : g + spare] for g in range(0, feats.shape[1], spare)]
    used = sum(p.shape[0] for p in pieces)
    pieces.append(jnp.zeros((rows - used, spare), f32))
    out_ref[:, :columns] = keyval_ref[...]
    out_ref[:, columns:] = jnp.concatenate(pieces, axis=0).astype(bf16)


def bundle(keyval, mine, other):
    return pl.pallas_call(
        bundle_kernel,
        name="bundle",
        out_shape=array((keyval.shape[0], lane_pad(keyval.shape[1])), bf16),
        in_specs=[whole_vmem()] * 3,
        out_specs=whole_vmem(),
        compiler_params=pltpu.CompilerParams(vmem_limit_bytes=4 * MIB),
    )(keyval, mine, other)


def attend_kernel(
    parts,
    heads,
    first,
    last,
    group,
    scale_ref,
    encoded_ref,
    gain_ref,
    query_weight_ref,
    start_ref,
    weight_ref,
    *rest,
):
    part_refs = rest[:parts]
    out_ref, done_ref, keys, values = rest[-4:]
    rows = encoded_ref.shape[0]
    key_dim = query_weight_ref.shape[1] // heads
    normed = normalised(encoded_ref, gain_ref)
    span = part_refs[0].shape[0]
    value_dim = values.shape[1]
    for k in range(parts):
        got = part_refs[k][...]
        keys[k * span : (k + 1) * span, :] = got[:, :key_dim]
        values[k * span : (k + 1) * span, :] = got[:, key_dim : key_dim + value_dim]
    total = start_ref[...].astype(f32)
    for n in range(first, last, group):
        got = jnp.dot(
            normed,
            query_weight_ref[:, n * key_dim : (n + group) * key_dim],
            preferred_element_type=f32,
        )
        queries = jnp.concatenate(
            [
                got[:, h * key_dim : (h + 1) * key_dim]
                * (scale_ref[n + h] / math.sqrt(key_dim))
                for h in range(group)
            ],
            axis=0,
        ).astype(bf16)
        scores = lax.dot_general(
            queries, keys[...], (((1,), (1,)), ((), ())), preferred_element_type=f32
        )
        weights = jnp.exp(logit_cap * jnp.tanh(scores * (1.0 / logit_cap)))
        sums = jnp.sum(weights, axis=-1, keepdims=True)
        mixed = jnp.dot(weights.astype(bf16), values[...], preferred_element_type=f32) / sums
        mixed = mixed.astype(bf16)
        for h in range(group):
            at = (n + h) * value_dim
            total = total + jnp.dot(
                mixed[h * rows : (h + 1) * rows],
                weight_ref[at : at + value_dim, :],
                preferred_element_type=f32,
            )
    out_ref[...] = total.astype(out_ref.dtype)
    done_ref[...] = total[0:8, 0:128]


def attend(
    encoded, gain, query_weight, scale, start, output_weight, parts, first, last, dtype, after
):
    rows, model_dim = start.shape
    heads = scale.shape[0]
    key_dim = query_weight.shape[1] // heads
    value_dim = output_weight.shape[0] // heads
    total_keys = parts[0].shape[0] * len(parts)
    group = 2
    return pl.pallas_call(
        functools.partial(attend_kernel, len(parts), heads, first, last, group),
        name="attend",
        out_shape=[array((rows, model_dim), dtype), array((8, 128), f32)],
        in_specs=[smem()] + [whole_vmem()] * (5 + len(parts)) + [anywhere()] * len(after),
        out_specs=[whole_vmem()] * 2,
        scratch_shapes=[
            pltpu.VMEM((total_keys, key_dim), bf16),
            pltpu.VMEM((total_keys, value_dim), bf16),
        ],
        compiler_params=pltpu.CompilerParams(
            vmem_limit_bytes=8 * MIB if total_keys <= 1024 else 32 * MIB
        ),
    )(scale, encoded, gain, query_weight, start, output_weight, *parts, *after)


def unpack_kernel(chips, pairs, rows, width, *refs):
    message_refs = refs[:chips][::-1]
    out_ref = refs[-1]
    dim = out_ref.shape[2]
    padded = message_refs[0].shape[1]
    for k in range(chips):
        spare = dim * SPARE_ROWS // rows
        first = jnp.concatenate(
            [
                message_refs[k][
                    g * SPARE_ROWS : (g + 1) * SPARE_ROWS, width + 8 : width + 8 + spare
                ]
                for g in range(dim // spare)
            ],
            axis=1,
        )
        piece = message_refs[k][rows:, :]
        piece = [piece[:, g : g + dim] for g in range(0, padded, dim)]
        piece = jnp.concatenate([first] + piece, axis=0)
        piece = piece[: 2 * pairs * pairs].reshape(pairs, 2 * pairs, dim)
        out_ref[k * pairs : (k + 1) * pairs] = piece


def unpack_pairs(messages, pairs, dim, rows, width, after):
    chips = len(messages)
    return pl.pallas_call(
        functools.partial(unpack_kernel, chips, pairs, rows, width),
        name="unpack_pairs",
        out_shape=array((chips * pairs, 2 * pairs, dim), bf16),
        in_specs=[whole_vmem()] * chips + [anywhere()] * len(after),
        out_specs=whole_vmem(),
        compiler_params=pltpu.CompilerParams(vmem_limit_bytes=4 * MIB),
    )(*messages[::-1], *after)


def pair_kernel(
    chips, columns_used, input_ref, cotangent_ref, other_cotangent_ref, flip_ref, turned_ref, other_ref, *rest
):
    bundle_refs = rest[:chips]
    out_ref, grad_ref, stacked, mirror, summed, flipped, cotangent = rest[-7:]
    rows, columns, dim = input_ref.shape
    parts = 2 * chips
    wide = 2 * rows
    chip, core = here()
    me = chip * 2 + core
    for k in range(chips):
        got = bundle_refs[k][:, columns_used:].astype(f32)
        count = 2 * dim // got.shape[1]
        for f in range(2):
            at = f * count * rows
            stacked[2 * k + f] = jnp.concatenate(
                [got[at + g * rows : at + (g + 1) * rows] for g in range(count)], axis=1
            )
    own, other = stacked[0], stacked[1]
    both_k = jnp.concatenate(
        [jnp.where(core == 0, own, other), jnp.where(core == 0, other, own)], axis=0
    )[:, dim:][None]
    for k in range(parts):
        source = turned_ref if k % 2 == 0 else other_ref
        value = source[k // 2 * rows : (k // 2 + 1) * rows].astype(f32)
        value = value + stacked[k][:, None, :dim] * both_k
        mirror[k] = value.reshape(rows * wide, dim).astype(bf16)
    target = lax.broadcasted_iota(jnp.int32, (rows * wide, rows * wide), 0)
    origin = lax.broadcasted_iota(jnp.int32, (rows * wide, rows * wide), 1)
    swap = jnp.where(origin == (target % rows) * wide + target // rows, 1.0, 0.0).astype(bf16)
    for b in range(parts):
        turned = jnp.dot(swap, mirror[b ^ me], preferred_element_type=f32)
        flipped[:, b * rows : (b + 1) * rows, :] = turned.reshape(wide, rows, dim)
    every = jnp.concatenate([stacked[b ^ me] for b in range(parts)], axis=0)[:, dim:]
    for i in range(rows):
        at = pl.ds(i * columns, columns)
        value = input_ref[i].astype(f32) + own[i : i + 1, :dim] * every
        summed[at, :] = value.astype(bf16)
    facing = flipped[pl.ds(core * rows, rows)].reshape(rows * columns, dim).astype(bf16)
    update = jnp.dot(facing, flip_ref[...], preferred_element_type=f32)
    update = update + summed[...].astype(f32)
    out_ref[...] = update.astype(bf16).reshape(rows, columns, dim)
    cotangent[pl.ds(core * rows, rows)] = cotangent_ref[...]
    cotangent[pl.ds((1 - core) * rows, rows)] = other_cotangent_ref[...]
    grad = lax.dot_general(
        flipped[...].reshape(wide * columns, dim).astype(bf16),
        cotangent[...].reshape(wide * columns, dim),
        (((0,), (0,)), ((), ())),
        preferred_element_type=f32,
    )
    grad_ref[...] = grad.astype(bf16)


def pair_update(pair_input, cotangents, flip_weight, turned, bundles, columns_used):
    rows, columns, dim = pair_input.shape
    chips = len(bundles)
    return pl.pallas_call(
        functools.partial(pair_kernel, chips, columns_used),
        name="pair",
        out_shape=[array((rows, columns, dim), bf16), array((dim, dim), bf16)],
        in_specs=[whole_vmem()] * (6 + chips),
        out_specs=[whole_vmem()] * 2,
        scratch_shapes=[
            pltpu.VMEM((2 * chips, rows, 2 * dim), f32),
            pltpu.VMEM((2 * chips, 2 * rows * rows, dim), bf16),
            pltpu.VMEM((rows * columns, dim), bf16),
            pltpu.VMEM((2 * rows, columns, dim), f32),
            pltpu.VMEM((2 * rows, columns, dim), bf16),
        ],
        compiler_params=pltpu.CompilerParams(
            vmem_limit_bytes=6 * MIB if chips <= 4 else 32 * MIB
        ),
    )(pair_input, *cotangents, flip_weight, *turned, *bundles)


def per_device(
    features,
    conv_weight,
    norm_gain,
    query_weight,
    keyval_weight,
    head_scale,
    output_weight,
    pair_weight,
    pair_input,
    flip_weight,
    pair_cotangent,
):
    chips = lax.axis_size("seq")
    bits = chips.bit_length() - 1
    windows = lax.axis_size("dp")
    taps = conv_weight.shape[0]
    model_dim = output_weight.shape[1]
    heads = head_scale.shape[0]
    features = features[0]

    masks = [(k, flipped_bits(k, bits)) for k in range(chips)]

    def send(value, mask, flip=0):
        cores = mask if isinstance(mask, tuple) else (mask, mask)
        return lax.ppermute(value, GROUP, hop_pairs(chips, cores, flip))

    rows, channels = features.shape
    width = channels // chips
    own_weight = conv_weight.reshape(-1, model_dim)
    peer_weight = send(own_weight, 0, 1)
    blocks = prep(features, pair_input[0], chips)

    messages = [blocks[0]] + [None] * (chips - 1)
    for k in range(chips - 1, 0, -1):
        messages[k] = send(blocks[k], k)
    weight = pack_filter(own_weight, peer_weight, taps, blocks[0].shape[1])
    cotangent, weight = lax.optimization_barrier((pair_cotangent[0], weight))
    cotangents = (pair_cotangent[0], send(cotangent, 0, 1))

    last = chips - 1
    rest = sorted(range(last), key=lambda k: (1 - (k & 1), -k))

    prepared = {}

    def active(k, wait):
        if k not in prepared:
            sources = [messages[j] for j in dict.fromkeys(masks[k])]
            prepared[k] = activate(sources, width, rows, wait)
        return prepared[k]

    def partials(ks, columns, edges, after, wait):
        dtypes = [bf16 if k & 1 else f32 for k in ks]
        blocks = [active(k, wait) for k in ks]
        got = conv(blocks, edges, features, weight, taps, ks, dtypes, columns, after)
        return dict(zip(ks, got))

    columns = [(0, model_dim // 2), (model_dim // 2, model_dim)]
    partial = partials([last], columns[:1], None, [], [])
    partial[last] += partials([last], columns[1:], None, [cotangents[1]], [])[last]
    edges = send(edge_rows(messages, width, rows, partial[last]), 0, 1)
    arrivals = [messages[k] for k in range(1, last)]
    partial[last] = [lax.optimization_barrier((v, *arrivals))[0] for v in partial[last]]
    pairs, _, pair_dim = pair_input.shape[1:]
    turned = unpack_pairs(
        messages, pairs, pair_dim, rows, width, partial[last]
    )
    turned = (turned, send(turned, 0, 1))
    odd = [k for k in rest if k & 1]
    even = [k for k in rest if k and not k & 1]
    partial.update(partials(odd, columns, edges, [turned[1]], partial[last]))
    own_terms = edge_terms(edges, weight, taps, partial[1])
    terms = send(own_terms, last)
    for ks in (even, [0]):
        partial.update(partials(ks, columns, edges, [turned[1]], [own_terms]))
    arrived = []
    for b in range(bits):
        bit = 1 << b
        leaving = [k for k in [last] + rest if k in partial and k & bit]
        got = {k ^ bit: [send(v, masks[bit]) for v in partial.pop(k)] for k in leaving}
        for k, values in got.items():
            if k == 0:
                arrived.append(values)
            else:
                dtype = bf16 if k & (2 * bit) else f32
                partial[k] = [
                    add_up([p, v], dtype, [turned[1]]) for p, v in zip(partial[k], values)
                ]

    encoded, feats = encode(partial[0], arrived, terms, pair_weight, [])
    keyval = project_keyvals(encoded, norm_gain, keyval_weight.T)
    own_bundle = bundle(keyval, feats, send(feats, 0, 1))
    bundles = [own_bundle] + [send(own_bundle, k) for k in range(1, chips)]
    pair_out, grad = pair_update(
        pair_input[0], cotangents, flip_weight, turned, bundles, keyval_weight.shape[1]
    )
    keyvals = bundles + [send(v, 0, 1) for v in bundles]

    def attend_heads(start, first, end, dtype, after):
        return attend(
            encoded,
            norm_gain,
            query_weight,
            head_scale,
            start,
            output_weight,
            keyvals,
            first,
            end,
            dtype,
            after,
        )

    halfway = heads // 2
    first_half, done = attend_heads(encoded, 0, halfway, f32, [])
    others = [send(grad, k) for k in range(chips - 1, 0, -1)][::-1]
    grad = add_up([grad] + others, bf16, [done], backwards=True)
    block_out, done = attend_heads(first_half, halfway, heads, bf16, [grad])
    planes = [
        lax.ppermute(grad, "dp", [(w, w ^ k) for w in range(windows)])
        for k in range(windows - 1, 0, -1)
    ]
    grad = add_up([grad] + planes[::-1], f32, [done], backwards=True)
    return (block_out[None], pair_out[None], grad)


def solution(mesh):
    placed = (
        P("dp", ("seq", "mp"), None),
        P(None, ("seq", "mp"), None),
        P(),
        P(),
        P(),
        P(),
        P(),
        P(),
        P("dp", ("seq", "mp"), None, None),
        P(),
        P("dp", ("seq", "mp"), None, None),
    )
    return jax.shard_map(
        per_device,
        mesh=mesh,
        in_specs=placed,
        out_specs=(P("dp", ("seq", "mp"), None), P("dp", ("seq", "mp"), None, None), P()),
        check_vma=False,
    )
```

```python
import functools
import math

import jax
import jax.numpy as jnp
from jax import lax
from jax.experimental import pallas as pl
from jax.experimental.pallas import tpu as pltpu
from jax.sharding import PartitionSpec as P

PAIR_POOL = 16
SPARE_ROWS = 32
norm_eps = 1e-06
logit_cap = 50.0
MIB = 1 << 20
GROUP = ("seq", "mp")
f32, bf16 = jnp.float32, jnp.bfloat16


def whole_vmem():
    return pl.BlockSpec(memory_space=pltpu.VMEM)


def anywhere():
    return pl.BlockSpec(memory_space=pl.ANY)


def smem():
    return pl.BlockSpec(memory_space=pltpu.SMEM)


def in_hbm(value):
    return pltpu.with_memory_space_constraint(value, pltpu.HBM)


def array(shape, dtype):
    return jax.ShapeDtypeStruct(shape, dtype)


def lane_pad(width):
    return (width + 127) // 128 * 128


def tree_sum(terms):
    while len(terms) > 1:
        terms = [terms[i] + terms[i + 1] for i in range(0, len(terms), 2)]
    return terms[0]


def flipped_bits(mask, bits):
    return sum(((mask >> b) & 1) << (bits - 1 - b) for b in range(bits))


def here():
    return lax.axis_index("seq"), lax.axis_index("mp")


def hop_pairs(chips, core_masks, core_flip):
    pairs = []
    for chip in range(chips):
        for core in range(2):
            target = (chip ^ core_masks[core]) * 2 + (core ^ core_flip)
            pairs.append((chip * 2 + core, target))
    return pairs


def pick_rows(rows):
    half = rows // 2
    target = lax.broadcasted_iota(jnp.int32, (rows, rows), 0)
    source = lax.broadcasted_iota(jnp.int32, (rows, rows), 1)
    wanted = jnp.where(target < half, 2 * target, 2 * (target - half) + 1)
    return jnp.where(source == wanted, 1.0, 0.0).astype(bf16)


def prep_kernel(chips, width, feat_hbm, pair_hbm, *rest):
    block_refs = rest[:chips]
    feat, pair, split, sems = rest[chips:]
    rows = feat.shape[0]
    chip, _ = here()
    chunks = sems.shape[0] - 1
    step = rows // chunks

    def copy(n):
        at = pl.ds(n * step, step)
        return pltpu.make_async_copy(feat_hbm.at[at, :], feat.at[at, :], sems.at[n])

    pair_copy = pltpu.make_async_copy(pair_hbm, pair, sems.at[chunks])
    for n in range(chunks):
        copy(n).start()
    pair_copy.start()
    for n in range(chunks):
        copy(n).wait()
        fill_rows(chips, width, n * step, step, feat, split)
    pair_copy.wait()
    pairs, _, dim = pair.shape
    lanes = split.shape[2] // dim
    extra = block_refs[0].shape[0] - rows
    spare = dim * SPARE_ROWS // rows
    for k in range(chips):
        at = pl.ds(pl.multiple_of((chip ^ k) * 2 * pairs, 16), 2 * pairs)
        piece = pair[:, at, :].reshape(2 * pairs * pairs, dim)
        block_refs[k][0:rows, :] = split[chip ^ k]
        for g in range(dim // spare):
            block_refs[k][
                g * SPARE_ROWS : (g + 1) * SPARE_ROWS, width + 8 : width + 8 + spare
            ] = piece[:SPARE_ROWS, g * spare : (g + 1) * spare]
        for g in range(lanes):
            part = piece[SPARE_ROWS + g * extra : SPARE_ROWS + (g + 1) * extra]
            block_refs[k][rows : rows + part.shape[0], g * dim : (g + 1) * dim] = part


def fill_rows(chips, width, start, step, feat, split):
    at = slice(start, start + step)
    x = feat[at, :].astype(f32)
    scale = lax.rsqrt(jnp.mean(x * x, axis=-1, keepdims=True) + norm_eps)
    high = scale.astype(bf16)
    middle = (scale - high.astype(f32)).astype(bf16)
    low = (scale - high.astype(f32) - middle.astype(f32)).astype(bf16)
    lane = lax.broadcasted_iota(jnp.int32, (step, split.shape[2] - width), 1)
    tail = jnp.where(
        lane == 0,
        high.astype(f32),
        jnp.where(
            lane == 1, middle.astype(f32), jnp.where(lane == 2, low.astype(f32), 0.0)
        ),
    ).astype(bf16)
    for q in range(chips):
        split[q, at, 0:width] = feat[at, q * width : (q + 1) * width]
        split[q, at, width:] = tail


def prep(features, pair_input, chips):
    rows, channels = features.shape
    width = channels // chips
    padded = lane_pad(width)
    pairs, _, dim = pair_input.shape
    extra = -(-(2 * pairs * pairs - SPARE_ROWS) // (16 * (padded // dim))) * 16
    return pl.pallas_call(
        functools.partial(prep_kernel, chips, width),
        name="prep",
        out_shape=[array((rows + extra, padded), bf16)] * chips,
        in_specs=[anywhere()] * 2,
        out_specs=[whole_vmem()] * chips,
        scratch_shapes=[
            pltpu.VMEM((rows, channels), bf16),
            pltpu.VMEM(pair_input.shape, bf16),
            pltpu.VMEM((chips, rows, padded), bf16),
            pltpu.SemaphoreType.DMA((2,)),
        ],
        compiler_params=pltpu.CompilerParams(vmem_limit_bytes=10 * MIB),
    )(in_hbm(features), in_hbm(pair_input))


def gelu_of(block, width):
    scale = block[:, width : width + 1] + block[:, width + 1 : width + 2]
    scale = scale + block[:, width + 2 : width + 3]
    v = block * scale
    g = (0.5 * v) * (1.0 + lax.erf(v * math.sqrt(0.5)))
    lane = lax.broadcasted_iota(jnp.int32, block.shape, 1)
    return jnp.where(lane < width, g, 0.0)


def edges_kernel(chips, width, rows, *refs):
    message_refs = refs[:chips][::-1]
    out_ref = refs[-1]
    strips = []
    for ref in message_refs:
        for start, row in ((0, 0), (0, 1), (rows - 16, 14), (rows - 16, 15)):
            strips.append(ref[start : start + 16, :].astype(f32)[row : row + 1])
    prepared = gelu_of(jnp.concatenate(strips, axis=0), width)
    for k in range(chips):
        out_ref[k, 0:4] = prepared[4 * k : 4 * k + 4]
        out_ref[k, 4:8] = jnp.zeros((4, prepared.shape[1]), f32)


def edge_rows(messages, width, rows, after):
    chips = len(messages)
    padded = messages[0].shape[1]
    return pl.pallas_call(
        functools.partial(edges_kernel, chips, width, rows),
        name="edge_rows",
        out_shape=array((chips, 8, padded), f32),
        in_specs=[whole_vmem()] * chips + [anywhere()] * len(after),
        out_specs=whole_vmem(),
        compiler_params=pltpu.CompilerParams(vmem_limit_bytes=2 * MIB),
    )(*messages[::-1], *after)


def activate_kernel(width, count, *refs):
    message_refs, out_ref, wide = refs[:count], refs[-2], refs[-1]
    _, core = here()
    step = 32
    rows = out_ref.shape[0]
    pick = pick_rows(rows)
    if count == 1:
        wide[...] = jnp.dot(pick, message_refs[0][0:rows, :], preferred_element_type=f32)
    else:

        @pl.when(core == 0)
        def _():
            wide[...] = jnp.dot(pick, message_refs[0][0:rows, :], preferred_element_type=f32)

        @pl.when(core != 0)
        def _():
            wide[...] = jnp.dot(pick, message_refs[1][0:rows, :], preferred_element_type=f32)

    def body(i, carry):
        at = pl.ds(pl.multiple_of(i * step, step), step)
        out_ref[at, :] = gelu_of(wide[at, :], width).astype(bf16)
        return carry

    lax.fori_loop(0, out_ref.shape[0] // step, body, 0)


def activate(messages, width, rows, after):
    return pl.pallas_call(
        functools.partial(activate_kernel, width, len(messages)),
        name="activate",
        out_shape=array((rows, messages[0].shape[1]), bf16),
        in_specs=[whole_vmem()] * len(messages) + [anywhere()] * len(after),
        out_specs=whole_vmem(),
        scratch_shapes=[pltpu.VMEM((rows, messages[0].shape[1]), f32)],
        compiler_params=pltpu.CompilerParams(vmem_limit_bytes=3 * MIB),
    )(*messages, *after)


def pack_kernel(taps, padded, own_hbm, peer_hbm, out_ref, sems):
    part = own_hbm.shape[0] // taps
    _, core = here()
    copies = []
    for p, source in enumerate((own_hbm, peer_hbm)):
        place = core if p == 0 else 1 - core
        for k in range(taps):
            to = pl.ds(pl.multiple_of(k * padded + place * part, 16), part)
            copies.append(
                pltpu.make_async_copy(
                    source.at[k * part : (k + 1) * part, :], out_ref.at[to, :], sems.at[p, k]
                )
            )
    for c in copies:
        c.start()
    if padded > 2 * part:
        for k in range(taps):
            out_ref[k * padded + 2 * part : (k + 1) * padded, :] = jnp.zeros(
                (padded - 2 * part, out_ref.shape[1]), bf16
            )
    for c in copies:
        c.wait()


def pack_filter(own, peer, taps, padded):
    model_dim = own.shape[1]
    part = own.shape[0] // taps
    if part % 16:
        own, peer = (w.reshape(taps, part, model_dim) for w in (own, peer))
        first = lax.axis_index("mp") == 0
        low, high = jnp.where(first, own, peer), jnp.where(first, peer, own)
        both = jnp.concatenate([low, high], axis=1)
        both = jnp.pad(both, ((0, 0), (0, padded - 2 * part), (0, 0)))
        return both.reshape(taps * padded, model_dim)
    return pl.pallas_call(
        functools.partial(pack_kernel, taps, padded),
        name="pack_filter",
        out_shape=array((taps * padded, model_dim), bf16),
        in_specs=[anywhere()] * 2,
        out_specs=whole_vmem(),
        scratch_shapes=[pltpu.SemaphoreType.DMA((2, taps))],
        compiler_params=pltpu.CompilerParams(vmem_limit_bytes=2 * MIB),
    )(in_hbm(own), peer)


def conv_kernel(
    chips, bits, taps, tile, wanted, columns, outs, edged, feat_hbm, edge_ref, *rest
):
    count = len(wanted)
    block_refs = rest[:count]
    weight_ref = rest[count]
    cols, feat, sem = rest[-3:]
    out_refs = rest[-3 - outs : -3]
    rows, padded = block_refs[0].shape
    half = rows // 2
    chip, core = here()
    if 0 in wanted:
        copy = pltpu.make_async_copy(feat_hbm, feat, sem)
        copy.start()
    row = lax.broadcasted_iota(jnp.int32, (half, padded), 0)
    for j, k in enumerate(wanted):
        mask = jnp.where(core == 0, k, flipped_bits(k, bits))
        left = (chip ^ mask) - (1 - core)
        right = (chip ^ mask) + core
        block = block_refs[j][...]
        if edged:
            before = edge_ref[jnp.where(left >= 0, left ^ chip, 0)]
            before = jnp.where(left >= 0, before, 0.0)
            after = edge_ref[jnp.where(right < chips, right ^ chip, 0)]
            after = jnp.where(right < chips, after, 0.0)
        else:
            before = after = jnp.zeros((8, padded), f32)
        even = block[0:half].astype(f32)
        odd = block[half:rows].astype(f32)

        def back(v, strip_row):
            return jnp.where(row == 0, before[strip_row : strip_row + 1], pltpu.roll(v, 1, 0))

        def ahead(v, strip_row):
            return jnp.where(
                row == half - 1, after[strip_row : strip_row + 1], pltpu.roll(v, half - 1, 0)
            )

        lagged = [back(even, 2), back(odd, 3), even, odd, ahead(even, 0), ahead(odd, 1)]
        for i, v in enumerate(lagged):
            piece = v.astype(bf16)
            if i < taps:
                cols[j * rows : j * rows + half, i * padded : (i + 1) * padded] = piece
            if i > 0:
                cols[j * rows + half : (j + 1) * rows, (i - 1) * padded : i * padded] = piece
    pick = pick_rows(rows)
    if 0 in wanted:
        copy.wait()
    for j, k in enumerate(wanted):
        for h, (first, last) in enumerate(columns):
            out_ref = out_refs[j * len(columns) + h]
            for at in range(first, last, tile):
                got = jnp.dot(
                    cols[j * rows : (j + 1) * rows],
                    weight_ref[:, at : at + tile],
                    preferred_element_type=f32,
                )
                if k == 0 and at < feat.shape[1]:
                    width = min(tile, feat.shape[1] - at)
                    skip = jnp.dot(
                        pick, feat[:, at : at + width], preferred_element_type=f32
                    )
                    if width < tile:
                        skip = jnp.concatenate(
                            [skip, jnp.zeros((rows, tile - width), f32)], axis=1
                        )
                    got = got + skip
                out_ref[:, at - first : at - first + tile] = got.astype(out_ref.dtype)


def edge_terms_kernel(chips, taps, edge_ref, weight_ref, *rest):
    out_ref, cols = rest[-2:]
    padded = edge_ref.shape[2]
    chip, core = here()
    left = (chip ^ (chips - 1)) - (1 - core)
    right = (chip ^ (chips - 1)) + core
    before = edge_ref[jnp.where(left >= 0, left ^ chip, 0)]
    before = jnp.where(left >= 0, before, 0.0)
    after = edge_ref[jnp.where(right < chips, right ^ chip, 0)]
    after = jnp.where(right < chips, after, 0.0)
    none = jnp.zeros((1, padded), f32)
    blank = jnp.zeros((12, padded), f32)
    terms = {
        0: (before[2:3], before[3:4], none, none),
        1: (before[3:4], none, none, none),
        3: (none, none, none, after[0:1]),
        4: (none, none, after[0:1], after[1:2]),
    }
    for k in range(taps):
        rows = terms.get(k, (none,) * 4)
        cols[:, k * padded : (k + 1) * padded] = jnp.concatenate(
            [*rows, blank], axis=0
        ).astype(bf16)
    span = out_ref.shape[1]
    quarters = [
        jnp.dot(cols[...], weight_ref[:, at : at + span], preferred_element_type=f32)[0:4]
        for at in range(0, 4 * span, span)
    ]
    out_ref[...] = jnp.concatenate(quarters, axis=0).astype(bf16)


def edge_terms(edges, weight, taps, after):
    chips = edges.shape[0]
    depth, model_dim = weight.shape
    return pl.pallas_call(
        functools.partial(edge_terms_kernel, chips, taps),
        name="edge_terms",
        out_shape=array((16, model_dim // 4), bf16),
        in_specs=[whole_vmem()] * 2 + [anywhere()] * len(after),
        out_specs=whole_vmem(),
        scratch_shapes=[pltpu.VMEM((16, depth), bf16)],
        compiler_params=pltpu.CompilerParams(vmem_limit_bytes=2 * MIB),
    )(edges, weight, *after)


def conv(blocks, edges, features, weight, taps, wanted, dtypes, columns, after):
    chips = lax.axis_size("seq")
    bits = chips.bit_length() - 1
    rows = features.shape[0]
    edged = edges is not None
    depth, model_dim = weight.shape
    count = len(wanted)
    pieces = len(columns)
    got = pl.pallas_call(
        functools.partial(
            conv_kernel, chips, bits, taps, 768, wanted, columns, count * pieces, edged
        ),
        name="conv",
        out_shape=[array((rows, b - a), d) for d in dtypes for a, b in columns],
        in_specs=[anywhere()] + [whole_vmem()] * (count + 2) + [anywhere()] * len(after),
        out_specs=[whole_vmem()] * (count * pieces),
        scratch_shapes=[
            pltpu.VMEM((count * rows, depth), bf16),
            pltpu.VMEM(features.shape, bf16),
            pltpu.SemaphoreType.DMA,
        ],
        compiler_params=pltpu.CompilerParams(vmem_limit_bytes=(5 + 2 * count) * MIB),
    )(in_hbm(features), edges if edged else blocks[0], *blocks, weight, *after)
    return [got[j * pieces : (j + 1) * pieces] for j in range(count)]


def sum_kernel(count, backwards, *refs):
    out_ref = refs[-1]
    terms = [r[...].astype(f32) for r in refs[:count]]
    out_ref[...] = tree_sum(terms[::-1] if backwards else terms).astype(out_ref.dtype)


def add_up(terms, dtype, after=(), backwards=False):
    terms = terms[::-1] if backwards else terms
    return pl.pallas_call(
        functools.partial(sum_kernel, len(terms), backwards),
        name="add_up",
        out_shape=array(terms[0].shape, dtype),
        in_specs=[whole_vmem()] * len(terms) + [anywhere()] * len(after),
        out_specs=whole_vmem(),
        compiler_params=pltpu.CompilerParams(vmem_limit_bytes=4 * MIB),
    )(*terms, *after)


def encode_kernel(pieces, arrivals, pair_weight_ref, term_ref, *rest):
    own_refs = rest[:pieces]
    come_refs = rest[pieces : pieces + arrivals * pieces]
    encoded_ref, feats_ref = rest[-2:]
    rows = own_refs[0].shape[0]
    half = rows // 2
    pairs = half // PAIR_POOL
    at = lax.broadcasted_iota(jnp.int32, (pairs, half), 0)
    of = lax.broadcasted_iota(jnp.int32, (pairs, half), 1) // PAIR_POOL
    spread = jnp.where(at == of, 1.0 / PAIR_POOL, 0.0).astype(bf16)
    feats = jnp.zeros(feats_ref.shape, f32)
    quarters = term_ref[...].astype(f32)
    all_terms = jnp.concatenate([quarters[q : q + 4] for q in range(0, 16, 4)], axis=1)
    first = 0
    for h in range(pieces):
        last = first + own_refs[h].shape[1]
        total = own_refs[h][...]
        for a in range(arrivals):
            total = total + come_refs[a * pieces + h][...].astype(f32)
        terms = all_terms[:, first:last]
        row = lax.broadcasted_iota(jnp.int32, (half, last - first), 0)
        even, odd = (
            part
            + jnp.where(row == 0, terms[i : i + 1], 0.0)
            + jnp.where(row == half - 1, terms[i + 2 : i + 3], 0.0)
            for i, part in enumerate((total[:half], total[half:]))
        )
        encoded = jnp.maximum(even, odd).astype(bf16)
        encoded_ref[:, first:last] = encoded
        pooled = jnp.dot(spread, encoded, preferred_element_type=f32).astype(bf16)
        feats = feats + jnp.dot(
            pooled, pair_weight_ref[first:last, :], preferred_element_type=f32
        )
        first = last
    feats_ref[...] = feats.astype(bf16).astype(f32)


def encode(own, come, terms, pair_weight, after):
    rows = own[0].shape[0]
    pieces = len(own)
    half = rows // 2
    return pl.pallas_call(
        functools.partial(encode_kernel, pieces, len(come)),
        name="encode",
        out_shape=[
            array((half, sum(v.shape[1] for v in own)), bf16),
            array((half // PAIR_POOL, pair_weight.shape[1]), f32),
        ],
        in_specs=[whole_vmem()] * (2 + pieces * (1 + len(come))) + [anywhere()] * len(after),
        out_specs=[whole_vmem()] * 2,
        compiler_params=pltpu.CompilerParams(vmem_limit_bytes=8 * MIB),
    )(pair_weight, terms, *own, *sum(come, []), *after)


def normalised(encoded_ref, gain_ref):
    wide = encoded_ref[...].astype(f32)
    scale = lax.rsqrt(jnp.mean(wide * wide, axis=-1, keepdims=True) + norm_eps)
    return (wide * scale * gain_ref[...][None]).astype(bf16)


def keyval_kernel(encoded_ref, gain_ref, weight_ref, out_ref):
    out_ref[...] = lax.dot_general(
        normalised(encoded_ref, gain_ref),
        weight_ref[...],
        (((1,), (1,)), ((), ())),
        preferred_element_type=f32,
    ).astype(bf16)


def project_keyvals(encoded, gain, weight_t):
    return pl.pallas_call(
        keyval_kernel,
        name="keyvals",
        out_shape=array((encoded.shape[0], weight_t.shape[0]), bf16),
        in_specs=[whole_vmem()] * 3,
        out_specs=whole_vmem(),
        compiler_params=pltpu.CompilerParams(vmem_limit_bytes=4 * MIB),
    )(encoded, gain, weight_t)


def bundle_kernel(keyval_ref, mine_ref, other_ref, out_ref):
    rows, columns = keyval_ref.shape
    spare = out_ref.shape[1] - columns
    pieces = []
    for ref in (mine_ref, other_ref):
        feats = ref[...]
        pieces += [feats[:, g : g + spare] for g in range(0, feats.shape[1], spare)]
    used = sum(p.shape[0] for p in pieces)
    pieces.append(jnp.zeros((rows - used, spare), f32))
    out_ref[:, :columns] = keyval_ref[...]
    out_ref[:, columns:] = jnp.concatenate(pieces, axis=0).astype(bf16)


def bundle(keyval, mine, other):
    return pl.pallas_call(
        bundle_kernel,
        name="bundle",
        out_shape=array((keyval.shape[0], lane_pad(keyval.shape[1])), bf16),
        in_specs=[whole_vmem()] * 3,
        out_specs=whole_vmem(),
        compiler_params=pltpu.CompilerParams(vmem_limit_bytes=4 * MIB),
    )(keyval, mine, other)


def attend_kernel(
    parts,
    heads,
    first,
    last,
    group,
    scale_ref,
    encoded_ref,
    gain_ref,
    query_weight_ref,
    start_ref,
    weight_ref,
    *rest,
):
    part_refs = rest[:parts]
    out_ref, done_ref, keys, values = rest[-4:]
    rows = encoded_ref.shape[0]
    key_dim = query_weight_ref.shape[1] // heads
    normed = normalised(encoded_ref, gain_ref)
    span = part_refs[0].shape[0]
    value_dim = values.shape[1]
    for k in range(parts):
        got = part_refs[k][...]
        keys[k * span : (k + 1) * span, :] = got[:, :key_dim]
        values[k * span : (k + 1) * span, :] = got[:, key_dim : key_dim + value_dim]
    total = start_ref[...].astype(f32)
    for n in range(first, last, group):
        got = jnp.dot(
            normed,
            query_weight_ref[:, n * key_dim : (n + group) * key_dim],
            preferred_element_type=f32,
        )
        queries = jnp.concatenate(
            [
                got[:, h * key_dim : (h + 1) * key_dim]
                * (scale_ref[n + h] / math.sqrt(key_dim))
                for h in range(group)
            ],
            axis=0,
        ).astype(bf16)
        scores = lax.dot_general(
            queries, keys[...], (((1,), (1,)), ((), ())), preferred_element_type=f32
        )
        weights = jnp.exp(logit_cap * jnp.tanh(scores * (1.0 / logit_cap)))
        sums = jnp.sum(weights, axis=-1, keepdims=True)
        mixed = jnp.dot(weights.astype(bf16), values[...], preferred_element_type=f32) / sums
        mixed = mixed.astype(bf16)
        for h in range(group):
            at = (n + h) * value_dim
            total = total + jnp.dot(
                mixed[h * rows : (h + 1) * rows],
                weight_ref[at : at + value_dim, :],
                preferred_element_type=f32,
            )
    out_ref[...] = total.astype(out_ref.dtype)
    done_ref[...] = total[0:8, 0:128]


def attend(
    encoded, gain, query_weight, scale, start, output_weight, parts, first, last, dtype, after
):
    rows, model_dim = start.shape
    heads = scale.shape[0]
    key_dim = query_weight.shape[1] // heads
    value_dim = output_weight.shape[0] // heads
    total_keys = parts[0].shape[0] * len(parts)
    group = 2
    return pl.pallas_call(
        functools.partial(attend_kernel, len(parts), heads, first, last, group),
        name="attend",
        out_shape=[array((rows, model_dim), dtype), array((8, 128), f32)],
        in_specs=[smem()] + [whole_vmem()] * (5 + len(parts)) + [anywhere()] * len(after),
        out_specs=[whole_vmem()] * 2,
        scratch_shapes=[
            pltpu.VMEM((total_keys, key_dim), bf16),
            pltpu.VMEM((total_keys, value_dim), bf16),
        ],
        compiler_params=pltpu.CompilerParams(
            vmem_limit_bytes=8 * MIB if total_keys <= 1024 else 32 * MIB
        ),
    )(scale, encoded, gain, query_weight, start, output_weight, *parts, *after)


def unpack_kernel(chips, pairs, rows, width, *refs):
    message_refs = refs[:chips][::-1]
    out_ref = refs[-1]
    dim = out_ref.shape[2]
    padded = message_refs[0].shape[1]
    for k in range(chips):
        spare = dim * SPARE_ROWS // rows
        first = jnp.concatenate(
            [
                message_refs[k][
                    g * SPARE_ROWS : (g + 1) * SPARE_ROWS, width + 8 : width + 8 + spare
                ]
                for g in range(dim // spare)
            ],
            axis=1,
        )
        piece = message_refs[k][rows:, :]
        piece = [piece[:, g : g + dim] for g in range(0, padded, dim)]
        piece = jnp.concatenate([first] + piece, axis=0)
        piece = piece[: 2 * pairs * pairs].reshape(pairs, 2 * pairs, dim)
        out_ref[k * pairs : (k + 1) * pairs] = piece


def unpack_pairs(messages, pairs, dim, rows, width, after):
    chips = len(messages)
    return pl.pallas_call(
        functools.partial(unpack_kernel, chips, pairs, rows, width),
        name="unpack_pairs",
        out_shape=array((chips * pairs, 2 * pairs, dim), bf16),
        in_specs=[whole_vmem()] * chips + [anywhere()] * len(after),
        out_specs=whole_vmem(),
        compiler_params=pltpu.CompilerParams(vmem_limit_bytes=4 * MIB),
    )(*messages[::-1], *after)


def pair_kernel(
    chips, columns_used, input_ref, cotangent_ref, other_cotangent_ref, flip_ref, turned_ref, other_ref, *rest
):
    bundle_refs = rest[:chips]
    out_ref, grad_ref, stacked, mirror, summed, flipped, cotangent = rest[-7:]
    rows, columns, dim = input_ref.shape
    parts = 2 * chips
    wide = 2 * rows
    chip, core = here()
    me = chip * 2 + core
    for k in range(chips):
        got = bundle_refs[k][:, columns_used:].astype(f32)
        count = 2 * dim // got.shape[1]
        for f in range(2):
            at = f * count * rows
            stacked[2 * k + f] = jnp.concatenate(
                [got[at + g * rows : at + (g + 1) * rows] for g in range(count)], axis=1
            )
    own, other = stacked[0], stacked[1]
    both_k = jnp.concatenate(
        [jnp.where(core == 0, own, other), jnp.where(core == 0, other, own)], axis=0
    )[:, dim:][None]
    for k in range(parts):
        source = turned_ref if k % 2 == 0 else other_ref
        value = source[k // 2 * rows : (k // 2 + 1) * rows].astype(f32)
        value = value + stacked[k][:, None, :dim] * both_k
        mirror[k] = value.reshape(rows * wide, dim).astype(bf16)
    target = lax.broadcasted_iota(jnp.int32, (rows * wide, rows * wide), 0)
    origin = lax.broadcasted_iota(jnp.int32, (rows * wide, rows * wide), 1)
    swap = jnp.where(origin == (target % rows) * wide + target // rows, 1.0, 0.0).astype(bf16)
    for b in range(parts):
        turned = jnp.dot(swap, mirror[b ^ me], preferred_element_type=f32)
        flipped[:, b * rows : (b + 1) * rows, :] = turned.reshape(wide, rows, dim)
    every = jnp.concatenate([stacked[b ^ me] for b in range(parts)], axis=0)[:, dim:]
    for i in range(rows):
        at = pl.ds(i * columns, columns)
        value = input_ref[i].astype(f32) + own[i : i + 1, :dim] * every
        summed[at, :] = value.astype(bf16)
    facing = flipped[pl.ds(core * rows, rows)].reshape(rows * columns, dim).astype(bf16)
    update = jnp.dot(facing, flip_ref[...], preferred_element_type=f32)
    update = update + summed[...].astype(f32)
    out_ref[...] = update.astype(bf16).reshape(rows, columns, dim)
    cotangent[pl.ds(core * rows, rows)] = cotangent_ref[...]
    cotangent[pl.ds((1 - core) * rows, rows)] = other_cotangent_ref[...]
    grad = lax.dot_general(
        flipped[...].reshape(wide * columns, dim).astype(bf16),
        cotangent[...].reshape(wide * columns, dim),
        (((0,), (0,)), ((), ())),
        preferred_element_type=f32,
    )
    grad_ref[...] = grad.astype(bf16)


def pair_update(pair_input, cotangents, flip_weight, turned, bundles, columns_used):
    rows, columns, dim = pair_input.shape
    chips = len(bundles)
    return pl.pallas_call(
        functools.partial(pair_kernel, chips, columns_used),
        name="pair",
        out_shape=[array((rows, columns, dim), bf16), array((dim, dim), bf16)],
        in_specs=[whole_vmem()] * (6 + chips),
        out_specs=[whole_vmem()] * 2,
        scratch_shapes=[
            pltpu.VMEM((2 * chips, rows, 2 * dim), f32),
            pltpu.VMEM((2 * chips, 2 * rows * rows, dim), bf16),
            pltpu.VMEM((rows * columns, dim), bf16),
            pltpu.VMEM((2 * rows, columns, dim), f32),
            pltpu.VMEM((2 * rows, columns, dim), bf16),
        ],
        compiler_params=pltpu.CompilerParams(
            vmem_limit_bytes=6 * MIB if chips <= 4 else 32 * MIB
        ),
    )(pair_input, *cotangents, flip_weight, *turned, *bundles)


def per_device(
    features,
    conv_weight,
    norm_gain,
    query_weight,
    keyval_weight,
    head_scale,
    output_weight,
    pair_weight,
    pair_input,
    flip_weight,
    pair_cotangent,
):
    chips = lax.axis_size("seq")
    bits = chips.bit_length() - 1
    windows = lax.axis_size("dp")
    taps = conv_weight.shape[0]
    model_dim = output_weight.shape[1]
    heads = head_scale.shape[0]
    features = features[0]

    masks = [(k, flipped_bits(k, bits)) for k in range(chips)]

    def send(value, mask, flip=0):
        cores = mask if isinstance(mask, tuple) else (mask, mask)
        return lax.ppermute(value, GROUP, hop_pairs(chips, cores, flip))

    rows, channels = features.shape
    width = channels // chips
    own_weight = conv_weight.reshape(-1, model_dim)
    peer_weight = send(own_weight, 0, 1)
    blocks = prep(features, pair_input[0], chips)

    messages = [blocks[0]] + [None] * (chips - 1)
    for k in range(chips - 1, 0, -1):
        messages[k] = send(blocks[k], k)
    weight = pack_filter(own_weight, peer_weight, taps, blocks[0].shape[1])
    cotangent, weight = lax.optimization_barrier((pair_cotangent[0], weight))
    cotangents = (pair_cotangent[0], send(cotangent, 0, 1))

    last = chips - 1
    rest = sorted(range(last), key=lambda k: (1 - (k & 1), -k))

    prepared = {}

    def active(k, wait):
        if k not in prepared:
            sources = [messages[j] for j in dict.fromkeys(masks[k])]
            prepared[k] = activate(sources, width, rows, wait)
        return prepared[k]

    def partials(ks, columns, edges, after, wait):
        dtypes = [bf16 if k & 1 else f32 for k in ks]
        blocks = [active(k, wait) for k in ks]
        got = conv(blocks, edges, features, weight, taps, ks, dtypes, columns, after)
        return dict(zip(ks, got))

    columns = [(0, model_dim // 2), (model_dim // 2, model_dim)]
    partial = partials([last], columns[:1], None, [], [])
    partial[last] += partials([last], columns[1:], None, [cotangents[1]], [])[last]
    edges = send(edge_rows(messages, width, rows, partial[last]), 0, 1)
    arrivals = [messages[k] for k in range(1, last)]
    partial[last] = [lax.optimization_barrier((v, *arrivals))[0] for v in partial[last]]
    pairs, _, pair_dim = pair_input.shape[1:]
    turned = unpack_pairs(
        messages, pairs, pair_dim, rows, width, partial[last]
    )
    turned = (turned, send(turned, 0, 1))
    odd = [k for k in rest if k & 1]
    even = [k for k in rest if k and not k & 1]
    partial.update(partials(odd, columns, edges, [turned[1]], partial[last]))
    own_terms = edge_terms(edges, weight, taps, partial[1])
    terms = send(own_terms, last)
    for ks in (even, [0]):
        partial.update(partials(ks, columns, edges, [turned[1]], [own_terms]))
    arrived = []
    for b in range(bits):
        bit = 1 << b
        leaving = [k for k in [last] + rest if k in partial and k & bit]
        got = {k ^ bit: [send(v, masks[bit]) for v in partial.pop(k)] for k in leaving}
        for k, values in got.items():
            if k == 0:
                arrived.append(values)
            else:
                dtype = bf16 if k & (2 * bit) else f32
                partial[k] = [
                    add_up([p, v], dtype, [turned[1]]) for p, v in zip(partial[k], values)
                ]

    encoded, feats = encode(partial[0], arrived, terms, pair_weight, [])
    keyval = project_keyvals(encoded, norm_gain, keyval_weight.T)
    own_bundle = bundle(keyval, feats, send(feats, 0, 1))
    bundles = [own_bundle] + [send(own_bundle, k) for k in range(1, chips)]
    pair_out, grad = pair_update(
        pair_input[0], cotangents, flip_weight, turned, bundles, keyval_weight.shape[1]
    )
    keyvals = bundles + [send(v, 0, 1) for v in bundles]

    def attend_heads(start, first, end, dtype, after):
        return attend(
            encoded,
            norm_gain,
            query_weight,
            head_scale,
            start,
            output_weight,
            keyvals,
            first,
            end,
            dtype,
            after,
        )

    halfway = heads // 2
    first_half, done = attend_heads(encoded, 0, halfway, f32, [])
    grad = add_up([grad] + [send(grad, k) for k in range(1, chips)], bf16, [done])
    block_out, done = attend_heads(first_half, halfway, heads, bf16, [grad])
    planes = [
        lax.ppermute(grad, "dp", [(w, w ^ k) for w in range(windows)])
        for k in range(windows - 1, 0, -1)
    ]
    grad = add_up([grad] + planes[::-1], f32, [done], backwards=True)
    return (block_out[None], pair_out[None], grad)


def solution(mesh):
    placed = (
        P("dp", ("seq", "mp"), None),
        P(None, ("seq", "mp"), None),
        P(),
        P(),
        P(),
        P(),
        P(),
        P(),
        P("dp", ("seq", "mp"), None, None),
        P(),
        P("dp", ("seq", "mp"), None, None),
    )
    return jax.shard_map(
        per_device,
        mesh=mesh,
        in_specs=placed,
        out_specs=(P("dp", ("seq", "mp"), None), P("dp", ("seq", "mp"), None, None), P()),
        check_vma=False,
    )
```
